256 devices in a mesh: gx: 32 (over x_lo, z, core), gy: 8 (over x_hi, y).
Axes of the slice: x: 4 (x_hi: 2, x_lo: 2; x = x_hi * 2 + x_lo), y: 4, z: 8, core: 2. Of those that a mesh axis runs over, the one named last changes fastest.
Arguments:
- e_field: float32 [2, 3, 16, 1024, 1024], P(None, None, None, 'gx', 'gy'), may hold values from -6 to 6
- h_field: float32 [2, 3, 16, 1024, 1024], P(None, None, None, 'gx', 'gy'), may hold values from -6 to 6
- material: int32 [16, 1024, 1024], P(None, 'gx', 'gy'), may hold values from 0 to 7
- pattern: int32 [16, 1024, 1024], P(None, 'gx', 'gy'), may hold values from 0 to 15
- base_eps: float32 [8], replicated, may hold values from 2 to 12
- mode_table: float32 [4, 16], replicated, may hold values from -0.1 to 0.1
- nodes: float32 [4], replicated, may hold values from -1 to 1
- bloch_phase: float32 [2], replicated, may hold values from -3.140625 to 3.140625
- monitor_z: int32 [1], replicated, may hold values from 0 to 15
Outputs:
- e_out: float32 [2, 3, 16, 1024, 1024], P(None, None, None, 'gx', 'gy')
- h_out: float32 [2, 3, 16, 1024, 1024], P(None, None, None, 'gx', 'gy')
- orders: float32 [2, 2, 256, 256], P(None, None, 'gx', 'gy')
The draws below stay inside these ranges and needn't reach their ends.
All inputs are finite; a program needn't handle non-finite values.
Results may differ from the reference program's by a relative error of at most 0.000078.
Values sent between devices are 32-bit elements; how exact they have to be, the bound alone decides.
No kernel may reach another device: no remote copies, remote signals or barrier semaphores. Data moves between devices by JAX's collectives and lax.ppermute only.
A program may use at most 64 MiB of HBM per device.

```python
import math
import jax
import jax.numpy as jnp
from jax import lax

NZ = 16
STEPS = 2
ORD_X = 256
ORD_Y = 256
NMAT = 8
NPAT = 16
NMODE = 4
NX = 1024
NY = 1024


def place_ends(values, own_key, low, high):
    index_at = [jax.random.randint(jax.random.fold_in(own_key, axis), (), 0, length) for axis, length in enumerate(values.shape)]
    widest = values.shape.index(max(values.shape))
    beside = index_at[:widest] + [(index_at[widest] + 1) % values.shape[widest]] + index_at[widest + 1:]
    return values.at[tuple(index_at)].set(low).at[tuple(beside)].set(high)


def levels(key, shape, pieces, smallest, largest):
    def one(position, parts):
        heights = jax.random.uniform(jax.random.fold_in(jax.random.fold_in(key, 6), position), (parts,), jnp.float32, smallest / len(pieces), largest / len(pieces))
        return jnp.repeat(jnp.exp(heights), shape[position] // parts).reshape((-1,) + (1,) * (len(shape) - position - 1))

    loudness = one(*pieces[0])
    for cut in pieces[1:]:
        loudness = loudness * one(*cut)
    return loudness


def gaussian(own_key, extent, deviation, reach, cuts=(), dtype=jnp.bfloat16):
    drawn = jax.random.normal(own_key, extent, jnp.float32) * deviation
    if len(cuts) > 0:
        drawn = levels(own_key, extent, cuts, -0.22, 0.18) * drawn
    return jnp.clip(drawn, min=-reach, max=reach).astype(dtype)


def setup_inputs(seed: int = 0) -> dict:
    splits = jax.random.split(jax.random.key(seed), 10)
    return {
        "e_field": gaussian(splits[0], (2, 3, NZ, NX, NY), 1.0, 6.0, ((3, 32), (4, 8)), jnp.float32),
        "h_field": gaussian(splits[1], (2, 3, NZ, NX, NY), 1.0, 6.0, ((3, 32), (4, 8)), jnp.float32),
        "material": place_ends(jax.random.randint(splits[2], (NZ, NX, NY), 0, NMAT), jax.random.fold_in(splits[2], 1), 0, NMAT - 1).astype(jnp.int32),
        "pattern": place_ends(jax.random.randint(splits[3], (NZ, NX, NY), 0, NPAT), jax.random.fold_in(splits[3], 1), 0, NPAT - 1).astype(jnp.int32),
        "base_eps": jnp.clip(jnp.exp(jax.random.uniform(splits[4], (NMAT,), jnp.float32, math.log(2.0), math.log(12.0))), 2.0, 12.0),
        "mode_table": jnp.clip(jax.random.uniform(splits[5], (NMODE, NPAT), jnp.float32, -0.1, 0.1), -0.1, 0.1),
        "nodes": jnp.clip(jax.random.uniform(splits[6], (NMODE,), jnp.float32, -1.0, 1.0), -1.0, 1.0),
        "bloch_phase": jnp.clip(jax.random.uniform(splits[7], (2,), jnp.float32, -3.140625, 3.140625), -3.140625, 3.140625),
        "monitor_z": jax.random.randint(splits[8], (1,), 0, NZ).astype(jnp.int32),
    }


STEP_DT = 0.5

def rotate(values, twist_cos, twist_sin):
    return jnp.stack([values[0] * twist_cos - values[1] * twist_sin, values[1] * twist_cos + values[0] * twist_sin])

def next_layer(values):
    return jnp.concatenate([values[:, 1:], jnp.zeros_like(values[:, :1])], axis=1)

def prev_layer(values):
    return jnp.concatenate([jnp.zeros_like(values[:, :1]), values[:, :-1]], axis=1)

def pair_xz(values):
    return jnp.stack([values[:, 0], values[:, 2]], axis=1)

def h_update(electric, magnetic, x_next, y_next):
    e_xcomp, e_ycomp, e_zcomp = (electric[:, 0], electric[:, 1], electric[:, 2])
    curl_xcomp = y_next[:, 1] - e_zcomp - (next_layer(e_ycomp) - e_ycomp)
    curl_ycomp = next_layer(e_xcomp) - e_xcomp - (x_next[:, 1] - e_zcomp)
    curl_zcomp = x_next[:, 0] - e_ycomp - (y_next[:, 0] - e_xcomp)
    return magnetic - STEP_DT * jnp.stack([curl_xcomp, curl_ycomp, curl_zcomp], axis=1)

def e_update(electric, magnetic, x_prev, y_prev, coef):
    h_xcomp, h_ycomp, h_zcomp = (magnetic[:, 0], magnetic[:, 1], magnetic[:, 2])
    curl_xcomp = h_zcomp - y_prev[:, 1] - (h_ycomp - prev_layer(h_ycomp))
    curl_ycomp = h_xcomp - prev_layer(h_xcomp) - (h_zcomp - x_prev[:, 1])
    curl_zcomp = h_ycomp - x_prev[:, 0] - (h_xcomp - y_prev[:, 0])
    return electric + coef * jnp.stack([curl_xcomp, curl_ycomp, curl_zcomp], axis=1)

def twiddles(start, count, half, offset, length, total, theta):
    order_index = start + lax.iota(jnp.int32, count) - half
    place = offset + lax.iota(jnp.int32, length)
    product = jnp.mod(order_index[:, None] * place[None, :], total).astype(jnp.int32)
    angle = (2.0 * math.pi * product.astype(jnp.float32) + theta * place.astype(jnp.float32)[None, :]) / total
    return (jnp.cos(angle), jnp.sin(angle))

def y_section(planes, wave_cos, wave_sin):
    width = planes.shape[1]
    count = wave_cos.shape[0]
    with_cos = jnp.einsum('kxy,qy->kxq', planes, wave_cos, precision=lax.Precision.HIGHEST, preferred_element_type=jnp.float32).reshape(2, 2, width, count)
    with_sin = jnp.einsum('kxy,qy->kxq', planes, wave_sin, precision=lax.Precision.HIGHEST, preferred_element_type=jnp.float32).reshape(2, 2, width, count)
    return jnp.stack([with_cos[:, 0] + with_sin[:, 1], with_cos[:, 1] - with_sin[:, 0]], axis=1)

def x_section(spread, wave_cos, wave_sin):
    count = wave_cos.shape[0]
    columns = spread.shape[2]
    with_cos = jnp.einsum('px,kxq->pkq', wave_cos, spread, precision=lax.Precision.HIGHEST, preferred_element_type=jnp.float32).reshape(count, 2, 2, columns)
    with_sin = jnp.einsum('px,kxq->pkq', wave_sin, spread, precision=lax.Precision.HIGHEST, preferred_element_type=jnp.float32).reshape(count, 2, 2, columns)
    return jnp.stack([with_cos[:, :, 0] + with_sin[:, :, 1], with_cos[:, :, 1] - with_sin[:, :, 0]], axis=2)

def shift_next(values, axis, twist_cos, twist_sin):
    length = values.shape[axis]
    inner = lax.slice_in_dim(values, 1, length, axis=axis)
    edge = rotate(lax.slice_in_dim(values, 0, 1, axis=axis), twist_cos, twist_sin)
    return jnp.concatenate([inner, edge], axis=axis)

def shift_prev(values, axis, twist_cos, twist_sin):
    length = values.shape[axis]
    inner = lax.slice_in_dim(values, 0, length - 1, axis=axis)
    edge = rotate(lax.slice_in_dim(values, length - 1, length, axis=axis), twist_cos, -twist_sin)
    return jnp.concatenate([edge, inner], axis=axis)

def reference(e_field, h_field, material, pattern, base_eps, mode_table, nodes, bloch_phase, monitor_z):
    xwrap_cos = jnp.cos(bloch_phase[0])
    xwrap_sin = jnp.sin(bloch_phase[0])
    ywrap_cos = jnp.cos(bloch_phase[1])
    ywrap_sin = jnp.sin(bloch_phase[1])
    factor = 1.0 + lax.optimization_barrier(jnp.sum(nodes[:, None] * mode_table, axis=0))
    coef = STEP_DT / (base_eps[material] * factor[pattern])
    electric, magnetic = (e_field, h_field)
    for instant in range(STEPS):
        magnetic = h_update(electric, magnetic, shift_next(electric[:, 1:3], 3, xwrap_cos, xwrap_sin), shift_next(pair_xz(electric), 4, ywrap_cos, ywrap_sin))
        electric = e_update(electric, magnetic, shift_prev(magnetic[:, 1:3], 3, xwrap_cos, xwrap_sin), shift_prev(pair_xz(magnetic), 4, ywrap_cos, ywrap_sin), coef)
    plane = lax.dynamic_index_in_dim(electric, monitor_z[0], axis=2, keepdims=False)
    scale = 1.0 / math.sqrt(NX * NY)
    planes = jnp.transpose(plane[:, 0:2], (1, 0, 2, 3)).reshape(4, NX, NY) * scale
    ycos, ysin = twiddles(0, ORD_Y, ORD_Y // 2, 0, NY, NY, bloch_phase[1])
    xcos, xsin = twiddles(0, ORD_X, ORD_X // 2, 0, NX, NX, bloch_phase[0])
    spread = y_section(planes, ycos, ysin).reshape(4, NX, ORD_Y)
    result = x_section(spread, xcos, xsin)
    return (electric, magnetic, jnp.transpose(result, (1, 2, 0, 3)))
```

```python
import math

import jax
import jax.numpy as jnp
from jax import lax
from jax.experimental import pallas as pl
from jax.experimental.pallas import tpu as pltpu
from jax.sharding import PartitionSpec as P

STEP_DT = 0.5
ORD_X = 256
ORD_Y = 256
NZ = 16
ROWS = 32
COLS = 128
EXT = 40
MAIN_BLOCKS = 52
EDGE_BLOCKS = 58
VMEM = pltpu.VMEM
SMEM = pltpu.SMEM


def passed_along(block, axis, distance):
    devices = range(lax.axis_size(axis))
    route = [((i - distance) % len(devices), i) for i in devices]
    return lax.ppermute(block, axis, route)


def roll(values, shift, axis):
    size = values.shape[axis]
    if isinstance(shift, int):
        shift = shift % size
        if shift == 0:
            return values
    return pltpu.roll(values, shift, axis)


def lanes_of(shape):
    return lax.broadcasted_iota(jnp.int32, shape, len(shape) - 1)


def coef_table(base_ref, mode_ref, node_ref):
    lane = lanes_of((8, 128))
    material = lane // 16
    pattern = lane % 16
    base = jnp.zeros((8, 128), jnp.float32)
    for m in range(8):
        base = jnp.where(material == m, base_ref[m], base)
    change = jnp.zeros((8, 128), jnp.float32)
    for k in range(4):
        mode = jnp.zeros((8, 128), jnp.float32)
        for p in range(16):
            mode = jnp.where(pattern == p, mode_ref[k, p], mode)
        change = change + node_ref[k] * mode
    return STEP_DT / (base * (1.0 + change))


def look_up(table, pair):
    rows = [
        jnp.take_along_axis(table, pair[8 * r : 8 * r + 8], axis=1)
        for r in range(pair.shape[0] // 8)
    ]
    return jnp.concatenate(rows, axis=0)


def pack_kernel(
    e_ref,
    h_ref,
    material_ref,
    pattern_ref,
    base_ref,
    mode_ref,
    node_ref,
    coef_ref,
    own_ref,
    right_ref,
    left_ref,
    first_ref,
    last_ref,
):
    table = coef_table(base_ref, mode_ref, node_ref)
    lane = lanes_of((ROWS, COLS))
    group = lane // 8
    place = lane % 8

    def coef_plane(z, carry):
        pair = material_ref[z] * 16 + pattern_ref[z]
        coef_ref[z] = look_up(table, pair)
        return carry

    lax.fori_loop(0, NZ, coef_plane, 0)

    def plane(index, z):
        if index == 12:
            return coef_ref.at[z]
        ref = e_ref if index < 6 else h_ref
        return ref.at[(index % 6) // 3, index % 3, z]

    for index in range(13):
        packed = jnp.zeros((ROWS, COLS), jnp.float32)
        for z in range(NZ):
            values = plane(index, z)[...]
            packed = jnp.where(group == z, roll(values, 8 * z + 6, 1), packed)
            block = index * 4 + z // 4
            slot = 2 * (z % 4)
            first_ref[block, slot : slot + 2, :] = values[0:2]
            last_ref[block, slot : slot + 2, :] = values[ROWS - 2 : ROWS]
        own_ref[index] = packed
        block = MAIN_BLOCKS + index // 4
        slot = 2 * (index % 4)
        first_ref[block, slot : slot + 2, :] = packed[0:2]
        last_ref[block, slot : slot + 2, :] = packed[ROWS - 2 : ROWS]
    for c in range(3):
        e_re, e_im, h_re, h_im = (own_ref[3 * k + c] for k in range(4))
        right_ref[c] = jnp.where(
            place < 4,
            jnp.where(place < 2, roll(h_re, -4, 1), roll(h_im, -2, 1)),
            jnp.where(place < 6, e_re, roll(e_im, 2, 1)),
        )
        left_ref[c] = jnp.where(
            place < 4,
            jnp.where(place < 2, roll(h_im, -6, 1), roll(h_re, -4, 1)),
            jnp.where(place < 6, roll(e_im, -2, 1), e_re),
        )
    right_ref[3] = own_ref[12]
    left_ref[3] = own_ref[12]


def turned(re, im, cos, sin):
    return re * cos - im * sin, im * cos + re * sin


def strip_of(own, right, left, rot):
    place = lanes_of(own[0].shape) % 8

    def joined(index, from_right, from_left):
        return jnp.where(
            place < 4,
            jnp.where(place < 2, roll(own[index], -4, 1), from_left),
            jnp.where(place < 6, from_right, own[index]),
        )

    strip = [None] * 13
    for c in range(3):
        r = right[c]
        l = left[c]
        e_right = turned(r, roll(r, -2, 1), rot[4], rot[5])
        h_right = turned(roll(r, 4, 1), roll(r, 2, 1), rot[4], rot[5])
        e_left = turned(roll(l, -4, 1), roll(l, -2, 1), rot[6], rot[7])
        h_left = turned(l, roll(l, 2, 1), rot[6], rot[7])
        for part in range(2):
            strip[3 * part + c] = joined(3 * part + c, e_right[part], e_left[part])
            strip[6 + 3 * part + c] = joined(6 + 3 * part + c, h_right[part], h_left[part])
    strip[12] = joined(12, right[3], roll(left[3], -4, 1))
    return strip


def next_row(values):
    return roll(values, -1, 0)


def prev_row(values):
    return roll(values, 1, 0)


def h_new(h, e, e_up, e_xn, e_yn):
    return (
        h[0] - STEP_DT * (e_yn[1] - e[2] - (e_up[1] - e[1])),
        h[1] - STEP_DT * (e_up[0] - e[0] - (e_xn[1] - e[2])),
        h[2] - STEP_DT * (e_xn[0] - e[1] - (e_yn[0] - e[0])),
    )


def e_new(e, h, h_down, h_xp, h_yp, coef):
    return (
        e[0] + coef * (h[2] - h_yp[1] - (h[1] - h_down[1])),
        e[1] + coef * (h[0] - h_down[0] - (h[2] - h_xp[1])),
        e[2] + coef * (h[1] - h_xp[0] - (h[0] - h_yp[0])),
    )


def strip_h(h, e):
    up = lanes_of((EXT, COLS)) < 8 * (NZ - 1)
    above = [jnp.where(up, roll(e[c], -8, 1), 0.0) for c in range(2)]
    return h_new(
        h,
        e,
        above,
        (next_row(e[1]), next_row(e[2])),
        (roll(e[0], -1, 1), roll(e[2], -1, 1)),
    )


def strip_e(e, h, coef):
    up = lanes_of((EXT, COLS)) >= 8
    below = [jnp.where(up, roll(h[c], 8, 1), 0.0) for c in range(2)]
    return e_new(
        e,
        h,
        below,
        (prev_row(h[1]), prev_row(h[2])),
        (roll(h[0], 1, 1), roll(h[2], 1, 1)),
        coef,
    )


def field_kernel(
    e_hbm,
    h_hbm,
    coef_ref,
    own_ref,
    right_ref,
    left_ref,
    next_ref,
    prev_ref,
    rot_ref,
    monitor_ref,
    wave_ref,
    e_out,
    h_out,
    spread_ref,
    e_all,
    h_all,
    coef_all,
    strip_ref,
    edge_ref,
    sem,
):
    load_e = pltpu.make_async_copy(e_hbm, e_all.at[:, :, 0:NZ, 0:ROWS, :], sem.at[0])
    load_h = pltpu.make_async_copy(h_hbm, h_all.at[:, :, 1 : NZ + 1, 0:ROWS, :], sem.at[1])
    load_e.start()
    load_h.start()
    rot = [rot_ref[k] for k in range(8)]

    for part in range(2):
        for c in range(3):
            e_all[part, c, NZ] = jnp.zeros((EXT, COLS), jnp.float32)
            h_all[part, c, 0] = jnp.zeros((EXT, COLS), jnp.float32)
    for ref, row, cos, sin in ((next_ref, 32, rot[0], rot[1]), (prev_ref, 38, rot[2], rot[3])):
        for field in range(2):
            for c in range(3):
                for quad in range(4):
                    re = ref[(6 * field + c) * 4 + quad]
                    im = ref[(6 * field + 3 + c) * 4 + quad]
                    for part, values in enumerate(turned(re, im, cos, sin)):
                        for k in range(4):
                            dest = h_all if field else e_all
                            z = 4 * quad + k + field
                            dest[part, c, z, row : row + 2, :] = values[2 * k : 2 * k + 2]
        for quad in range(4):
            values = ref[48 + quad]
            for k in range(4):
                coef_all[4 * quad + k, row : row + 2, :] = values[2 * k : 2 * k + 2]
        pieces = [
            ref[MAIN_BLOCKS + a // 4, 2 * (a % 4) : 2 * (a % 4) + 2, :] for a in range(24)
        ]
        strip = strip_of(pieces[0:13], pieces[16:20], pieces[20:24], rot)
        for field in range(2):
            for c in range(3):
                for part, values in enumerate(
                    turned(strip[6 * field + c], strip[6 * field + 3 + c], cos, sin)
                ):
                    strip_ref[6 * field + 3 * part + c, row : row + 2, :] = values
        strip_ref[12, row : row + 2, :] = strip[12]
    strip = strip_of(
        [own_ref[a] for a in range(13)],
        [right_ref[a] for a in range(4)],
        [left_ref[a] for a in range(4)],
        rot,
    )
    for a in range(13):
        strip_ref[a, 0:ROWS, :] = strip[a]
    for z in range(NZ):
        coef_all[z, 0:ROWS, :] = coef_ref[z]

    strip_coef = strip_ref[12]
    for part in range(2):
        e = tuple(strip_ref[3 * part + c] for c in range(3))
        h = tuple(strip_ref[6 + 3 * part + c] for c in range(3))
        for step in range(2):
            edge_ref[part, 2 * step, 0] = e[0]
            edge_ref[part, 2 * step, 1] = e[2]
            h = strip_h(h, e)
            edge_ref[part, 2 * step + 1, 0] = h[0]
            edge_ref[part, 2 * step + 1, 1] = h[2]
            if step == 0:
                e = strip_e(e, h, strip_coef)

    lane = lanes_of((EXT, COLS))

    def next_col(values, edge, z):
        arrived = roll(edge, lax.rem(COLS + 125 - 8 * z, COLS), 1)
        return jnp.where(lane == COLS - 1, arrived, roll(values, -1, 1))

    def prev_col(values, edge, z):
        arrived = roll(edge, lax.rem(COLS + 123 - 8 * z, COLS), 1)
        return jnp.where(lane == 0, arrived, roll(values, 1, 1))

    def do_h(step, z):
        for part in range(2):
            e = tuple(e_all[part, c, z] for c in range(3))
            h = tuple(h_all[part, c, z + 1] for c in range(3))
            e_up = (e_all[part, 0, z + 1], e_all[part, 1, z + 1])
            e_yn = (
                next_col(e[0], edge_ref[part, 2 * step, 0], z),
                next_col(e[2], edge_ref[part, 2 * step, 1], z),
            )
            new = h_new(h, e, e_up, (next_row(e[1]), next_row(e[2])), e_yn)
            for c in range(3):
                h_all[part, c, z + 1] = new[c]

    def do_e(step, z):
        coef = coef_all[z]
        for part in range(2):
            e = tuple(e_all[part, c, z] for c in range(3))
            h = tuple(h_all[part, c, z + 1] for c in range(3))
            h_down = (h_all[part, 0, z], h_all[part, 1, z])
            h_yp = (
                prev_col(h[0], edge_ref[part, 2 * step + 1, 0], z),
                prev_col(h[2], edge_ref[part, 2 * step + 1, 1], z),
            )
            new = e_new(e, h, h_down, (prev_row(h[1]), prev_row(h[2])), h_yp, coef)
            for c in range(3):
                e_all[part, c, z] = new[c]

    load_e.wait()
    load_h.wait()

    def sweep(update, step):
        def body(z, carry):
            update(step, z)
            return carry

        lax.fori_loop(0, NZ, body, 0)

    for step in range(2):
        sweep(do_h, step)
        if step == 1:
            store_h = pltpu.make_async_copy(
                h_all.at[:, :, 1 : NZ + 1, 0:ROWS, :], h_out, sem.at[1]
            )
            store_h.start()
        sweep(do_e, step)
    store_e = pltpu.make_async_copy(e_all.at[:, :, 0:NZ, 0:ROWS, :], e_out, sem.at[0])
    store_e.start()

    level = monitor_ref[0]
    re = jnp.concatenate([e_all[0, c, level, 0:ROWS, :] for c in range(2)], axis=0)
    im = jnp.concatenate([e_all[1, c, level, 0:ROWS, :] for c in range(2)], axis=0)
    y_section(re, im, wave_ref, spread_ref)
    store_h.wait()
    store_e.wait()


def y_section(re, im, wave_ref, spread_ref):
    wave = wave_ref[...]
    owners, _, lanes = spread_ref.shape
    each = lanes // 4
    out = [
        jnp.dot(
            jnp.concatenate(pair, axis=1),
            wave,
            precision=lax.Precision.HIGHEST,
            preferred_element_type=jnp.float32,
        )
        for pair in ((re, im), (im, -re))
    ]
    for owner in range(owners):
        pieces = [
            out[part][c * ROWS : (c + 1) * ROWS, owner * each : (owner + 1) * each]
            for part in range(2)
            for c in range(2)
        ]
        spread_ref[owner] = jnp.concatenate(pieces, axis=1)


def x_kernel(got_ref, wave_ref, part_ref):
    total = got_ref[0]
    for source in range(1, got_ref.shape[0]):
        total = total + got_ref[source]
    half = total.shape[1] // 2
    other = roll(total, half, 1)
    other = jnp.where(lanes_of(other.shape) < half, other, -other)
    result = jnp.dot(
        wave_ref[...],
        jnp.concatenate([total, other], axis=0),
        precision=lax.Precision.HIGHEST,
        preferred_element_type=jnp.float32,
    )
    part_ref[...] = result.reshape(part_ref.shape)


def sum_kernel(got_ref, out_ref):
    total = got_ref[0]
    for source in range(1, got_ref.shape[0]):
        total = total + got_ref[source]
    each = total.shape[1] // 4
    for c in range(2):
        for part in range(2):
            start = (2 * part + c) * each
            out_ref[c, part] = total[:, start : start + each]


def angles(count, half, offset, length, total, theta, order_axis):
    shape = (count, length) if order_axis == 0 else (length, count)
    order_index = lax.broadcasted_iota(jnp.int32, shape, order_axis) - half
    place = offset + lax.broadcasted_iota(jnp.int32, shape, 1 - order_axis)
    product = jnp.mod(order_index * place, total)
    return (
        2.0 * math.pi * product.astype(jnp.float32) + theta * place.astype(jnp.float32)
    ) / total


def f32(*shape):
    return jax.ShapeDtypeStruct(shape, jnp.float32)


def shards(
    e_field, h_field, material, pattern, base_eps, mode_table, nodes, bloch_phase, monitor_z
):
    count_x = lax.axis_size("gx")
    count_y = lax.axis_size("gy")
    index_x = lax.axis_index("gx")
    index_y = lax.axis_index("gy")
    total_x = ROWS * count_x
    total_y = COLS * count_y
    each_p = ORD_X // count_x
    each_q = ORD_Y // count_y
    vmem = pl.BlockSpec(memory_space=VMEM)
    smem = pl.BlockSpec(memory_space=SMEM)
    hbm = pl.BlockSpec(memory_space=pl.ANY)

    cos_x, sin_x = jnp.cos(bloch_phase[0]), jnp.sin(bloch_phase[0])
    cos_y, sin_y = jnp.cos(bloch_phase[1]), jnp.sin(bloch_phase[1])
    last_x = index_x == count_x - 1
    last_y = index_y == count_y - 1
    rot = jnp.stack(
        [
            jnp.where(last_x, cos_x, 1.0),
            jnp.where(last_x, sin_x, 0.0),
            jnp.where(index_x == 0, cos_x, 1.0),
            jnp.where(index_x == 0, -sin_x, 0.0),
            jnp.where(index_y == 0, cos_y, 1.0),
            jnp.where(index_y == 0, -sin_y, 0.0),
            jnp.where(last_y, cos_y, 1.0),
            jnp.where(last_y, sin_y, 0.0),
        ]
    )
    y_angle = angles(
        ORD_Y, ORD_Y // 2, index_y * COLS, COLS, total_y, bloch_phase[1], 1
    )
    scale = 1.0 / math.sqrt(total_x * total_y)
    y_wave = jnp.concatenate([jnp.cos(y_angle), jnp.sin(y_angle)], axis=0) * scale
    x_angle = angles(
        ORD_X, ORD_X // 2, index_x * ROWS, ROWS, total_x, bloch_phase[0], 0
    )
    x_wave = jnp.concatenate([jnp.cos(x_angle), jnp.sin(x_angle)], axis=1)

    coef, own, right, left, first, last = pl.pallas_call(
        pack_kernel,
        out_shape=(
            f32(NZ, ROWS, COLS),
            f32(13, ROWS, COLS),
            f32(4, ROWS, COLS),
            f32(4, ROWS, COLS),
            f32(EDGE_BLOCKS, 8, COLS),
            f32(EDGE_BLOCKS, 8, COLS),
        ),
        in_specs=[vmem] * 4 + [smem] * 3,
        out_specs=(vmem,) * 6,
        compiler_params=pltpu.CompilerParams(vmem_limit_bytes=32 << 20),
        name="pack",
    )(e_field, h_field, material, pattern, base_eps, mode_table, nodes)
    from_right = passed_along(right, "gy", 1)
    from_left = passed_along(left, "gy", -1)
    corner_first = jnp.concatenate([from_right[:, 0:2], from_left[:, 0:2]]).reshape(2, 8, COLS)
    corner_last = jnp.concatenate(
        [from_right[:, ROWS - 2 :], from_left[:, ROWS - 2 :]]
    ).reshape(2, 8, COLS)
    first = lax.dynamic_update_slice(first, corner_first, (EDGE_BLOCKS - 2, 0, 0))
    last = lax.dynamic_update_slice(last, corner_last, (EDGE_BLOCKS - 2, 0, 0))
    from_next = passed_along(first, "gx", -1)
    from_prev = passed_along(last, "gx", 1)

    e_out, h_out, spread = pl.pallas_call(
        field_kernel,
        out_shape=(
            f32(*e_field.shape),
            f32(*h_field.shape),
            f32(count_y, ROWS, 4 * each_q),
        ),
        in_specs=[hbm, hbm] + [vmem] * 6 + [smem, smem, vmem],
        out_specs=(hbm, hbm, vmem),
        scratch_shapes=[
            VMEM((2, 3, NZ + 1, EXT, COLS), jnp.float32),
            VMEM((2, 3, NZ + 1, EXT, COLS), jnp.float32),
            VMEM((NZ, EXT, COLS), jnp.float32),
            VMEM((13, EXT, COLS), jnp.float32),
            VMEM((2, 4, 2, EXT, COLS), jnp.float32),
            pltpu.SemaphoreType.DMA((2,)),
        ],
        compiler_params=pltpu.CompilerParams(vmem_limit_bytes=32 << 20),
        name="fields",
    )(
        e_field,
        h_field,
        coef,
        own,
        from_right,
        from_left,
        from_next,
        from_prev,
        rot,
        monitor_z,
        y_wave,
    )
    got = lax.all_to_all(spread, "gy", 0, 0, tiled=True)
    partial = pl.pallas_call(
        x_kernel,
        out_shape=f32(count_x, each_p, 4 * each_q),
        in_specs=[vmem, vmem],
        out_specs=vmem,
        name="x_section",
    )(got, x_wave)
    got = lax.all_to_all(partial, "gx", 0, 0, tiled=True)
    orders = pl.pallas_call(
        sum_kernel,
        out_shape=f32(2, 2, each_p, each_q),
        in_specs=[vmem],
        out_specs=vmem,
        name="order_sum",
    )(got)
    return e_out, h_out, orders


def solution(mesh):
    grid = P(None, None, None, "gx", "gy")
    cells = P(None, "gx", "gy")
    return jax.shard_map(
        shards,
        mesh=mesh,
        in_specs=(grid, grid, cells, cells, P(), P(), P(), P(), P()),
        out_specs=(grid, grid, P(None, None, "gx", "gy")),
        check_vma=False,
    )
```

```python
import functools
import math

import jax
import jax.numpy as jnp
from jax import lax
from jax.experimental import pallas as pl
from jax.experimental.pallas import tpu as pltpu
from jax.sharding import PartitionSpec as P

STEP_DT = 0.5
ORD_X = 256
ORD_Y = 256
NZ = 16
ROWS = 32
COLS = 128
EXT = 40
MAIN_BLOCKS = 52
VMEM = pltpu.VMEM
SMEM = pltpu.SMEM


def passed_along(block, axis, distance):
    devices = range(lax.axis_size(axis))
    route = [((i - distance) % len(devices), i) for i in devices]
    return lax.ppermute(block, axis, route)


def roll(values, shift, axis):
    size = values.shape[axis]
    if isinstance(shift, int):
        shift = shift % size
        if shift == 0:
            return values
    return pltpu.roll(values, shift, axis)


def lanes_of(shape):
    return lax.broadcasted_iota(jnp.int32, shape, len(shape) - 1)


def coef_table(base_ref, mode_ref, node_ref):
    lane = lanes_of((8, 128))
    material = lane // 16
    pattern = lane % 16
    base = jnp.zeros((8, 128), jnp.float32)
    for m in range(8):
        base = jnp.where(material == m, base_ref[m], base)
    change = jnp.zeros((8, 128), jnp.float32)
    for k in range(4):
        mode = jnp.zeros((8, 128), jnp.float32)
        for p in range(16):
            mode = jnp.where(pattern == p, mode_ref[k, p], mode)
        change = change + node_ref[k] * mode
    return STEP_DT / (base * (1.0 + change))


def look_up(table, pair):
    rows = [
        jnp.take_along_axis(table, pair[8 * r : 8 * r + 8], axis=1)
        for r in range(pair.shape[0] // 8)
    ]
    return jnp.concatenate(rows, axis=0)


def fetched(pairs, sem):
    copies = [
        pltpu.make_async_copy(source, target, sem.at[k])
        for k, (source, target) in enumerate(pairs)
    ]
    for copy in copies:
        copy.start()
    for copy in copies:
        copy.wait()


def plane_of(e_ref, h_ref, n, z):
    ref = e_ref if n < 6 else h_ref
    return ref[(n % 6) // 3, n % 3, z]


def rows_kernel(
    e_hbm,
    h_hbm,
    material_hbm,
    pattern_hbm,
    base_hbm,
    mode_hbm,
    node_hbm,
    monitor_hbm,
    after_hbm,
    plane_ref,
    coef_ref,
    own_ref,
    first_ref,
    last_ref,
    e_ref,
    h_ref,
    material_ref,
    pattern_ref,
    base_ref,
    mode_ref,
    node_ref,
    monitor_ref,
    sem,
):
    fetched(
        [
            (e_hbm, e_ref),
            (h_hbm, h_ref),
            (material_hbm, material_ref),
            (pattern_hbm, pattern_ref),
            (base_hbm, base_ref),
            (mode_hbm, mode_ref),
            (node_hbm, node_ref),
            (monitor_hbm, monitor_ref),
        ],
        sem,
    )
    table = coef_table(base_ref, mode_ref, node_ref)

    def coef_plane(z, carry):
        coef_ref[z] = look_up(table, material_ref[z] * 16 + pattern_ref[z])
        return carry

    lax.fori_loop(0, NZ, coef_plane, 0)
    group = lanes_of((ROWS, COLS)) // 8
    for n in range(13):
        packed = jnp.zeros((ROWS, COLS), jnp.float32)
        for z in range(NZ):
            values = coef_ref[z] if n == 12 else plane_of(e_ref, h_ref, n, z)
            packed = jnp.where(group == z, roll(values, 8 * z + 6, 1), packed)
        own_ref[n] = packed
        for quad in range(NZ // 4):
            planes = [
                coef_ref[z] if n == 12 else plane_of(e_ref, h_ref, n, z)
                for z in range(4 * quad, 4 * quad + 4)
            ]
            first_ref[NEAR_BLOCKS + 4 * n + quad] = jnp.concatenate(
                [values[0:2] for values in planes], axis=0
            )
            last_ref[4 * n + quad] = jnp.concatenate(
                [values[ROWS - 2 : ROWS] for values in planes], axis=0
            )
    level = monitor_ref[0]
    for n in range(COUNT):
        if n < 2 * HALF:
            field, c, k = NEAR[n % HALF]
            z = level - 2 + k
            inside = z >= 0 if field else z < NZ
            ref = h_ref if field else e_ref
            values = jnp.where(inside, ref[n // HALF, c, jnp.clip(z, 0, NZ - 1)], 0.0)
        else:
            values = coef_ref[jnp.clip(level - 1 + n - 2 * HALF, 0, NZ - 1)]
        plane_ref[n] = values
        start = 4 * (n % 2)
        first_ref[n // 2, start : start + 4, :] = values[0:4]
    first_ref[NEAR_BLOCKS - 1, 4:8, :] = jnp.zeros((4, COLS), jnp.float32)
    for k in range(2):
        first_ref[NEAR_BLOCKS + MAIN_BLOCKS + k] = jnp.zeros((8, COLS), jnp.float32)


def pack_kernel(
    own_ref, next_ref, prev_ref, rot_ref, after_ref, tail_ref, right_ref, left_ref
):
    rot = [rot_ref[k : k + 1, :] for k in range(8)]
    group = lanes_of((2, COLS)) // 8
    place = lanes_of((EXT, COLS)) % 8

    tail_ref[...] = jnp.zeros_like(tail_ref)
    for ref, start, row, cos, sin in (
        (next_ref, NEAR_BLOCKS, 32, rot[0], rot[1]),
        (prev_ref, 0, 38, rot[2], rot[3]),
    ):
        for n in (0, 1, 2, 6, 7, 8, 12):
            parts = 1 if n == 12 else 2
            packed = [jnp.zeros((2, COLS), jnp.float32) for _ in range(parts)]
            for quad in range(NZ // 4):
                values = [ref[start + 4 * (n + 3 * part) + quad] for part in range(parts)]
                if parts == 2:
                    values = turned(values[0], values[1], cos, sin)
                for k in range(4):
                    z = 4 * quad + k
                    for part in range(parts):
                        packed[part] = jnp.where(
                            group == z,
                            roll(values[part][2 * k : 2 * k + 2], 8 * z + 6, 1),
                            packed[part],
                        )
            for part in range(parts):
                tail_ref[n + 3 * part, row - ROWS : row - ROWS + 2, :] = packed[part]
    def column(n):
        return jnp.concatenate([own_ref[n], tail_ref[n]], axis=0)

    for c in range(3):
        e_re, e_im, h_re, h_im = (column(3 * k + c) for k in range(4))
        right_ref[c] = jnp.where(
            place < 4,
            jnp.where(place < 2, roll(h_re, -4, 1), roll(h_im, -2, 1)),
            jnp.where(place < 6, e_re, roll(e_im, 2, 1)),
        )
        left_ref[c] = jnp.where(
            place < 4,
            jnp.where(place < 2, roll(h_im, -6, 1), roll(h_re, -4, 1)),
            jnp.where(place < 6, roll(e_im, -2, 1), e_re),
        )
    right_ref[3] = column(12)
    left_ref[3] = column(12)


def turned(re, im, cos, sin):
    return re * cos - im * sin, im * cos + re * sin


def strip_of(own, right, left, rot):
    place = lanes_of(own[0].shape) % 8

    def joined(index, from_right, from_left):
        return jnp.where(
            place < 4,
            jnp.where(place < 2, roll(own[index], -4, 1), from_left),
            jnp.where(place < 6, from_right, own[index]),
        )

    strip = [None] * 13
    for c in range(3):
        r = right[c]
        l = left[c]
        e_right = turned(r, roll(r, -2, 1), rot[4], rot[5])
        h_right = turned(roll(r, 4, 1), roll(r, 2, 1), rot[4], rot[5])
        e_left = turned(roll(l, -4, 1), roll(l, -2, 1), rot[6], rot[7])
        h_left = turned(l, roll(l, 2, 1), rot[6], rot[7])
        for part in range(2):
            strip[3 * part + c] = joined(3 * part + c, e_right[part], e_left[part])
            strip[6 + 3 * part + c] = joined(6 + 3 * part + c, h_right[part], h_left[part])
    strip[12] = joined(12, right[3], roll(left[3], -4, 1))
    return strip


def next_row(values):
    return roll(values, -1, 0)


def prev_row(values):
    return roll(values, 1, 0)


def h_new(h, e, e_up, e_xn, e_yn):
    return (
        h[0] - STEP_DT * (e_yn[1] - e[2] - (e_up[1] - e[1])),
        h[1] - STEP_DT * (e_up[0] - e[0] - (e_xn[1] - e[2])),
        h[2] - STEP_DT * (e_xn[0] - e[1] - (e_yn[0] - e[0])),
    )


def e_new(e, h, h_down, h_xp, h_yp, coef):
    return (
        e[0] + coef * (h[2] - h_yp[1] - (h[1] - h_down[1])),
        e[1] + coef * (h[0] - h_down[0] - (h[2] - h_xp[1])),
        e[2] + coef * (h[1] - h_xp[0] - (h[0] - h_yp[0])),
    )


def strip_h(h, e):
    up = lanes_of((EXT, COLS)) < 8 * (NZ - 1)
    above = [jnp.where(up, roll(e[c], -8, 1), 0.0) for c in range(2)]
    return h_new(
        h,
        e,
        above,
        (next_row(e[1]), next_row(e[2])),
        (roll(e[0], -1, 1), roll(e[2], -1, 1)),
    )


def strip_e(e, h, coef):
    up = lanes_of((EXT, COLS)) >= 8
    below = [jnp.where(up, roll(h[c], 8, 1), 0.0) for c in range(2)]
    return e_new(
        e,
        h,
        below,
        (prev_row(h[1]), prev_row(h[2])),
        (roll(h[0], 1, 1), roll(h[2], 1, 1)),
        coef,
    )


def field_kernel(
    e_hbm,
    h_hbm,
    coef_hbm,
    own_hbm,
    tail_hbm,
    right_hbm,
    left_hbm,
    next_hbm,
    prev_hbm,
    rot_hbm,
    after_hbm,
    e_out,
    h_out,
    e_all,
    h_all,
    coef_all,
    own_ref,
    right_ref,
    left_ref,
    next_ref,
    prev_ref,
    rot_ref,
    edge_ref,
    sem,
):
    load_e = pltpu.make_async_copy(e_hbm, e_all.at[:, :, 0:NZ, 0:ROWS, :], sem.at[0])
    load_h = pltpu.make_async_copy(h_hbm, h_all.at[:, :, 1 : NZ + 1, 0:ROWS, :], sem.at[1])
    small = [
        pltpu.make_async_copy(source, target, sem.at[4 + k])
        for k, (source, target) in enumerate(
            [
                (rot_hbm, rot_ref),
                (own_hbm, own_ref.at[:, 0:ROWS]),
                (tail_hbm, own_ref.at[:, ROWS:EXT]),
                (right_hbm, right_ref),
                (left_hbm, left_ref),
                (next_hbm, next_ref),
                (prev_hbm, prev_ref),
                (coef_hbm, coef_all.at[:, 0:ROWS]),
            ]
        )
    ]
    for copy in small:
        copy.start()
    load_e.start()
    load_h.start()
    for copy in small:
        copy.wait()
    rot = [rot_ref[k : k + 1, :] for k in range(8)]

    for part in range(2):
        for c in range(3):
            e_all[part, c, NZ] = jnp.zeros((EXT, COLS), jnp.float32)
            h_all[part, c, 0] = jnp.zeros((EXT, COLS), jnp.float32)
    for ref, start, row, cos, sin in (
        (next_ref, NEAR_BLOCKS, 32, rot[0], rot[1]),
        (prev_ref, 0, 38, rot[2], rot[3]),
    ):
        for field in range(2):
            for c in range(3):
                for quad in range(4):
                    re = ref[start + (6 * field + c) * 4 + quad]
                    im = ref[start + (6 * field + 3 + c) * 4 + quad]
                    for part, values in enumerate(turned(re, im, cos, sin)):
                        for k in range(4):
                            dest = h_all if field else e_all
                            z = 4 * quad + k + field
                            dest[part, c, z, row : row + 2, :] = values[2 * k : 2 * k + 2]
        for quad in range(4):
            values = ref[start + 48 + quad]
            for k in range(4):
                coef_all[4 * quad + k, row : row + 2, :] = values[2 * k : 2 * k + 2]
    strip = strip_of(
        [own_ref[a] for a in range(13)],
        [right_ref[a] for a in range(4)],
        [left_ref[a] for a in range(4)],
        rot,
    )
    for part in range(2):
        e = tuple(strip[3 * part + c] for c in range(3))
        h = tuple(strip[6 + 3 * part + c] for c in range(3))
        for step in range(2):
            edge_ref[part, 2 * step, 0] = e[0]
            edge_ref[part, 2 * step, 1] = e[2]
            h = strip_h(h, e)
            edge_ref[part, 2 * step + 1, 0] = h[0]
            edge_ref[part, 2 * step + 1, 1] = h[2]
            if step == 0:
                e = strip_e(e, h, strip[12])

    lane = lanes_of((EXT, COLS))

    def next_col(values, edge, z):
        arrived = roll(edge, lax.rem(COLS + 125 - 8 * z, COLS), 1)
        return jnp.where(lane == COLS - 1, arrived, roll(values, -1, 1))

    def prev_col(values, edge, z):
        arrived = roll(edge, lax.rem(COLS + 123 - 8 * z, COLS), 1)
        return jnp.where(lane == 0, arrived, roll(values, 1, 1))

    def do_h(step, z):
        for part in range(2):
            e = tuple(e_all[part, c, z] for c in range(3))
            h = tuple(h_all[part, c, z + 1] for c in range(3))
            e_up = (e_all[part, 0, z + 1], e_all[part, 1, z + 1])
            e_yn = (
                next_col(e[0], edge_ref[part, 2 * step, 0], z),
                next_col(e[2], edge_ref[part, 2 * step, 1], z),
            )
            new = h_new(h, e, e_up, (next_row(e[1]), next_row(e[2])), e_yn)
            for c in range(3):
                h_all[part, c, z + 1] = new[c]

    def do_e(step, z):
        coef = coef_all[z]
        for part in range(2):
            e = tuple(e_all[part, c, z] for c in range(3))
            h = tuple(h_all[part, c, z + 1] for c in range(3))
            h_down = (h_all[part, 0, z], h_all[part, 1, z])
            h_yp = (
                prev_col(h[0], edge_ref[part, 2 * step + 1, 0], z),
                prev_col(h[2], edge_ref[part, 2 * step + 1, 1], z),
            )
            new = e_new(e, h, h_down, (prev_row(h[1]), prev_row(h[2])), h_yp, coef)
            for c in range(3):
                e_all[part, c, z] = new[c]

    load_e.wait()
    load_h.wait()

    def store(z):
        pltpu.make_async_copy(
            e_all.at[:, :, z, 0:ROWS, :], e_out.at[:, :, z], sem.at[2]
        ).start()
        pltpu.make_async_copy(
            h_all.at[:, :, z + 1, 0:ROWS, :], h_out.at[:, :, z], sem.at[3]
        ).start()

    do_h(0, 0)
    do_e(0, 0)

    def layer(z, carry):
        do_h(0, z)
        do_e(0, z)
        do_h(1, z - 1)
        do_e(1, z - 1)
        store(z - 1)
        return carry

    lax.fori_loop(1, NZ, layer, 0)
    do_h(1, NZ - 1)
    do_e(1, NZ - 1)
    store(NZ - 1)
    pltpu.make_async_copy(e_all.at[:, :, 0:NZ, 0:ROWS, :], e_out, sem.at[2]).wait()
    pltpu.make_async_copy(h_all.at[:, :, 1 : NZ + 1, 0:ROWS, :], h_out, sem.at[3]).wait()


def y_section(re, im, wave_ref, spread_ref):
    wave = wave_ref[...]
    owners, _, lanes = spread_ref.shape
    each = lanes // 4
    out = [
        jnp.dot(
            jnp.concatenate(pair, axis=1),
            wave,
            precision=lax.Precision.HIGHEST,
            preferred_element_type=jnp.float32,
        )
        for pair in ((re, im), (im, -re))
    ]
    for owner in range(owners):
        pieces = [
            out[part][c * ROWS : (c + 1) * ROWS, owner * each : (owner + 1) * each]
            for part in range(2)
            for c in range(2)
        ]
        spread_ref[owner] = jnp.concatenate(pieces, axis=1)


def x_kernel(got_ref, wave_ref, part_ref):
    total = got_ref[0]
    for source in range(1, got_ref.shape[0]):
        total = total + got_ref[source]
    half = total.shape[1] // 2
    other = roll(total, half, 1)
    other = jnp.where(lanes_of(other.shape) < half, other, -other)
    result = jnp.dot(
        wave_ref[...],
        jnp.concatenate([total, other], axis=0),
        precision=lax.Precision.HIGHEST,
        preferred_element_type=jnp.float32,
    )
    part_ref[...] = result.reshape(part_ref.shape)


def sum_kernel(got_ref, out_ref):
    total = got_ref[0]
    for source in range(1, got_ref.shape[0]):
        total = total + got_ref[source]
    each = total.shape[1] // 4
    for c in range(2):
        for part in range(2):
            start = (2 * part + c) * each
            out_ref[c, part] = total[:, start : start + each]


NEAR = (
    [(0, 0, k) for k in range(0, 5)]
    + [(0, 1, k) for k in range(0, 5)]
    + [(0, 2, k) for k in range(0, 4)]
    + [(1, 0, k) for k in range(0, 4)]
    + [(1, 1, k) for k in range(0, 4)]
    + [(1, 2, k) for k in range(1, 4)]
)
HALF = len(NEAR)
COUNT = 2 * HALF + 3
NEAR_BLOCKS = (COUNT + 1) // 2
CORNER = NEAR_BLOCKS + MAIN_BLOCKS
WIDE = 2 * COLS


def near_kernel(
    e_hbm,
    h_hbm,
    material_hbm,
    pattern_hbm,
    base_hbm,
    mode_hbm,
    node_hbm,
    monitor_hbm,
    cols_ref,
    e_ref,
    h_ref,
    material_ref,
    pattern_ref,
    base_ref,
    mode_ref,
    node_ref,
    monitor_ref,
    sem,
):
    fetched(
        [
            (e_hbm, e_ref),
            (h_hbm, h_ref),
            (material_hbm, material_ref),
            (pattern_hbm, pattern_ref),
            (base_hbm, base_ref),
            (mode_hbm, mode_ref),
            (node_hbm, node_ref),
            (monitor_hbm, monitor_ref),
        ],
        sem,
    )
    level = monitor_ref[0]
    table = coef_table(base_ref, mode_ref, node_ref)
    slot = lanes_of((ROWS, COLS)) // 4
    packed = [jnp.zeros((ROWS, COLS), jnp.float32) for _ in range(2)]
    for n in range(COUNT):
        if n < 2 * HALF:
            field, c, k = NEAR[n % HALF]
            z = level - 2 + k
            inside = z >= 0 if field else z < NZ
            ref = h_ref if field else e_ref
            values = ref[n // HALF, c, jnp.clip(z, 0, NZ - 1)]
            values = jnp.where(inside, values, 0.0)
        else:
            z = jnp.clip(level - 1 + n - 2 * HALF, 0, NZ - 1)
            values = look_up(table, material_ref[z] * 16 + pattern_ref[z])
        packed[n // 32] = jnp.where(
            slot == n % 32, roll(values, 4 * (n % 32), 1), packed[n // 32]
        )
    for k in range(2):
        cols_ref[k] = packed[k]


def plane_kernel(
    plane_ref, cols_ref, rows_ref, rot_ref, wave_ref, monitor_ref, spread_ref, all_ref
):
    rot = [rot_ref[k : k + 1, :] for k in range(8)]
    level = monitor_ref[0]

    def put(n, rows, main, side):
        all_ref[n, rows, 0:COLS] = main
        all_ref[n, rows, COLS:WIDE] = side

    def side_of(n):
        return roll(cols_ref[n // 32], -4 * (n % 32), 1)

    def foot_of(n):
        start = 4 * (n % 2)
        return rows_ref[n // 2, start : start + 4, :]

    def corner_of(n):
        return roll(rows_ref[CORNER + n // 32, 0:4, :], -4 * (n % 32), 1)

    body = slice(0, ROWS)
    foot = slice(ROWS, ROWS + 4)
    for n in range(HALF):
        m = n + HALF
        sides = turned(side_of(n), side_of(m), rot[6], rot[7])
        feet = turned(foot_of(n), foot_of(m), rot[0], rot[1])
        corners = turned(corner_of(n), corner_of(m), rot[6], rot[7])
        corners = turned(*corners, rot[0], rot[1])
        for part, at in enumerate((n, m)):
            put(at, body, plane_ref[at], sides[part])
            put(at, foot, feet[part], corners[part])
    for n in range(2 * HALF, COUNT):
        put(n, body, plane_ref[n], side_of(n))
        put(n, foot, foot_of(n), corner_of(n))

    def where(field, c, k, part):
        return NEAR.index((field, c, k)) + part * HALF

    def e_at(c, k, part):
        return all_ref[where(0, c, k, part)]

    def h_at(c, k, part):
        return all_ref[where(1, c, k, part)]

    def next_col(values):
        return roll(values, -1, 1)

    def prev_col(values):
        return roll(values, 1, 1)

    def update_h(k, part, wanted):
        above = level - 2 + k >= 0
        new = {}
        if 0 in wanted:
            ez, ey = e_at(2, k, part), e_at(1, k, part)
            new[0] = h_at(0, k, part) - STEP_DT * (
                next_col(ez) - ez - (e_at(1, k + 1, part) - ey)
            )
        if 1 in wanted:
            ez, ex = e_at(2, k, part), e_at(0, k, part)
            new[1] = h_at(1, k, part) - STEP_DT * (
                e_at(0, k + 1, part) - ex - (next_row(ez) - ez)
            )
        if 2 in wanted:
            ex, ey = e_at(0, k, part), e_at(1, k, part)
            new[2] = h_at(2, k, part) - STEP_DT * (
                next_row(ey) - ey - (next_col(ex) - ex)
            )
        for c, values in new.items():
            if k < 2:
                values = jnp.where(above, values, 0.0)
            all_ref[where(1, c, k, part)] = values

    def update_e(k, part, wanted):
        below = level - 2 + k < NZ
        coef = all_ref[2 * HALF + k - 1]
        hx, hy, hz = (h_at(c, k, part) for c in range(3)) if 2 not in wanted else (
            h_at(0, k, part),
            h_at(1, k, part),
            h_at(2, k, part) if k > 0 else None,
        )
        new = {}
        if 0 in wanted:
            new[0] = e_at(0, k, part) + coef * (
                hz - prev_col(hz) - (hy - h_at(1, k - 1, part))
            )
        if 1 in wanted:
            new[1] = e_at(1, k, part) + coef * (
                hx - h_at(0, k - 1, part) - (hz - prev_row(hz))
            )
        if 2 in wanted:
            new[2] = e_at(2, k, part) + coef * (
                hy - prev_row(hy) - (hx - prev_col(hx))
            )
        for c, values in new.items():
            if k > 2:
                values = jnp.where(below, values, 0.0)
            all_ref[where(0, c, k, part)] = values

    for part in range(2):
        for k in range(4):
            update_h(k, part, (0, 1, 2) if k > 0 else (0, 1))
        for k in range(1, 4):
            update_e(k, part, (0, 1, 2) if k < 3 else (0, 1))
        update_h(1, part, (0, 1))
        update_h(2, part, (0, 1, 2))
        update_e(2, part, (0, 1))

    def cells(c, part):
        values = all_ref[where(0, c, 2, part), 2 : ROWS + 2, :]
        return roll(values, -2, 1)[:, 0:COLS]

    re = jnp.concatenate([cells(c, 0) for c in range(2)], axis=0)
    im = jnp.concatenate([cells(c, 1) for c in range(2)], axis=0)
    y_section(re, im, wave_ref, spread_ref)


def table_kernel(
    count_x, count_y, phase_hbm, place_ref, after_hbm, rot_ref, y_ref, x_ref, phase_ref, sem
):
    fetched([(phase_hbm, phase_ref)], sem)
    index_x, index_y = place_ref[0], place_ref[1]
    theta_x, theta_y = phase_ref[0], phase_ref[1]
    total_x, total_y = ROWS * count_x, COLS * count_y
    row = lax.broadcasted_iota(jnp.int32, (8, COLS), 0)
    angle = jnp.where(row < 4, theta_x, theta_y)
    flags = [
        jnp.where(flag, 1, 0)
        for flag in (index_x == count_x - 1, index_x == 0, index_y == 0, index_y == count_y - 1)
    ]
    here = jnp.where(
        row < 4,
        jnp.where(row < 2, flags[0], flags[1]),
        jnp.where(row < 6, flags[2], flags[3]),
    )
    angle = jnp.where(here == 1, angle, 0.0)
    angle = jnp.where(row // 2 == 1, -angle, jnp.where(row // 2 == 2, -angle, angle))
    rot_ref[...] = jnp.where(row % 2 == 0, jnp.cos(angle), jnp.sin(angle))

    def angles(order, place, total, theta):
        product = (order * place) & (total - 1)
        return (
            2.0 * math.pi * product.astype(jnp.float32) + theta * place.astype(jnp.float32)
        ) / total

    scale = 1.0 / math.sqrt(total_x * total_y)
    shape = (COLS, ORD_Y)
    place = index_y * COLS + 2 + lax.broadcasted_iota(jnp.int32, shape, 0)
    order = lax.broadcasted_iota(jnp.int32, shape, 1) - ORD_Y // 2
    angle = angles(order, place, total_y, theta_y)
    y_ref[0:COLS, :] = jnp.cos(angle) * scale
    y_ref[COLS:, :] = jnp.sin(angle) * scale
    shape = (ORD_X, 2 * ROWS)
    lane = lax.broadcasted_iota(jnp.int32, shape, 1)
    place = index_x * ROWS + 2 + lane % ROWS
    order = lax.broadcasted_iota(jnp.int32, shape, 0) - ORD_X // 2
    angle = angles(order, place, total_x, theta_x)
    x_ref[...] = jnp.where(lane < ROWS, jnp.cos(angle), jnp.sin(angle))


def params(mebibytes):
    return pltpu.CompilerParams(vmem_limit_bytes=mebibytes << 20)


def cost(microseconds):
    return pl.CostEstimate(
        flops=0, bytes_accessed=microseconds * 3_000_000, transcendentals=0
    )


def f32(*shape):
    return jax.ShapeDtypeStruct(shape, jnp.float32)


def shards(
    e_field, h_field, material, pattern, base_eps, mode_table, nodes, bloch_phase, monitor_z
):
    count_x = lax.axis_size("gx")
    count_y = lax.axis_size("gy")
    index_x = lax.axis_index("gx")
    index_y = lax.axis_index("gy")
    each_p = ORD_X // count_x
    each_q = ORD_Y // count_y
    vmem = pl.BlockSpec(memory_space=VMEM)
    smem = pl.BlockSpec(memory_space=SMEM)
    hbm = pl.BlockSpec(memory_space=pltpu.HBM)
    f32_vmem = lambda *shape: VMEM(shape, jnp.float32)
    tables = [
        SMEM(base_eps.shape, jnp.float32),
        SMEM(mode_table.shape, jnp.float32),
        SMEM(nodes.shape, jnp.float32),
    ]

    cols = pl.pallas_call(
        near_kernel,
        out_shape=f32(2, ROWS, COLS),
        in_specs=[hbm] * 8,
        out_specs=vmem,
        scratch_shapes=[
            f32_vmem(*e_field.shape),
            f32_vmem(*h_field.shape),
            VMEM(material.shape, jnp.int32),
            VMEM(pattern.shape, jnp.int32),
            *tables,
            SMEM((1,), jnp.int32),
            pltpu.SemaphoreType.DMA((8,)),
        ],
        compiler_params=params(60),
        name="near",
    )(e_field, h_field, material, pattern, base_eps, mode_table, nodes, monitor_z)
    near_cols = passed_along(cols, "gy", -1)

    planes, coef, own, first, last = pl.pallas_call(
        rows_kernel,
        out_shape=(
            f32(COUNT, ROWS, COLS),
            f32(NZ, ROWS, COLS),
            f32(13, ROWS, COLS),
            f32(CORNER + 2, 8, COLS),
            f32(MAIN_BLOCKS, 8, COLS),
        ),
        in_specs=[hbm] * 9,
        out_specs=(vmem,) * 5,
        scratch_shapes=[
            f32_vmem(*e_field.shape),
            f32_vmem(*h_field.shape),
            VMEM(material.shape, jnp.int32),
            VMEM(pattern.shape, jnp.int32),
            *tables,
            SMEM((1,), jnp.int32),
            pltpu.SemaphoreType.DMA((8,)),
        ],
        compiler_params=params(60),
        cost_estimate=cost(0),
        name="rows",
    )(e_field, h_field, material, pattern, base_eps, mode_table, nodes, monitor_z, cols)
    first = lax.dynamic_update_slice(first, near_cols[:, 0:8], (CORNER, 0, 0))
    from_next = passed_along(first, "gx", -1)
    from_prev = passed_along(last, "gx", 1)
    rot, y_wave, x_wave = pl.pallas_call(
        functools.partial(table_kernel, count_x, count_y),
        out_shape=(f32(8, COLS), f32(2 * COLS, ORD_Y), f32(ORD_X, 2 * ROWS)),
        in_specs=[hbm, smem, hbm],
        out_specs=(vmem,) * 3,
        scratch_shapes=[SMEM((2,), jnp.float32), pltpu.SemaphoreType.DMA((1,))],
        compiler_params=params(8),
        cost_estimate=cost(0),
        name="tables",
    )(bloch_phase, jnp.stack([index_x, index_y]), near_cols)
    spread = pl.pallas_call(
        plane_kernel,
        out_shape=f32(count_y, ROWS, 4 * each_q),
        in_specs=[vmem] * 5 + [smem],
        out_specs=vmem,
        scratch_shapes=[f32_vmem(COUNT, EXT, WIDE)],
        compiler_params=params(12),
        cost_estimate=cost(0),
        name="plane",
    )(planes, near_cols, from_next, rot, y_wave, monitor_z)
    tail, right, left = pl.pallas_call(
        pack_kernel,
        out_shape=(f32(13, 8, COLS), f32(4, EXT, COLS), f32(4, EXT, COLS)),
        in_specs=[vmem] * 5,
        out_specs=(vmem,) * 3,
        compiler_params=params(8),
        cost_estimate=cost(0),
        name="pack",
    )(own, from_next, from_prev, rot, spread)
    from_right = passed_along(right, "gy", 1)
    from_left = passed_along(left, "gy", -1)
    got = lax.all_to_all(spread, "gy", 0, 0, tiled=True)
    partial = pl.pallas_call(
        x_kernel,
        out_shape=f32(count_x, each_p, 4 * each_q),
        in_specs=[vmem, vmem],
        out_specs=vmem,
        compiler_params=params(8),
        cost_estimate=cost(0),
        name="x_section",
    )(got, x_wave)
    got = lax.all_to_all(partial, "gx", 0, 0, tiled=True)
    e_out, h_out = pl.pallas_call(
        field_kernel,
        out_shape=(f32(*e_field.shape), f32(*h_field.shape)),
        in_specs=[hbm] * 11,
        out_specs=(hbm, hbm),
        scratch_shapes=[
            f32_vmem(2, 3, NZ + 1, EXT, COLS),
            f32_vmem(2, 3, NZ + 1, EXT, COLS),
            f32_vmem(NZ, EXT, COLS),
            f32_vmem(13, EXT, COLS),
            f32_vmem(4, EXT, COLS),
            f32_vmem(4, EXT, COLS),
            f32_vmem(CORNER + 2, 8, COLS),
            f32_vmem(MAIN_BLOCKS, 8, COLS),
            f32_vmem(8, COLS),
            f32_vmem(2, 4, 2, EXT, COLS),
            pltpu.SemaphoreType.DMA((12,)),
        ],
        compiler_params=params(60),
        cost_estimate=cost(0),
        name="fields",
    )(
        e_field,
        h_field,
        coef,
        own,
        tail,
        from_right,
        from_left,
        from_next,
        from_prev,
        rot,
        partial,
    )
    orders = pl.pallas_call(
        sum_kernel,
        out_shape=f32(2, 2, each_p, each_q),
        in_specs=[vmem],
        out_specs=vmem,
        compiler_params=params(8),
        cost_estimate=cost(0),
        name="order_sum",
    )(got)
    return e_out, h_out, orders


def solution(mesh):
    grid = P(None, None, None, "gx", "gy")
    cells = P(None, "gx", "gy")
    return jax.shard_map(
        shards,
        mesh=mesh,
        in_specs=(grid, grid, cells, cells, P(), P(), P(), P(), P()),
        out_specs=(grid, grid, P(None, None, "gx", "gy")),
        check_vma=False,
    )
```

```python
import functools
import math

import jax
import jax.numpy as jnp
from jax import lax
from jax.experimental import pallas as pl
from jax.experimental.pallas import tpu as pltpu
from jax.sharding import PartitionSpec as P

STEP_DT = 0.5
ORD_X = 256
ORD_Y = 256
NZ = 16
ROWS = 32
COLS = 128
EXT = 40
MAIN_BLOCKS = 52
VMEM = pltpu.VMEM
SMEM = pltpu.SMEM


def swapped(block, axis, first):
    count = lax.axis_size(axis)
    route = []
    for i in range(count):
        ahead = (i % 2 == 0) == first
        route.append((i, (i + 1) % count if ahead else (i - 1) % count))
    return lax.ppermute(block, axis, route)


def roll(values, shift, axis):
    size = values.shape[axis]
    if isinstance(shift, int):
        shift = shift % size
        if shift == 0:
            return values
    return pltpu.roll(values, shift, axis)


def lanes_of(shape):
    return lax.broadcasted_iota(jnp.int32, shape, len(shape) - 1)


def coef_table(base_ref, mode_ref, node_ref):
    lane = lanes_of((8, 128))
    material = lane // 16
    pattern = lane % 16
    base = jnp.zeros((8, 128), jnp.float32)
    for m in range(8):
        base = jnp.where(material == m, base_ref[m], base)
    change = jnp.zeros((8, 128), jnp.float32)
    for k in range(4):
        mode = jnp.zeros((8, 128), jnp.float32)
        for p in range(16):
            mode = jnp.where(pattern == p, mode_ref[k, p], mode)
        change = change + node_ref[k] * mode
    return STEP_DT / (base * (1.0 + change))


def look_up(table, pair):
    rows = [
        jnp.take_along_axis(table, pair[8 * r : 8 * r + 8], axis=1)
        for r in range(pair.shape[0] // 8)
    ]
    return jnp.concatenate(rows, axis=0)


def fetch(pairs, sem, first=0):
    copies = [
        pltpu.make_async_copy(source, target, sem.at[first + k])
        for k, (source, target) in enumerate(pairs)
    ]
    for copy in copies:
        copy.start()
    return copies


def arrived(copies):
    for copy in copies:
        copy.wait()


def is_even(axis):
    return lax.rem(lax.axis_index(axis), 2) == 0


def fetch_swapped(got, ahead_ref, behind_ref, even, sem, first):
    @pl.when(even)
    def _():
        fetch(((got[0], ahead_ref), (got[1], behind_ref)), sem, first)

    @pl.when(jnp.logical_not(even))
    def _():
        fetch(((got[1], ahead_ref), (got[0], behind_ref)), sem, first)

    return [
        pltpu.make_async_copy(got[k], ref, sem.at[first + k])
        for k, ref in enumerate((ahead_ref, behind_ref))
    ]


def plane_of(e_ref, h_ref, n, z):
    ref = e_ref if n < 6 else h_ref
    return ref[(n % 6) // 3, n % 3, z]


def rows_kernel(
    e_hbm,
    h_hbm,
    material_hbm,
    pattern_hbm,
    base_hbm,
    mode_hbm,
    node_hbm,
    table_ref,
    first_swap_ref,
    second_swap_ref,
    e_ref,
    h_ref,
    material_ref,
    pattern_ref,
    base_ref,
    mode_ref,
    node_ref,
    sem,
):
    small = fetch([(base_hbm, base_ref), (mode_hbm, mode_ref), (node_hbm, node_ref)], sem)
    ends = (slice(0, 8), slice(ROWS - 8, ROWS))
    large = fetch(
        [
            (source.at[..., end, :], target.at[k])
            for source, target in (
                (e_hbm, e_ref),
                (h_hbm, h_ref),
                (material_hbm, material_ref),
                (pattern_hbm, pattern_ref),
            )
            for k, end in enumerate(ends)
        ],
        sem,
        3,
    )
    even = is_even("gx")
    arrived(small)
    table = coef_table(base_ref, mode_ref, node_ref)
    table_ref[...] = table
    arrived(large)
    for n in range(13):
        for quad in range(NZ // 4):
            blocks = []
            for k in range(2):
                pieces = []
                for z in range(4 * quad, 4 * quad + 4):
                    if n == 12:
                        values = look_up(table, material_ref[k, z] * 16 + pattern_ref[k, z])
                    else:
                        ref = e_ref if n < 6 else h_ref
                        values = ref[k, (n % 6) // 3, n % 3, z]
                    pieces.append(values[6 * k : 6 * k + 2])
                blocks.append(jnp.concatenate(pieces, axis=0))
            first_swap_ref[4 * n + quad] = jnp.where(even, blocks[1], blocks[0])
            second_swap_ref[4 * n + quad] = jnp.where(even, blocks[0], blocks[1])


def own_kernel(
    e_hbm,
    h_hbm,
    material_hbm,
    pattern_hbm,
    table_hbm,
    own_ref,
    coef_ref,
    e_ref,
    h_ref,
    material_ref,
    pattern_ref,
    table_ref,
    sem,
):
    small = fetch(
        [(material_hbm, material_ref), (pattern_hbm, pattern_ref), (table_hbm, table_ref)], sem
    )
    large = fetch([(e_hbm, e_ref), (h_hbm, h_ref)], sem, 3)
    arrived(small)
    table = table_ref[...]
    for z in range(NZ):
        coef_ref[z] = look_up(table, material_ref[z] * 16 + pattern_ref[z])
    arrived(large)
    group = lanes_of((ROWS, COLS)) // 8
    for n in range(13):
        packed = jnp.zeros((ROWS, COLS), jnp.float32)
        for z in range(NZ):
            values = coef_ref[z] if n == 12 else plane_of(e_ref, h_ref, n, z)
            packed = jnp.where(group == z, roll(values, 8 * z + 6, 1), packed)
        own_ref[n] = packed


def bloch_factors(theta_x, theta_y):
    count_x, count_y = lax.axis_size("gx"), lax.axis_size("gy")
    index_x, index_y = lax.axis_index("gx"), lax.axis_index("gy")
    row = lax.broadcasted_iota(jnp.int32, (8, COLS), 0)
    angle = jnp.where(row < 4, theta_x, theta_y)
    flags = [
        jnp.where(flag, 1, 0)
        for flag in (index_x == count_x - 1, index_x == 0, index_y == 0, index_y == count_y - 1)
    ]
    here = jnp.where(
        row < 4,
        jnp.where(row < 2, flags[0], flags[1]),
        jnp.where(row < 6, flags[2], flags[3]),
    )
    angle = jnp.where(here == 1, angle, 0.0)
    angle = jnp.where(row // 2 == 1, -angle, jnp.where(row // 2 == 2, -angle, angle))
    return jnp.where(row % 2 == 0, jnp.cos(angle), jnp.sin(angle))


def pack_kernel(
    own_hbm,
    rows_a_hbm,
    rows_b_hbm,
    phase_hbm,
    all_ref,
    first_swap_ref,
    second_swap_ref,
    rot_ref,
    own_ref,
    next_ref,
    prev_ref,
    phase_ref,
    sem,
):
    small = fetch([(phase_hbm, phase_ref)], sem)
    copies = fetch([(own_hbm, own_ref)], sem, 1)
    copies += fetch_swapped(
        (rows_a_hbm, rows_b_hbm), next_ref, prev_ref, is_even("gx"), sem, 2
    )
    even = is_even("gy")
    arrived(small)
    rot_ref[...] = bloch_factors(phase_ref[0], phase_ref[1])
    arrived(copies)
    rot = [rot_ref[k : k + 1, :] for k in range(8)]
    group = lanes_of((2, COLS)) // 8
    place = lanes_of((EXT, COLS)) % 8
    for n in range(13):
        all_ref[n, 0:ROWS, :] = own_ref[n]
        all_ref[n, ROWS:EXT, :] = jnp.zeros((EXT - ROWS, COLS), jnp.float32)
    for ref, row, cos, sin in ((next_ref, 32, rot[0], rot[1]), (prev_ref, 38, rot[2], rot[3])):
        for n in (0, 1, 2, 6, 7, 8, 12):
            parts = 1 if n == 12 else 2
            packed = [jnp.zeros((2, COLS), jnp.float32) for _ in range(parts)]
            for quad in range(NZ // 4):
                values = [ref[4 * (n + 3 * part) + quad] for part in range(parts)]
                if parts == 2:
                    values = turned(values[0], values[1], cos, sin)
                for k in range(4):
                    z = 4 * quad + k
                    for part in range(parts):
                        packed[part] = jnp.where(
                            group == z,
                            roll(values[part][2 * k : 2 * k + 2], 8 * z + 6, 1),
                            packed[part],
                        )
            for part in range(parts):
                all_ref[n + 3 * part, row : row + 2, :] = packed[part]
    for c in range(4):
        if c == 3:
            right = left = all_ref[12]
        else:
            e_re, e_im, h_re, h_im = (all_ref[3 * k + c] for k in range(4))
            right = jnp.where(
                place < 4,
                jnp.where(place < 2, roll(h_re, -4, 1), roll(h_im, -2, 1)),
                jnp.where(place < 6, e_re, roll(e_im, 2, 1)),
            )
            left = jnp.where(
                place < 4,
                jnp.where(place < 2, roll(h_im, -6, 1), roll(h_re, -4, 1)),
                jnp.where(place < 6, roll(e_im, -2, 1), e_re),
            )
        first_swap_ref[c] = jnp.where(even, right, left)
        second_swap_ref[c] = jnp.where(even, left, right)


def turned(re, im, cos, sin):
    return re * cos - im * sin, im * cos + re * sin


def strip_of(own, right, left, rot):
    place = lanes_of(own[0].shape) % 8

    def joined(index, from_right, from_left):
        return jnp.where(
            place < 4,
            jnp.where(place < 2, roll(own[index], -4, 1), from_left),
            jnp.where(place < 6, from_right, own[index]),
        )

    strip = [None] * 13
    for c in range(3):
        r = right[c]
        l = left[c]
        e_right = turned(r, roll(r, -2, 1), rot[4], rot[5])
        h_right = turned(roll(r, 4, 1), roll(r, 2, 1), rot[4], rot[5])
        e_left = turned(roll(l, -4, 1), roll(l, -2, 1), rot[6], rot[7])
        h_left = turned(l, roll(l, 2, 1), rot[6], rot[7])
        for part in range(2):
            strip[3 * part + c] = joined(3 * part + c, e_right[part], e_left[part])
            strip[6 + 3 * part + c] = joined(6 + 3 * part + c, h_right[part], h_left[part])
    strip[12] = joined(12, right[3], roll(left[3], -4, 1))
    return strip


def next_row(values):
    return roll(values, -1, 0)


def prev_row(values):
    return roll(values, 1, 0)


def h_new(h, e, e_up, e_xn, e_yn):
    return (
        h[0] - STEP_DT * (e_yn[1] - e[2] - (e_up[1] - e[1])),
        h[1] - STEP_DT * (e_up[0] - e[0] - (e_xn[1] - e[2])),
        h[2] - STEP_DT * (e_xn[0] - e[1] - (e_yn[0] - e[0])),
    )


def e_new(e, h, h_down, h_xp, h_yp, coef):
    return (
        e[0] + coef * (h[2] - h_yp[1] - (h[1] - h_down[1])),
        e[1] + coef * (h[0] - h_down[0] - (h[2] - h_xp[1])),
        e[2] + coef * (h[1] - h_xp[0] - (h[0] - h_yp[0])),
    )


def strip_h(h, e):
    up = lanes_of((EXT, COLS)) < 8 * (NZ - 1)
    above = [jnp.where(up, roll(e[c], -8, 1), 0.0) for c in range(2)]
    return h_new(
        h,
        e,
        above,
        (next_row(e[1]), next_row(e[2])),
        (roll(e[0], -1, 1), roll(e[2], -1, 1)),
    )


def strip_e(e, h, coef):
    up = lanes_of((EXT, COLS)) >= 8
    below = [jnp.where(up, roll(h[c], 8, 1), 0.0) for c in range(2)]
    return e_new(
        e,
        h,
        below,
        (prev_row(h[1]), prev_row(h[2])),
        (roll(h[0], 1, 1), roll(h[2], 1, 1)),
        coef,
    )


def fetch_edges(own_hbm, rows_hbm, cols_hbm, rot_hbm, edges, sem, first):
    own_ref, next_ref, prev_ref, right_ref, left_ref, rot_ref = edges
    copies = fetch([(own_hbm, own_ref), (rot_hbm, rot_ref)], sem, first)
    copies += fetch_swapped(rows_hbm, next_ref, prev_ref, is_even("gx"), sem, first + 2)
    copies += fetch_swapped(cols_hbm, left_ref, right_ref, is_even("gy"), sem, first + 4)
    return copies


def edge_scratch():
    return [
        VMEM(shape, jnp.float32)
        for shape in (
            (13, EXT, COLS),
            (MAIN_BLOCKS, 8, COLS),
            (MAIN_BLOCKS, 8, COLS),
            (4, EXT, COLS),
            (4, EXT, COLS),
            (8, COLS),
        )
    ]


def block_scratch(parts):
    return [
        VMEM((parts, 3, NZ + 1, EXT, COLS), jnp.float32),
        VMEM((parts, 3, NZ + 1, EXT, COLS), jnp.float32),
        VMEM((NZ, EXT, COLS), jnp.float32),
        VMEM((parts, 4, 2, EXT, COLS), jnp.float32),
    ]


def fill_edges(edges, block, parts):
    own_ref, next_ref, prev_ref, right_ref, left_ref, rot_ref = edges
    e_all, h_all, coef_all, edge_ref = block
    rot = [rot_ref[k : k + 1, :] for k in range(8)]
    for at in range(len(parts)):
        for c in range(3):
            e_all[at, c, NZ] = jnp.zeros((EXT, COLS), jnp.float32)
            h_all[at, c, 0] = jnp.zeros((EXT, COLS), jnp.float32)
    for ref, row, cos, sin in ((next_ref, 32, rot[0], rot[1]), (prev_ref, 38, rot[2], rot[3])):
        for field in range(2):
            dest = h_all if field else e_all
            for c in range(3):
                for quad in range(4):
                    re = ref[(6 * field + c) * 4 + quad]
                    im = ref[(6 * field + 3 + c) * 4 + quad]
                    both = turned(re, im, cos, sin)
                    for at, part in enumerate(parts):
                        for k in range(4):
                            z = 4 * quad + k + field
                            dest[at, c, z, row : row + 2, :] = both[part][2 * k : 2 * k + 2]
        for quad in range(4):
            values = ref[48 + quad]
            for k in range(4):
                coef_all[4 * quad + k, row : row + 2, :] = values[2 * k : 2 * k + 2]
    strip = strip_of(
        [own_ref[a] for a in range(13)],
        [right_ref[a] for a in range(4)],
        [left_ref[a] for a in range(4)],
        rot,
    )
    for at, part in enumerate(parts):
        e = tuple(strip[3 * part + c] for c in range(3))
        h = tuple(strip[6 + 3 * part + c] for c in range(3))
        for step in range(2):
            edge_ref[at, 2 * step, 0] = e[0]
            edge_ref[at, 2 * step, 1] = e[2]
            h = strip_h(h, e)
            edge_ref[at, 2 * step + 1, 0] = h[0]
            edge_ref[at, 2 * step + 1, 1] = h[2]
            if step == 0:
                e = strip_e(e, h, strip[12])


def updates(block, parts):
    e_all, h_all, coef_all, edge_ref = block
    lane = lanes_of((EXT, COLS))

    def next_col(values, edge, z):
        edge = roll(edge, lax.rem(COLS + 125 - 8 * z, COLS), 1)
        return jnp.where(lane == COLS - 1, edge, roll(values, -1, 1))

    def prev_col(values, edge, z):
        edge = roll(edge, lax.rem(COLS + 123 - 8 * z, COLS), 1)
        return jnp.where(lane == 0, edge, roll(values, 1, 1))

    def do_h(step, layers):
        new = []
        for at in range(parts):
            for z in layers:
                e = tuple(e_all[at, c, z] for c in range(3))
                h = tuple(h_all[at, c, z + 1] for c in range(3))
                e_up = (e_all[at, 0, z + 1], e_all[at, 1, z + 1])
                e_yn = (
                    next_col(e[0], edge_ref[at, 2 * step, 0], z),
                    next_col(e[2], edge_ref[at, 2 * step, 1], z),
                )
                values = h_new(h, e, e_up, (next_row(e[1]), next_row(e[2])), e_yn)
                new.append((at, z, values))
        for at, z, values in new:
            for c in range(3):
                h_all[at, c, z + 1] = values[c]

    def do_e(step, layers):
        new = []
        for at in range(parts):
            for z in layers:
                e = tuple(e_all[at, c, z] for c in range(3))
                h = tuple(h_all[at, c, z + 1] for c in range(3))
                h_down = (h_all[at, 0, z], h_all[at, 1, z])
                h_yp = (
                    prev_col(h[0], edge_ref[at, 2 * step + 1, 0], z),
                    prev_col(h[2], edge_ref[at, 2 * step + 1, 1], z),
                )
                values = e_new(
                    e, h, h_down, (prev_row(h[1]), prev_row(h[2])), h_yp, coef_all[z]
                )
                new.append((at, z, values))
        for at, z, values in new:
            for c in range(3):
                e_all[at, c, z] = values[c]

    return do_h, do_e


def plane_kernel(
    e_hbm,
    h_hbm,
    coef_hbm,
    own_hbm,
    rows_a_hbm,
    rows_b_hbm,
    cols_a_hbm,
    cols_b_hbm,
    rot_hbm,
    wave_hbm,
    monitor_hbm,
    spread_ref,
    *scratch,
):
    edges, block = scratch[0:6], scratch[6:10]
    wave_ref, monitor_ref, sem = scratch[10:13]
    e_all, h_all, coef_all, edge_ref = block
    scalar = fetch([(monitor_hbm, monitor_ref)], sem)
    copies = fetch_edges(
        own_hbm,
        (rows_a_hbm, rows_b_hbm),
        (cols_a_hbm, cols_b_hbm),
        rot_hbm,
            edges,
        sem,
        1,
    )
    arrived(scalar)
    level = monitor_ref[0]
    low = jnp.clip(level - 2, 0, NZ - 5)
    large = fetch(
        [
            (e_hbm.at[:, :, pl.ds(low, 5)], e_all.at[:, :, pl.ds(low, 5), 0:ROWS, :]),
            (h_hbm.at[:, :, pl.ds(low, 5)], h_all.at[:, :, pl.ds(low + 1, 5), 0:ROWS, :]),
            (coef_hbm.at[pl.ds(low, 5)], coef_all.at[pl.ds(low, 5), 0:ROWS, :]),
            (wave_hbm, wave_ref),
        ],
        sem,
        7,
    )
    arrived(copies)
    fill_edges(edges, block, (0, 1))
    arrived(large)
    near = {}
    for k in range(-2, 3):
        z = jnp.clip(level + k, 0, NZ - 1)
        for part in range(2):
            for c in range(3):
                if c < 2 or k < 2:
                    e = e_all[part, c, z]
                    near["e", part, c, k] = jnp.where(level + k < NZ, e, 0.0) if k > 0 else e
                if k < 2 and (c < 2 or k > -2):
                    h = h_all[part, c, z + 1]
                    near["h", part, c, k] = jnp.where(level + k >= 0, h, 0.0) if k < 0 else h
    lane = lanes_of((EXT, COLS))

    def next_col(values, edge, z):
        edge = roll(edge, lax.rem(COLS + 125 - 8 * z, COLS), 1)
        return jnp.where(lane == COLS - 1, edge, roll(values, -1, 1))

    def prev_col(values, edge, z):
        edge = roll(edge, lax.rem(COLS + 123 - 8 * z, COLS), 1)
        return jnp.where(lane == 0, edge, roll(values, 1, 1))

    def update_h(step, part, k, wanted):
        z = jnp.clip(level + k, 0, NZ - 1)
        ex, ey, ez = (near["e", part, c, k] for c in range(3))
        edge = edge_ref.at[part, 2 * step]
        new = {}
        if 0 in wanted:
            new[0] = next_col(ez, edge[1], z) - ez - (near["e", part, 1, k + 1] - ey)
        if 1 in wanted:
            new[1] = near["e", part, 0, k + 1] - ex - (next_row(ez) - ez)
        if 2 in wanted:
            new[2] = next_row(ey) - ey - (next_col(ex, edge[0], z) - ex)
        for c, curl in new.items():
            values = near["h", part, c, k] - STEP_DT * curl
            near["h", part, c, k] = jnp.where(level + k >= 0, values, 0.0) if k < 0 else values

    def update_e(step, part, k, wanted):
        z = jnp.clip(level + k, 0, NZ - 1)
        hx, hy, hz = (near["h", part, c, k] for c in range(3))
        edge = edge_ref.at[part, 2 * step + 1]
        coef = coef_all[z]
        new = {}
        if 0 in wanted:
            new[0] = hz - prev_col(hz, edge[1], z) - (hy - near["h", part, 1, k - 1])
        if 1 in wanted:
            new[1] = hx - near["h", part, 0, k - 1] - (hz - prev_row(hz))
        if 2 in wanted:
            new[2] = hy - prev_row(hy) - (hx - prev_col(hx, edge[0], z))
        for c, curl in new.items():
            values = near["e", part, c, k] + coef * curl
            near["e", part, c, k] = jnp.where(level + k < NZ, values, 0.0) if k > 0 else values

    for part in range(2):
        for k in range(-2, 2):
            update_h(0, part, k, (0, 1, 2) if k > -2 else (0, 1))
        for k in range(-1, 2):
            update_e(0, part, k, (0, 1, 2) if k < 1 else (0, 1))
        update_h(1, part, -1, (0, 1))
        update_h(1, part, 0, (0, 1, 2))
        update_e(1, part, 0, (0, 1))
    re, im = (
        jnp.concatenate([near["e", part, c, 0][0:ROWS] for c in range(2)], axis=0)
        for part in range(2)
    )
    y_section(re, im, wave_ref, spread_ref)


def field_kernel(parts, inputs, *refs):
    (
        e_hbm,
        h_hbm,
        coef_hbm,
        own_hbm,
        rows_a_hbm,
        rows_b_hbm,
        cols_a_hbm,
        cols_b_hbm,
        rot_hbm,
        ) = refs[0:9]
    e_out, h_out = refs[inputs : inputs + 2]
    scratch = refs[inputs + 2 :]
    edges, block, sem = scratch[0:6], scratch[6:10], scratch[10]
    e_all, h_all, coef_all, _ = block
    copies = fetch_edges(
        own_hbm,
        (rows_a_hbm, rows_b_hbm),
        (cols_a_hbm, cols_b_hbm),
        rot_hbm,
            edges,
        sem,
        0,
    )
    large = fetch(
        [
            (coef_hbm, coef_all.at[:, 0:ROWS, :]),
            (e_hbm.at[parts[0] : parts[-1] + 1], e_all.at[:, :, 0:NZ, 0:ROWS, :]),
            (h_hbm.at[parts[0] : parts[-1] + 1], h_all.at[:, :, 1 : NZ + 1, 0:ROWS, :]),
        ],
        sem,
        6,
    )
    arrived(copies)
    fill_edges(edges, block, parts)
    arrived(large)
    do_h, do_e = updates(block, len(parts))

    def sweep(update, step, store=None):
        def layers(quad, carry):
            start = 4 * quad
            update(step, [start + k for k in range(4)])
            if store is not None:
                store(start)
            return carry

        lax.fori_loop(0, NZ // 4, layers, 0)

    def store_h(start):
        fetch(
            [
                (
                    h_all.at[at, :, pl.ds(start + 1, 4), 0:ROWS, :],
                    h_out.at[part, :, pl.ds(start, 4)],
                )
                for at, part in enumerate(parts)
            ],
            sem,
            10,
        )

    def store_e(start):
        fetch(
            [
                (
                    e_all.at[at, :, pl.ds(start, 4), 0:ROWS, :],
                    e_out.at[part, :, pl.ds(start, 4)],
                )
                for at, part in enumerate(parts)
            ],
            sem,
            12,
        )

    sweep(do_h, 0)
    sweep(do_e, 0)
    sweep(do_h, 1, store_h)
    sweep(do_e, 1, store_e)
    for at, part in enumerate(parts):
        pltpu.make_async_copy(
            h_all.at[at, :, 1 : NZ + 1, 0:ROWS, :], h_out.at[part], sem.at[10 + at]
        ).wait()
        pltpu.make_async_copy(
            e_all.at[at, :, 0:NZ, 0:ROWS, :], e_out.at[part], sem.at[12 + at]
        ).wait()


def y_section(re, im, wave_ref, spread_ref):
    wave = wave_ref[...]
    owners, _, lanes = spread_ref.shape
    each = lanes // 4
    out = [
        jnp.dot(
            jnp.concatenate(pair, axis=1),
            wave,
            precision=lax.Precision.HIGHEST,
            preferred_element_type=jnp.float32,
        )
        for pair in ((re, im), (im, -re))
    ]
    for owner in range(owners):
        pieces = [
            out[part][c * ROWS : (c + 1) * ROWS, owner * each : (owner + 1) * each]
            for part in range(2)
            for c in range(2)
        ]
        spread_ref[owner] = jnp.concatenate(pieces, axis=1)


def x_kernel(got_ref, wave_ref, part_ref):
    total = got_ref[0]
    for source in range(1, got_ref.shape[0]):
        total = total + got_ref[source]
    half = total.shape[1] // 2
    other = roll(total, half, 1)
    other = jnp.where(lanes_of(other.shape) < half, other, -other)
    result = jnp.dot(
        wave_ref[...],
        jnp.concatenate([total, other], axis=0),
        precision=lax.Precision.HIGHEST,
        preferred_element_type=jnp.float32,
    )
    part_ref[...] = result.reshape(part_ref.shape)


def sum_kernel(got_ref, out_ref):
    total = got_ref[0]
    for source in range(1, got_ref.shape[0]):
        total = total + got_ref[source]
    each = total.shape[1] // 4
    for c in range(2):
        for part in range(2):
            start = (2 * part + c) * each
            out_ref[c, part] = total[:, start : start + each]


def table_kernel(
    count_x, count_y, phase_hbm, after_hbm, y_ref, x_ref, phase_ref, sem
):
    arrived(fetch([(phase_hbm, phase_ref)], sem))
    index_x, index_y = lax.axis_index("gx"), lax.axis_index("gy")
    theta_x, theta_y = phase_ref[0], phase_ref[1]
    total_x, total_y = ROWS * count_x, COLS * count_y

    def waves(product, place, total, theta):
        angle = (
            2.0 * math.pi * (product & (total - 1)).astype(jnp.float32)
            + theta * place.astype(jnp.float32)
        ) / total
        return jnp.cos(angle), jnp.sin(angle)

    def joined(a, b):
        return a[0] * b[0] - a[1] * b[1], a[1] * b[0] + a[0] * b[1]

    scale = 1.0 / math.sqrt(total_x * total_y)
    blocks = COLS // 8
    start = index_y * COLS
    order = lax.broadcasted_iota(jnp.int32, (blocks, ORD_Y), 1) - ORD_Y // 2
    place = start + 8 * lax.broadcasted_iota(jnp.int32, (blocks, ORD_Y), 0)
    coarse = waves(order * place, place, total_y, theta_y)
    place = lax.broadcasted_iota(jnp.int32, (8, ORD_Y), 0)
    fine = waves(order[0:8] * place, place, total_y, theta_y)
    fine = (fine[0] * scale, fine[1] * scale)
    for block in range(blocks):
        part = tuple(values[block : block + 1] for values in coarse)
        cos, sin = joined(part, fine)
        y_ref[8 * block : 8 * block + 8, :] = cos
        y_ref[COLS + 8 * block : COLS + 8 * block + 8, :] = sin
    blocks = ORD_X // 8
    shape = (blocks, 2 * ROWS)
    place = index_x * ROWS + lax.broadcasted_iota(jnp.int32, shape, 1) % ROWS
    order = 8 * lax.broadcasted_iota(jnp.int32, shape, 0) - ORD_X // 2
    coarse = waves(order * place, place, total_x, theta_x)
    order = lax.broadcasted_iota(jnp.int32, (8, 2 * ROWS), 0)
    fine = waves(order * place[0:8], place[0:8], total_x, 0.0)
    lane = lax.broadcasted_iota(jnp.int32, (8, 2 * ROWS), 1)
    for block in range(blocks):
        part = tuple(values[block : block + 1] for values in coarse)
        cos, sin = joined(part, fine)
        x_ref[8 * block : 8 * block + 8, :] = jnp.where(lane < ROWS, cos, sin)


def params(mebibytes):
    return pltpu.CompilerParams(vmem_limit_bytes=mebibytes << 20)


def cost(microseconds):
    return pl.CostEstimate(
        flops=0, bytes_accessed=microseconds * 3_000_000, transcendentals=0
    )


def f32(*shape):
    return jax.ShapeDtypeStruct(shape, jnp.float32)


def shards(
    e_field, h_field, material, pattern, base_eps, mode_table, nodes, bloch_phase, monitor_z
):
    count_x = lax.axis_size("gx")
    count_y = lax.axis_size("gy")
    each_p = ORD_X // count_x
    each_q = ORD_Y // count_y
    vmem = pl.BlockSpec(memory_space=VMEM)
    hbm = pl.BlockSpec(memory_space=pltpu.HBM)
    f32_vmem = lambda *shape: VMEM(shape, jnp.float32)
    dma = pltpu.SemaphoreType.DMA

    table, rows_a, rows_b = pl.pallas_call(
        rows_kernel,
        out_shape=(
            f32(8, COLS),
            f32(MAIN_BLOCKS, 8, COLS),
            f32(MAIN_BLOCKS, 8, COLS),
        ),
        in_specs=[hbm] * 7,
        out_specs=(vmem,) * 3,
        scratch_shapes=[
            f32_vmem(2, 2, 3, NZ, 8, COLS),
            f32_vmem(2, 2, 3, NZ, 8, COLS),
            VMEM((2, NZ, 8, COLS), jnp.int32),
            VMEM((2, NZ, 8, COLS), jnp.int32),
            SMEM(base_eps.shape, jnp.float32),
            SMEM(mode_table.shape, jnp.float32),
            SMEM(nodes.shape, jnp.float32),
            dma((11,)),
        ],
        compiler_params=params(60),
        cost_estimate=cost(3),
        name="rows",
    )(e_field, h_field, material, pattern, base_eps, mode_table, nodes)
    rows_a = swapped(rows_a, "gx", True)
    rows_b = swapped(rows_b, "gx", False)
    own, coef = pl.pallas_call(
        own_kernel,
        out_shape=(f32(13, ROWS, COLS), f32(NZ, ROWS, COLS)),
        in_specs=[hbm] * 5,
        out_specs=(vmem,) * 2,
        scratch_shapes=[
            f32_vmem(*e_field.shape),
            f32_vmem(*h_field.shape),
            VMEM(material.shape, jnp.int32),
            VMEM(pattern.shape, jnp.int32),
            f32_vmem(8, COLS),
            dma((5,)),
        ],
        compiler_params=params(60),
        cost_estimate=cost(4),
        name="own",
    )(e_field, h_field, material, pattern, table)
    own, cols_a, cols_b, rot = pl.pallas_call(
        pack_kernel,
        out_shape=(
            f32(13, EXT, COLS),
            f32(4, EXT, COLS),
            f32(4, EXT, COLS),
            f32(8, COLS),
        ),
        in_specs=[hbm] * 4,
        out_specs=(vmem,) * 4,
        scratch_shapes=[
            f32_vmem(*own.shape),
            f32_vmem(MAIN_BLOCKS, 8, COLS),
            f32_vmem(MAIN_BLOCKS, 8, COLS),
            SMEM((2,), jnp.float32),
            dma((4,)),
        ],
        compiler_params=params(60),
        cost_estimate=cost(2),
        name="pack",
    )(own, rows_a, rows_b, bloch_phase)
    y_wave, x_wave = pl.pallas_call(
        functools.partial(table_kernel, count_x, count_y),
        out_shape=(f32(2 * COLS, ORD_Y), f32(ORD_X, 2 * ROWS)),
        in_specs=[hbm, hbm],
        out_specs=(vmem,) * 2,
        scratch_shapes=[SMEM((2,), jnp.float32), dma((1,))],
        compiler_params=params(60),
        cost_estimate=cost(2),
        name="tables",
    )(bloch_phase, rot)
    cols_b = swapped(cols_b, "gy", False)
    cols_a = swapped(cols_a, "gy", True)
    around = (e_field, h_field, coef, own, rows_a, rows_b, cols_a, cols_b, rot)
    spread = pl.pallas_call(
        plane_kernel,
        out_shape=f32(count_y, ROWS, 4 * each_q),
        in_specs=[hbm] * 11,
        out_specs=vmem,
        scratch_shapes=[
            *edge_scratch(),
            *block_scratch(2),
            f32_vmem(*y_wave.shape),
            SMEM((1,), jnp.int32),
            dma((11,)),
        ],
        compiler_params=params(60),
        cost_estimate=cost(3),
        name="plane",
    )(*around, y_wave, monitor_z)

    def fields(parts, after, before=()):
        return pl.pallas_call(
            functools.partial(field_kernel, parts, 10 + len(before)),
            out_shape=(f32(*e_field.shape), f32(*h_field.shape)),
            in_specs=[hbm] * (10 + len(before)),
            out_specs=(hbm, hbm),
            scratch_shapes=[*edge_scratch(), *block_scratch(len(parts)), dma((14,))],
            input_output_aliases={10 + k: k for k in range(len(before))},
            compiler_params=params(60),
            cost_estimate=cost(6),
            name="fields",
        )(*around, after, *before)

    got = lax.all_to_all(spread, "gy", 0, 0, tiled=True)
    partial = pl.pallas_call(
        x_kernel,
        out_shape=f32(count_x, each_p, 4 * each_q),
        in_specs=[vmem, vmem],
        out_specs=vmem,
        compiler_params=params(8),
        cost_estimate=cost(1),
        name="x_section",
    )(got, x_wave)
    got = lax.all_to_all(partial, "gx", 0, 0, tiled=True)
    e_out, h_out = fields((0, 1), partial)
    orders = pl.pallas_call(
        sum_kernel,
        out_shape=f32(2, 2, each_p, each_q),
        in_specs=[vmem],
        out_specs=vmem,
        compiler_params=params(8),
        cost_estimate=cost(1),
        name="order_sum",
    )(got)
    return e_out, h_out, orders


def solution(mesh):
    grid = P(None, None, None, "gx", "gy")
    cells = P(None, "gx", "gy")
    return jax.shard_map(
        shards,
        mesh=mesh,
        in_specs=(grid, grid, cells, cells, P(), P(), P(), P(), P()),
        out_specs=(grid, grid, P(None, None, "gx", "gy")),
        check_vma=False,
    )
```

```python
import functools
import math

import jax
import jax.numpy as jnp
from jax import lax
from jax.experimental import pallas as pl
from jax.experimental.pallas import tpu as pltpu
from jax.sharding import PartitionSpec as P

STEP_DT = 0.5
ORD_X = 256
ORD_Y = 256
NZ = 16
ROWS = 32
COLS = 128
EXT = 40
MAIN_BLOCKS = 52
VMEM = pltpu.VMEM
SMEM = pltpu.SMEM


def swapped(block, axis, first):
    count = lax.axis_size(axis)
    route = []
    for i in range(count):
        ahead = (i % 2 == 0) == first
        route.append((i, (i + 1) % count if ahead else (i - 1) % count))
    return lax.ppermute(block, axis, route)


def roll(values, shift, axis):
    size = values.shape[axis]
    if isinstance(shift, int):
        shift = shift % size
        if shift == 0:
            return values
    return pltpu.roll(values, shift, axis)


def lanes_of(shape):
    return lax.broadcasted_iota(jnp.int32, shape, len(shape) - 1)


def coef_table(base_ref, mode_ref, node_ref):
    lane = lanes_of((8, 128))
    material = lane // 16
    pattern = lane % 16
    base = jnp.zeros((8, 128), jnp.float32)
    for m in range(8):
        base = jnp.where(material == m, base_ref[m], base)
    change = jnp.zeros((8, 128), jnp.float32)
    for k in range(4):
        mode = jnp.zeros((8, 128), jnp.float32)
        for p in range(16):
            mode = jnp.where(pattern == p, mode_ref[k, p], mode)
        change = change + node_ref[k] * mode
    return STEP_DT / (base * (1.0 + change))


def look_up(table, pair):
    rows = [
        jnp.take_along_axis(table, pair[8 * r : 8 * r + 8], axis=1)
        for r in range(pair.shape[0] // 8)
    ]
    return jnp.concatenate(rows, axis=0)


def fetch(pairs, sem, first=0):
    copies = [
        pltpu.make_async_copy(source, target, sem.at[first + k])
        for k, (source, target) in enumerate(pairs)
    ]
    for copy in copies:
        copy.start()
    return copies


def arrived(copies):
    for copy in copies:
        copy.wait()


def is_even(axis):
    return lax.rem(lax.axis_index(axis), 2) == 0


def fetch_swapped(got, ahead_ref, behind_ref, even, sem, first):
    @pl.when(even)
    def _():
        fetch(((got[0], ahead_ref), (got[1], behind_ref)), sem, first)

    @pl.when(jnp.logical_not(even))
    def _():
        fetch(((got[1], ahead_ref), (got[0], behind_ref)), sem, first)

    return [
        pltpu.make_async_copy(got[k], ref, sem.at[first + k])
        for k, ref in enumerate((ahead_ref, behind_ref))
    ]


def plane_of(e_ref, h_ref, n, z):
    ref = e_ref if n < 6 else h_ref
    return ref[(n % 6) // 3, n % 3, z]


def rows_kernel(
    e_hbm,
    h_hbm,
    material_hbm,
    pattern_hbm,
    base_hbm,
    mode_hbm,
    node_hbm,
    table_ref,
    first_swap_ref,
    second_swap_ref,
    e_ref,
    h_ref,
    material_ref,
    pattern_ref,
    base_ref,
    mode_ref,
    node_ref,
    sem,
):
    small = fetch([(base_hbm, base_ref), (mode_hbm, mode_ref), (node_hbm, node_ref)], sem)
    ends = (slice(0, 8), slice(ROWS - 8, ROWS))
    large = fetch(
        [
            (source.at[..., end, :], target.at[k])
            for source, target in (
                (e_hbm, e_ref),
                (h_hbm, h_ref),
                (material_hbm, material_ref),
                (pattern_hbm, pattern_ref),
            )
            for k, end in enumerate(ends)
        ],
        sem,
        3,
    )
    even = is_even("gx")
    arrived(small)
    table = coef_table(base_ref, mode_ref, node_ref)
    table_ref[...] = table
    arrived(large)
    for n in range(13):
        for quad in range(NZ // 4):
            blocks = []
            for k in range(2):
                pieces = []
                for z in range(4 * quad, 4 * quad + 4):
                    if n == 12:
                        values = look_up(table, material_ref[k, z] * 16 + pattern_ref[k, z])
                    else:
                        ref = e_ref if n < 6 else h_ref
                        values = ref[k, (n % 6) // 3, n % 3, z]
                    pieces.append(values[6 * k : 6 * k + 2])
                blocks.append(jnp.concatenate(pieces, axis=0))
            first_swap_ref[4 * n + quad] = jnp.where(even, blocks[1], blocks[0])
            second_swap_ref[4 * n + quad] = jnp.where(even, blocks[0], blocks[1])


def messages(own_ref, rows, first_swap_ref, second_swap_ref):
    even = is_even("gy")
    place = lanes_of((rows.stop - rows.start, COLS)) % 8
    for c in range(4):
        if c == 3:
            right = left = own_ref[12, rows, :]
        else:
            e_re, e_im, h_re, h_im = (own_ref[3 * k + c, rows, :] for k in range(4))
            right = jnp.where(
                place < 4,
                jnp.where(place < 2, roll(h_re, -4, 1), roll(h_im, -2, 1)),
                jnp.where(place < 6, e_re, roll(e_im, 2, 1)),
            )
            left = jnp.where(
                place < 4,
                jnp.where(place < 2, roll(h_im, -6, 1), roll(h_re, -4, 1)),
                jnp.where(place < 6, roll(e_im, -2, 1), e_re),
            )
        first_swap_ref[c, rows, :] = jnp.where(even, right, left)
        second_swap_ref[c, rows, :] = jnp.where(even, left, right)


def own_kernel(
    e_hbm,
    h_hbm,
    material_hbm,
    pattern_hbm,
    table_hbm,
    own_ref,
    first_swap_ref,
    second_swap_ref,
    coef_ref,
    e_ref,
    h_ref,
    material_ref,
    pattern_ref,
    table_ref,
    sem,
):
    small = fetch(
        [(material_hbm, material_ref), (pattern_hbm, pattern_ref), (table_hbm, table_ref)], sem
    )
    large = fetch([(e_hbm, e_ref), (h_hbm, h_ref)], sem, 3)
    arrived(small)
    table = table_ref[...]
    for z in range(NZ):
        coef_ref[z] = look_up(table, material_ref[z] * 16 + pattern_ref[z])
    arrived(large)
    group = lanes_of((ROWS, COLS)) // 8
    for n in range(13):
        packed = jnp.zeros((ROWS, COLS), jnp.float32)
        for z in range(NZ):
            values = coef_ref[z] if n == 12 else plane_of(e_ref, h_ref, n, z)
            packed = jnp.where(group == z, roll(values, 8 * z + 6, 1), packed)
        own_ref[n] = packed
    messages(own_ref, slice(0, ROWS), first_swap_ref, second_swap_ref)


def bloch_factors(theta_x, theta_y):
    count_x, count_y = lax.axis_size("gx"), lax.axis_size("gy")
    index_x, index_y = lax.axis_index("gx"), lax.axis_index("gy")
    row = lax.broadcasted_iota(jnp.int32, (8, COLS), 0)
    angle = jnp.where(row < 4, theta_x, theta_y)
    flags = [
        jnp.where(flag, 1, 0)
        for flag in (index_x == count_x - 1, index_x == 0, index_y == 0, index_y == count_y - 1)
    ]
    here = jnp.where(
        row < 4,
        jnp.where(row < 2, flags[0], flags[1]),
        jnp.where(row < 6, flags[2], flags[3]),
    )
    angle = jnp.where(here == 1, angle, 0.0)
    angle = jnp.where(row // 2 == 1, -angle, jnp.where(row // 2 == 2, -angle, angle))
    return jnp.where(row % 2 == 0, jnp.cos(angle), jnp.sin(angle))


def pack_kernel(
    own_hbm,
    main_a_hbm,
    main_b_hbm,
    rows_b_hbm,
    rows_a_hbm,
    phase_hbm,
    all_ref,
    first_swap_ref,
    second_swap_ref,
    rot_ref,
    next_ref,
    prev_ref,
    phase_ref,
    sem,
):
    small = fetch([(phase_hbm, phase_ref)], sem)
    copies = fetch_swapped((rows_a_hbm, rows_b_hbm), next_ref, prev_ref, is_even("gx"), sem, 1)
    mains = fetch(
        [
            (own_hbm, all_ref.at[:, 0:ROWS]),
            (main_a_hbm, first_swap_ref.at[:, 0:ROWS]),
            (main_b_hbm, second_swap_ref.at[:, 0:ROWS]),
        ],
        sem,
        3,
    )
    arrived(small)
    rot_ref[...] = bloch_factors(phase_ref[0], phase_ref[1])
    arrived(copies)
    rot = [rot_ref[k : k + 1, :] for k in range(8)]
    group = lanes_of((2, COLS)) // 8
    row = lax.broadcasted_iota(jnp.int32, (8, COLS), 0)
    lane = lanes_of((8, COLS))
    group = (lane + COLS + 2 - 4 * (row % 2)) % COLS // 8

    def packed(blocks):
        total = jnp.zeros((8, COLS), jnp.float32)
        for quad, values in enumerate(blocks):
            moved = pltpu.roll(values, 32 * quad, 1, stride=4, stride_axis=0)
            total = jnp.where(group == 4 * quad + row // 2, moved, total)
        total = jnp.where(row % 2 == 1, roll(total, 2, 1), roll(total, 6, 1))
        total = total + roll(total, 2, 0)
        return total + roll(total, 4, 0)

    quads = range(NZ // 4)
    for n in (0, 1, 2, 6, 7, 8, 12):
        parts = 1 if n == 12 else 2
        sides = []
        for ref, cos, sin in ((next_ref, rot[0], rot[1]), (prev_ref, rot[2], rot[3])):
            found = [packed([ref[4 * (n + 3 * part) + quad] for quad in quads]) for part in range(parts)]
            sides.append(turned(found[0], found[1], cos, sin) if parts == 2 else found)
        for part in range(parts):
            all_ref[n + 3 * part, ROWS:EXT, :] = jnp.where(
                row < 2, sides[0][part], jnp.where(row < 6, 0.0, sides[1][part])
            )
    messages(all_ref, slice(ROWS, EXT), first_swap_ref, second_swap_ref)
    arrived(mains)


def turned(re, im, cos, sin):
    return re * cos - im * sin, im * cos + re * sin


def strip_of(own, right, left, rot):
    place = lanes_of(own[0].shape) % 8

    def joined(index, from_right, from_left):
        return jnp.where(
            place < 4,
            jnp.where(place < 2, roll(own[index], -4, 1), from_left),
            jnp.where(place < 6, from_right, own[index]),
        )

    strip = [None] * 13
    for c in range(3):
        r = right[c]
        l = left[c]
        e_right = turned(r, roll(r, -2, 1), rot[4], rot[5])
        h_right = turned(roll(r, 4, 1), roll(r, 2, 1), rot[4], rot[5])
        e_left = turned(roll(l, -4, 1), roll(l, -2, 1), rot[6], rot[7])
        h_left = turned(l, roll(l, 2, 1), rot[6], rot[7])
        for part in range(2):
            strip[3 * part + c] = joined(3 * part + c, e_right[part], e_left[part])
            strip[6 + 3 * part + c] = joined(6 + 3 * part + c, h_right[part], h_left[part])
    strip[12] = joined(12, right[3], roll(left[3], -4, 1))
    return strip


def next_row(values):
    return roll(values, -1, 0)


def prev_row(values):
    return roll(values, 1, 0)


def h_new(h, e, e_up, e_xn, e_yn):
    return (
        h[0] - STEP_DT * (e_yn[1] - e[2] - (e_up[1] - e[1])),
        h[1] - STEP_DT * (e_up[0] - e[0] - (e_xn[1] - e[2])),
        h[2] - STEP_DT * (e_xn[0] - e[1] - (e_yn[0] - e[0])),
    )


def e_new(e, h, h_down, h_xp, h_yp, coef):
    return (
        e[0] + coef * (h[2] - h_yp[1] - (h[1] - h_down[1])),
        e[1] + coef * (h[0] - h_down[0] - (h[2] - h_xp[1])),
        e[2] + coef * (h[1] - h_xp[0] - (h[0] - h_yp[0])),
    )


def strip_h(h, e):
    up = lanes_of((EXT, COLS)) < 8 * (NZ - 1)
    above = [jnp.where(up, roll(e[c], -8, 1), 0.0) for c in range(2)]
    return h_new(
        h,
        e,
        above,
        (next_row(e[1]), next_row(e[2])),
        (roll(e[0], -1, 1), roll(e[2], -1, 1)),
    )


def strip_e(e, h, coef):
    up = lanes_of((EXT, COLS)) >= 8
    below = [jnp.where(up, roll(h[c], 8, 1), 0.0) for c in range(2)]
    return e_new(
        e,
        h,
        below,
        (prev_row(h[1]), prev_row(h[2])),
        (roll(h[0], 1, 1), roll(h[2], 1, 1)),
        coef,
    )


def feet_kernel(
    rows_b_hbm, rows_a_hbm, rot_hbm, e_ref, h_ref, coef_ref, next_ref, prev_ref, rot_ref, sem
):
    copies = fetch([(rot_hbm, rot_ref)], sem)
    copies += fetch_swapped((rows_a_hbm, rows_b_hbm), next_ref, prev_ref, is_even("gx"), sem, 1)
    arrived(copies)
    rot = [rot_ref[k : k + 1, :] for k in range(8)]
    row = lax.broadcasted_iota(jnp.int32, (8, COLS), 0)

    def foot(ahead, behind, k):
        return jnp.where(
            row < 2,
            roll(ahead, -2 * k, 0),
            jnp.where(row < 6, 0.0, roll(behind, 6 - 2 * k, 0)),
        )

    for quad in range(NZ // 4):
        for field, target in ((0, e_ref), (1, h_ref)):
            for c in range(3):
                n = (6 * field + c) * 4 + quad
                m = n + 12
                ahead = turned(next_ref[n], next_ref[m], rot[0], rot[1])
                behind = turned(prev_ref[n], prev_ref[m], rot[2], rot[3])
                for part in range(2):
                    for k in range(4):
                        target[part, c, 4 * quad + k] = foot(ahead[part], behind[part], k)
        for k in range(4):
            coef_ref[4 * quad + k] = foot(next_ref[48 + quad], prev_ref[48 + quad], k)


def fetch_edges(own_hbm, cols_hbm, rot_hbm, edges, sem, first):
    own_ref, right_ref, left_ref, rot_ref = edges
    copies = fetch([(own_hbm, own_ref), (rot_hbm, rot_ref)], sem, first)
    copies += fetch_swapped(cols_hbm, left_ref, right_ref, is_even("gy"), sem, first + 2)
    return copies


def edge_scratch():
    return [
        VMEM(shape, jnp.float32)
        for shape in (
            (13, EXT, COLS),
            (4, EXT, COLS),
            (4, EXT, COLS),
            (8, COLS),
        )
    ]


def block_scratch(parts):
    return [
        VMEM((parts, 3, NZ + 1, EXT, COLS), jnp.float32),
        VMEM((parts, 3, NZ + 1, EXT, COLS), jnp.float32),
        VMEM((NZ, EXT, COLS), jnp.float32),
        VMEM((parts, 4, 2, EXT, COLS), jnp.float32),
    ]


def fill_edges(edges, block, parts):
    own_ref, right_ref, left_ref, rot_ref = edges
    e_all, h_all, coef_all, edge_ref = block
    rot = [rot_ref[k : k + 1, :] for k in range(8)]
    for at in range(len(parts)):
        for c in range(3):
            e_all[at, c, NZ] = jnp.zeros((EXT, COLS), jnp.float32)
            h_all[at, c, 0] = jnp.zeros((EXT, COLS), jnp.float32)
    strip = strip_of(
        [own_ref[a] for a in range(13)],
        [right_ref[a] for a in range(4)],
        [left_ref[a] for a in range(4)],
        rot,
    )
    for at, part in enumerate(parts):
        e = tuple(strip[3 * part + c] for c in range(3))
        h = tuple(strip[6 + 3 * part + c] for c in range(3))
        for step in range(2):
            edge_ref[at, 2 * step, 0] = e[0]
            edge_ref[at, 2 * step, 1] = e[2]
            h = strip_h(h, e)
            edge_ref[at, 2 * step + 1, 0] = h[0]
            edge_ref[at, 2 * step + 1, 1] = h[2]
            if step == 0:
                e = strip_e(e, h, strip[12])


def beside(edge, values, z, ahead):
    shift = COLS + (125 if ahead else 123) - 8 * z
    shift = shift % COLS if isinstance(z, int) else lax.rem(shift, COLS)
    lane = lanes_of(values.shape)
    if ahead:
        return jnp.where(lane == COLS - 1, roll(edge, shift, 1), roll(values, -1, 1))
    return jnp.where(lane == 0, roll(edge, shift, 1), roll(values, 1, 1))


def updates(block, parts):
    e_all, h_all, coef_all, edge_ref = block

    def do_h(step, layers):
        new = []
        for at in range(parts):
            for z in layers:
                e = tuple(e_all[at, c, z] for c in range(3))
                h = tuple(h_all[at, c, z + 1] for c in range(3))
                e_up = (e_all[at, 0, z + 1], e_all[at, 1, z + 1])
                e_yn = (
                    beside(edge_ref[at, 2 * step, 0], e[0], z, True),
                    beside(edge_ref[at, 2 * step, 1], e[2], z, True),
                )
                values = h_new(h, e, e_up, (next_row(e[1]), next_row(e[2])), e_yn)
                new.append((at, z, values))
        for at, z, values in new:
            for c in range(3):
                h_all[at, c, z + 1] = values[c]

    def do_e(step, layers):
        new = []
        for at in range(parts):
            for z in layers:
                e = tuple(e_all[at, c, z] for c in range(3))
                h = tuple(h_all[at, c, z + 1] for c in range(3))
                h_down = (h_all[at, 0, z], h_all[at, 1, z])
                h_yp = (
                    beside(edge_ref[at, 2 * step + 1, 0], h[0], z, False),
                    beside(edge_ref[at, 2 * step + 1, 1], h[2], z, False),
                )
                values = e_new(
                    e, h, h_down, (prev_row(h[1]), prev_row(h[2])), h_yp, coef_all[z]
                )
                new.append((at, z, values))
        for at, z, values in new:
            for c in range(3):
                e_all[at, c, z] = values[c]

    return do_h, do_e


def plane_kernel(
    e_hbm,
    h_hbm,
    coef_hbm,
    e_foot_hbm,
    h_foot_hbm,
    coef_foot_hbm,
    own_hbm,
    cols_b_hbm,
    cols_a_hbm,
    rot_hbm,
    wave_hbm,
    monitor_ref,
    spread_ref,
    *scratch,
):
    edges, block = scratch[0:4], scratch[4:8]
    wave_ref, sem = scratch[8:10]
    e_all, h_all, coef_all, edge_ref = block
    copies = fetch_edges(own_hbm, (cols_a_hbm, cols_b_hbm), rot_hbm, edges, sem, 0)
    level = monitor_ref[0]
    low = jnp.clip(level - 2, 0, NZ - 5)
    here, there = pl.ds(low, 5), pl.ds(low + 1, 5)
    large = fetch(
        [
            (e_hbm.at[:, :, here], e_all.at[:, :, here, 0:ROWS, :]),
            (h_hbm.at[:, :, here], h_all.at[:, :, there, 0:ROWS, :]),
            (coef_hbm.at[here], coef_all.at[here, 0:ROWS, :]),
            (e_foot_hbm.at[:, :, here], e_all.at[:, :, here, ROWS:EXT, :]),
            (h_foot_hbm.at[:, :, here], h_all.at[:, :, there, ROWS:EXT, :]),
            (coef_foot_hbm.at[here], coef_all.at[here, ROWS:EXT, :]),
            (wave_hbm, wave_ref),
        ],
        sem,
        4,
    )
    arrived(copies)
    fill_edges(edges, block, (0, 1))
    arrived(large)
    near = {}
    for k in range(-2, 3):
        z = jnp.clip(level + k, 0, NZ - 1)
        for part in range(2):
            for c in range(3):
                if c < 2 or k < 2:
                    e = e_all[part, c, z]
                    near["e", part, c, k] = jnp.where(level + k < NZ, e, 0.0) if k > 0 else e
                if k < 2 and (c < 2 or k > -2):
                    h = h_all[part, c, z + 1]
                    near["h", part, c, k] = jnp.where(level + k >= 0, h, 0.0) if k < 0 else h
    def update_h(step, part, k, wanted):
        z = jnp.clip(level + k, 0, NZ - 1)
        ex, ey, ez = (near["e", part, c, k] for c in range(3))
        edge = edge_ref.at[part, 2 * step]
        new = {}
        if 0 in wanted:
            new[0] = beside(edge[1], ez, z, True) - ez - (near["e", part, 1, k + 1] - ey)
        if 1 in wanted:
            new[1] = near["e", part, 0, k + 1] - ex - (next_row(ez) - ez)
        if 2 in wanted:
            new[2] = next_row(ey) - ey - (beside(edge[0], ex, z, True) - ex)
        for c, curl in new.items():
            values = near["h", part, c, k] - STEP_DT * curl
            near["h", part, c, k] = jnp.where(level + k >= 0, values, 0.0) if k < 0 else values

    def update_e(step, part, k, wanted):
        z = jnp.clip(level + k, 0, NZ - 1)
        hx, hy, hz = (near["h", part, c, k] for c in range(3))
        edge = edge_ref.at[part, 2 * step + 1]
        coef = coef_all[z]
        new = {}
        if 0 in wanted:
            new[0] = hz - beside(edge[1], hz, z, False) - (hy - near["h", part, 1, k - 1])
        if 1 in wanted:
            new[1] = hx - near["h", part, 0, k - 1] - (hz - prev_row(hz))
        if 2 in wanted:
            new[2] = hy - prev_row(hy) - (hx - beside(edge[0], hx, z, False))
        for c, curl in new.items():
            values = near["e", part, c, k] + coef * curl
            near["e", part, c, k] = jnp.where(level + k < NZ, values, 0.0) if k > 0 else values

    for part in range(2):
        for k in range(-2, 2):
            update_h(0, part, k, (0, 1, 2) if k > -2 else (0, 1))
        for k in range(-1, 2):
            update_e(0, part, k, (0, 1, 2) if k < 1 else (0, 1))
        update_h(1, part, -1, (0, 1))
        update_h(1, part, 0, (0, 1, 2))
        update_e(1, part, 0, (0, 1))
    re, im = (
        jnp.concatenate([near["e", part, c, 0][0:ROWS] for c in range(2)], axis=0)
        for part in range(2)
    )
    y_section(re, im, wave_ref, spread_ref)


def field_kernel(parts, inputs, *refs):
    (
        e_hbm,
        h_hbm,
        coef_hbm,
        e_foot_hbm,
        h_foot_hbm,
        coef_foot_hbm,
        own_hbm,
        cols_b_hbm,
        cols_a_hbm,
        rot_hbm,
    ) = refs[0:10]
    e_out, h_out, token_ref = refs[inputs : inputs + 3]
    token_ref[...] = jnp.zeros_like(token_ref)
    scratch = refs[inputs + 3 :]
    edges, block, sem = scratch[0:4], scratch[4:8], scratch[8]
    e_all, h_all, coef_all, _ = block
    copies = fetch_edges(own_hbm, (cols_a_hbm, cols_b_hbm), rot_hbm, edges, sem, 0)
    some = slice(parts[0], parts[-1] + 1)
    quads = range(NZ // 4)
    loads = []
    for quad in quads:
        here, there = pl.ds(4 * quad, 4), pl.ds(4 * quad + 1, 4)
        loads.append(
            fetch(
                [
                    (e_hbm.at[some, :, here], e_all.at[:, :, here, 0:ROWS, :]),
                    (e_foot_hbm.at[some, :, here], e_all.at[:, :, here, ROWS:EXT, :]),
                    (h_hbm.at[some, :, here], h_all.at[:, :, there, 0:ROWS, :]),
                    (h_foot_hbm.at[some, :, here], h_all.at[:, :, there, ROWS:EXT, :]),
                    (coef_hbm.at[here], coef_all.at[here, 0:ROWS, :]),
                    (coef_foot_hbm.at[here], coef_all.at[here, ROWS:EXT, :]),
                ],
                sem,
                6 + 6 * quad,
            )
        )
    arrived(copies)
    fill_edges(edges, block, parts)
    do_h, do_e = updates(block, len(parts))

    def finish(quad):
        layers = [4 * quad + k for k in range(4)]
        here, there = pl.ds(4 * quad, 4), pl.ds(4 * quad + 1, 4)
        do_h(1, layers)
        fetch([(h_all.at[:, :, there, 0:ROWS, :], h_out.at[some, :, here])], sem, 4)
        do_e(1, layers)
        fetch([(e_all.at[:, :, here, 0:ROWS, :], e_out.at[some, :, here])], sem, 5)

    arrived(loads[0])
    for quad in quads:
        if quad + 1 < len(quads):
            arrived(loads[quad + 1])
        layers = [4 * quad + k for k in range(4)]
        do_h(0, layers)
        do_e(0, layers)
        if quad > 0:
            finish(quad - 1)
    finish(quads[-1])
    stored = (
        (h_all.at[:, :, 1 : NZ + 1, 0:ROWS, :], h_out.at[some]),
        (e_all.at[:, :, 0:NZ, 0:ROWS, :], e_out.at[some]),
    )
    for k, (source, target) in enumerate(stored):
        pltpu.make_async_copy(source, target, sem.at[4 + k]).wait()


def y_section(re, im, wave_ref, spread_ref):
    wave = wave_ref[...]
    _, owners, _, lanes = spread_ref.shape
    each = lanes // 4
    out = [
        jnp.dot(
            jnp.concatenate(pair, axis=1),
            wave,
            precision=lax.Precision.HIGHEST,
            preferred_element_type=jnp.float32,
        )
        for pair in ((re, im), (im, -re))
    ]
    for owner in range(owners):
        pieces = [
            out[part][c * ROWS : (c + 1) * ROWS, owner * each : (owner + 1) * each]
            for part in range(2)
            for c in range(2)
        ]
        joined = jnp.concatenate(pieces, axis=1)
        for half in range(2):
            spread_ref[half, owner] = joined


def x_kernel(got_ref, wave_ref, after_hbm, part_ref):
    each = got_ref.shape[0] // 2
    totals = []
    for half in range(2):
        total = got_ref[half * each]
        for source in range(1, each):
            total = total + got_ref[half * each + source]
        totals.append(total)
    total = jnp.concatenate(totals, axis=0)
    half = total.shape[1] // 2
    other = roll(total, half, 1)
    other = jnp.where(lanes_of(other.shape) < half, other, -other)
    result = jnp.dot(
        wave_ref[...],
        jnp.concatenate([total, other], axis=0),
        precision=lax.Precision.HIGHEST,
        preferred_element_type=jnp.float32,
    )
    part_ref[...] = result.reshape(part_ref.shape)


def groups(mesh_shape):
    count_x, count_y = mesh_shape
    rest = count_x // 2
    near = [
        [(half * rest + r) * count_y + y for half in range(2) for y in range(count_y)]
        for r in range(rest)
    ]
    far = [
        [(half * rest + r) * count_y + y for r in range(rest)]
        for half in range(2)
        for y in range(count_y)
    ]
    return near, far


def sum_kernel(got_ref, out_ref):
    total = got_ref[0]
    for source in range(1, got_ref.shape[0]):
        total = total + got_ref[source]
    each = total.shape[1] // 4
    for c in range(2):
        for part in range(2):
            start = (2 * part + c) * each
            out_ref[c, part] = total[:, start : start + each]


def table_kernel(
    count_x, count_y, phase_hbm, after_hbm, y_ref, x_ref, phase_ref, sem
):
    arrived(fetch([(phase_hbm, phase_ref)], sem))
    index_x, index_y = lax.axis_index("gx"), lax.axis_index("gy")
    theta_x, theta_y = phase_ref[0], phase_ref[1]
    total_x, total_y = ROWS * count_x, COLS * count_y

    def waves(product, place, total, theta):
        angle = (
            2.0 * math.pi * (product & (total - 1)).astype(jnp.float32)
            + theta * place.astype(jnp.float32)
        ) / total
        return jnp.cos(angle), jnp.sin(angle)

    def joined(a, b):
        return a[0] * b[0] - a[1] * b[1], a[1] * b[0] + a[0] * b[1]

    scale = 1.0 / math.sqrt(total_x * total_y)
    blocks = COLS // 8
    start = index_y * COLS
    order = lax.broadcasted_iota(jnp.int32, (blocks, ORD_Y), 1) - ORD_Y // 2
    place = start + 8 * lax.broadcasted_iota(jnp.int32, (blocks, ORD_Y), 0)
    coarse = waves(order * place, place, total_y, theta_y)
    place = lax.broadcasted_iota(jnp.int32, (8, ORD_Y), 0)
    fine = waves(order[0:8] * place, place, total_y, theta_y)
    fine = (fine[0] * scale, fine[1] * scale)
    for block in range(blocks):
        part = tuple(values[block : block + 1] for values in coarse)
        cos, sin = joined(part, fine)
        y_ref[8 * block : 8 * block + 8, :] = cos
        y_ref[COLS + 8 * block : COLS + 8 * block + 8, :] = sin
    blocks = ORD_X // 16
    shape = (blocks, 4 * ROWS)
    rest = count_x // 2
    lane = lax.broadcasted_iota(jnp.int32, shape, 1)
    block_x = lax.rem(index_x, rest) + rest * (lane // ROWS % 2)
    place = block_x * ROWS + lane % ROWS
    own_half = index_x // rest * (ORD_X // 2)
    order = 8 * lax.broadcasted_iota(jnp.int32, shape, 0) + own_half - ORD_X // 2
    coarse = waves(order * place, place, total_x, theta_x)
    order = lax.broadcasted_iota(jnp.int32, (8, 4 * ROWS), 0)
    fine = waves(order * place[0:8], place[0:8], total_x, 0.0)
    for block in range(blocks):
        part = tuple(values[block : block + 1] for values in coarse)
        cos, sin = joined(part, fine)
        x_ref[8 * block : 8 * block + 8, :] = jnp.where(lane[0:8] < 2 * ROWS, cos, sin)


def params(mebibytes):
    return pltpu.CompilerParams(vmem_limit_bytes=mebibytes << 20)


def cost(microseconds):
    return pl.CostEstimate(
        flops=0, bytes_accessed=microseconds * 3_000_000, transcendentals=0
    )


def f32(*shape):
    return jax.ShapeDtypeStruct(shape, jnp.float32)


def shards(
    e_field, h_field, material, pattern, base_eps, mode_table, nodes, bloch_phase, monitor_z
):
    count_x = lax.axis_size("gx")
    count_y = lax.axis_size("gy")
    each_p = ORD_X // count_x
    each_q = ORD_Y // count_y
    vmem = pl.BlockSpec(memory_space=VMEM)
    hbm = pl.BlockSpec(memory_space=pltpu.HBM)
    f32_vmem = lambda *shape: VMEM(shape, jnp.float32)
    dma = pltpu.SemaphoreType.DMA

    table, rows_a, rows_b = pl.pallas_call(
        rows_kernel,
        out_shape=(
            f32(8, COLS),
            f32(MAIN_BLOCKS, 8, COLS),
            f32(MAIN_BLOCKS, 8, COLS),
        ),
        in_specs=[hbm] * 7,
        out_specs=(vmem,) * 3,
        scratch_shapes=[
            f32_vmem(2, 2, 3, NZ, 8, COLS),
            f32_vmem(2, 2, 3, NZ, 8, COLS),
            VMEM((2, NZ, 8, COLS), jnp.int32),
            VMEM((2, NZ, 8, COLS), jnp.int32),
            SMEM(base_eps.shape, jnp.float32),
            SMEM(mode_table.shape, jnp.float32),
            SMEM(nodes.shape, jnp.float32),
            dma((11,)),
        ],
        compiler_params=params(64),
        cost_estimate=cost(3),
        name="rows",
    )(e_field, h_field, material, pattern, base_eps, mode_table, nodes)
    rows_b = swapped(rows_b, "gx", False)
    rows_a = swapped(rows_a, "gx", True)
    own, cols_a, cols_b, coef = pl.pallas_call(
        own_kernel,
        out_shape=(
            f32(13, ROWS, COLS),
            f32(4, ROWS, COLS),
            f32(4, ROWS, COLS),
            f32(NZ, ROWS, COLS),
        ),
        in_specs=[hbm] * 5,
        out_specs=(vmem,) * 4,
        scratch_shapes=[
            f32_vmem(*e_field.shape),
            f32_vmem(*h_field.shape),
            VMEM(material.shape, jnp.int32),
            VMEM(pattern.shape, jnp.int32),
            f32_vmem(8, COLS),
            dma((5,)),
        ],
        compiler_params=params(64),
        cost_estimate=cost(4),
        name="own",
    )(e_field, h_field, material, pattern, table)
    own, cols_a, cols_b, rot = pl.pallas_call(
        pack_kernel,
        out_shape=(
            f32(13, EXT, COLS),
            f32(4, EXT, COLS),
            f32(4, EXT, COLS),
            f32(8, COLS),
        ),
        in_specs=[hbm] * 6,
        out_specs=(vmem,) * 4,
        scratch_shapes=[
            f32_vmem(MAIN_BLOCKS, 8, COLS),
            f32_vmem(MAIN_BLOCKS, 8, COLS),
            SMEM((2,), jnp.float32),
            dma((6,)),
        ],
        compiler_params=params(64),
        cost_estimate=cost(2),
        name="pack",
    )(own, cols_a, cols_b, rows_b, rows_a, bloch_phase)
    y_wave, x_wave = pl.pallas_call(
        functools.partial(table_kernel, count_x, count_y),
        out_shape=(f32(2 * COLS, ORD_Y), f32(ORD_X // 2, 4 * ROWS)),
        in_specs=[hbm, hbm],
        out_specs=(vmem,) * 2,
        scratch_shapes=[SMEM((2,), jnp.float32), dma((1,))],
        compiler_params=params(64),
        cost_estimate=cost(2),
        name="tables",
    )(bloch_phase, rot)
    cols_b = swapped(cols_b, "gy", False)
    cols_a = swapped(cols_a, "gy", True)
    feet = pl.pallas_call(
        feet_kernel,
        out_shape=(
            f32(2, 3, NZ, EXT - ROWS, COLS),
            f32(2, 3, NZ, EXT - ROWS, COLS),
            f32(NZ, EXT - ROWS, COLS),
        ),
        in_specs=[hbm] * 3,
        out_specs=(vmem,) * 3,
        scratch_shapes=[
            f32_vmem(MAIN_BLOCKS, 8, COLS),
            f32_vmem(MAIN_BLOCKS, 8, COLS),
            f32_vmem(8, COLS),
            dma((3,)),
        ],
        compiler_params=params(64),
        cost_estimate=cost(2),
        name="feet",
    )(rows_b, rows_a, rot)
    around = (e_field, h_field, coef, *feet, own, cols_b, cols_a, rot)
    spread = pl.pallas_call(
        plane_kernel,
        out_shape=f32(2, count_y, ROWS, 4 * each_q),
        in_specs=[hbm] * 11 + [pl.BlockSpec(memory_space=SMEM)],
        out_specs=vmem,
        scratch_shapes=[
            *edge_scratch(),
            *block_scratch(2),
            f32_vmem(*y_wave.shape),
            dma((11,)),
        ],
        compiler_params=params(60),
        cost_estimate=cost(3),
        name="plane",
    )(*around, y_wave, monitor_z)

    near, far = groups((count_x, count_y))
    both = ("gx", "gy")
    spread = spread.reshape(2 * count_y, ROWS, 4 * each_q)
    got = lax.all_to_all(spread, both, 0, 0, tiled=True, axis_index_groups=near)
    e_out, h_out, token = pl.pallas_call(
        functools.partial(field_kernel, (0, 1), 11),
        out_shape=(f32(*e_field.shape), f32(*h_field.shape), f32(8, COLS)),
        in_specs=[hbm] * 11,
        out_specs=(hbm, hbm, vmem),
        scratch_shapes=[*edge_scratch(), *block_scratch(2), dma((30,))],
        compiler_params=params(60),
        cost_estimate=cost(6),
        name="fields",
    )(*around, spread)
    partial = pl.pallas_call(
        x_kernel,
        out_shape=f32(count_x // 2, each_p, 4 * each_q),
        in_specs=[vmem, vmem, hbm],
        out_specs=vmem,
        compiler_params=params(8),
        cost_estimate=cost(1),
        name="x_section",
    )(got, x_wave, token)
    got = lax.all_to_all(partial, both, 0, 0, tiled=True, axis_index_groups=far)
    orders = pl.pallas_call(
        sum_kernel,
        out_shape=f32(2, 2, each_p, each_q),
        in_specs=[vmem],
        out_specs=vmem,
        compiler_params=params(8),
        cost_estimate=cost(1),
        name="order_sum",
    )(got)
    return e_out, h_out, orders


def solution(mesh):
    grid = P(None, None, None, "gx", "gy")
    cells = P(None, "gx", "gy")
    return jax.shard_map(
        shards,
        mesh=mesh,
        in_specs=(grid, grid, cells, cells, P(), P(), P(), P(), P()),
        out_specs=(grid, grid, P(None, None, "gx", "gy")),
        check_vma=False,
    )
```

```python
import functools
import math

import jax
import jax.numpy as jnp
from jax import lax
from jax.experimental import pallas as pl
from jax.experimental.pallas import tpu as pltpu
from jax.sharding import PartitionSpec as P

STEP_DT = 0.5
ORD_X = 256
ORD_Y = 256
NZ = 16
ROWS = 32
COLS = 128
EXT = 40
MAIN_BLOCKS = 48
VMEM = pltpu.VMEM
SMEM = pltpu.SMEM


def swapped(block, axis, first):
    count = lax.axis_size(axis)
    route = []
    for i in range(count):
        ahead = (i % 2 == 0) == first
        route.append((i, (i + 1) % count if ahead else (i - 1) % count))
    return lax.ppermute(block, axis, route)


def roll(values, shift, axis):
    size = values.shape[axis]
    if isinstance(shift, int):
        shift = shift % size
        if shift == 0:
            return values
    return pltpu.roll(values, shift, axis)


def lanes_of(shape):
    return lax.broadcasted_iota(jnp.int32, shape, len(shape) - 1)


def coef_table(base_ref, mode_ref, node_ref):
    lane = lanes_of((8, 128))
    material = lane // 16
    pattern = lane % 16
    base = jnp.zeros((8, 128), jnp.float32)
    for m in range(8):
        base = jnp.where(material == m, base_ref[m], base)
    change = jnp.zeros((8, 128), jnp.float32)
    for k in range(4):
        mode = jnp.zeros((8, 128), jnp.float32)
        for p in range(16):
            mode = jnp.where(pattern == p, mode_ref[k, p], mode)
        change = change + node_ref[k] * mode
    return STEP_DT / (base * (1.0 + change))


def look_up(table, pair):
    rows = [
        jnp.take_along_axis(table, pair[8 * r : 8 * r + 8], axis=1)
        for r in range(pair.shape[0] // 8)
    ]
    return jnp.concatenate(rows, axis=0)


def fetch(pairs, sem, first=0):
    copies = [
        pltpu.make_async_copy(source, target, sem.at[first + k])
        for k, (source, target) in enumerate(pairs)
    ]
    for copy in copies:
        copy.start()
    return copies


def arrived(copies):
    for copy in copies:
        copy.wait()


def is_even(axis):
    return lax.rem(lax.axis_index(axis), 2) == 0


def fetch_swapped(got, ahead_ref, behind_ref, even, sem, first):
    @pl.when(even)
    def _():
        fetch(((got[0], ahead_ref), (got[1], behind_ref)), sem, first)

    @pl.when(jnp.logical_not(even))
    def _():
        fetch(((got[1], ahead_ref), (got[0], behind_ref)), sem, first)

    return [
        pltpu.make_async_copy(got[k], ref, sem.at[first + k])
        for k, ref in enumerate((ahead_ref, behind_ref))
    ]


def plane_of(e_ref, h_ref, n, z):
    ref = e_ref if n < 6 else h_ref
    return ref[(n % 6) // 3, n % 3, z]


def rows_kernel(
    e_hbm,
    h_hbm,
    material_hbm,
    pattern_hbm,
    base_hbm,
    mode_hbm,
    node_hbm,
    table_ref,
    first_swap_ref,
    second_swap_ref,
    e_ref,
    h_ref,
    material_ref,
    pattern_ref,
    base_ref,
    mode_ref,
    node_ref,
    sem,
):
    small = fetch([(base_hbm, base_ref), (mode_hbm, mode_ref), (node_hbm, node_ref)], sem)
    ends = (slice(0, 8), slice(ROWS - 8, ROWS))
    large = fetch(
        [
            (source.at[..., end, :], target.at[k])
            for source, target in (
                (e_hbm, e_ref),
                (h_hbm, h_ref),
                (material_hbm, material_ref),
                (pattern_hbm, pattern_ref),
            )
            for k, end in enumerate(ends)
        ],
        sem,
        3,
    )
    even = is_even("gx")
    arrived(small)
    table = coef_table(base_ref, mode_ref, node_ref)
    table_ref[...] = table
    row = lax.broadcasted_iota(jnp.int32, (8, COLS), 0)
    for n in range(12):
        if n % 6 == 0:
            arrived(large[0:2] if n == 0 else large[2:])
        for quad in range(NZ // 4):
            blocks = []
            for k in range(2):
                pieces = []
                for z in range(4 * quad, 4 * quad + 4):
                    ref = e_ref if n < 6 else h_ref
                    values = ref[k, (n % 6) // 3, n % 3, z]
                    if n == 6:
                        coef = look_up(table, material_ref[k, z] * 16 + pattern_ref[k, z])
                        coef = roll(coef, -1 if k else 1, 0)
                        values = jnp.where(row == (6 if k else 1), coef, values)
                    pieces.append(values[6 * k : 6 * k + 2])
                blocks.append(jnp.concatenate(pieces, axis=0))
            first_swap_ref[4 * n + quad] = jnp.where(even, blocks[1], blocks[0])
            second_swap_ref[4 * n + quad] = jnp.where(even, blocks[0], blocks[1])


def messages(own_ref, rows, first_swap_ref, second_swap_ref):
    even = is_even("gy")
    place = lanes_of((rows.stop - rows.start, COLS)) % 8
    for c in range(3):
        e_re, e_im, h_re, h_im = (own_ref[3 * k + c] for k in range(4))
        right = jnp.where(
            place < 4,
            jnp.where(place < 2, roll(h_re, -4, 1), roll(h_im, -2, 1)),
            jnp.where(place < 6, e_re, roll(e_im, 2, 1)),
        )
        left = jnp.where(
            place < 4,
            jnp.where(place < 2, roll(h_im, -6, 1), roll(h_re, -4, 1)),
            jnp.where(place < 6, roll(e_im, -2, 1), e_re),
        )
        if c == 1:
            coef = own_ref[12]
            right = jnp.where(place == 0, roll(coef, -5, 1), right)
            left = jnp.where(place == 3, roll(coef, -3, 1), left)
        first_swap_ref[c, rows, :] = jnp.where(even, right, left)
        second_swap_ref[c, rows, :] = jnp.where(even, left, right)


def own_kernel(
    e_hbm,
    h_hbm,
    material_hbm,
    pattern_hbm,
    table_hbm,
    own_ref,
    first_swap_ref,
    second_swap_ref,
    coef_ref,
    e_ref,
    h_ref,
    material_ref,
    pattern_ref,
    table_ref,
    sem,
):
    small = fetch(
        [(material_hbm, material_ref), (pattern_hbm, pattern_ref), (table_hbm, table_ref)], sem
    )
    large = fetch([(e_hbm, e_ref), (h_hbm, h_ref)], sem, 3)
    arrived(small)
    table = table_ref[...]
    for z in range(NZ):
        coef_ref[z] = look_up(table, material_ref[z] * 16 + pattern_ref[z])
    group = lanes_of((ROWS, COLS)) // 8
    for n in range(13):
        if n in (0, 6):
            arrived(large[n // 6 : n // 6 + 1])
        packed = jnp.zeros((ROWS, COLS), jnp.float32)
        for z in range(NZ):
            values = coef_ref[z] if n == 12 else plane_of(e_ref, h_ref, n, z)
            packed = jnp.where(group == z, roll(values, 8 * z + 6, 1), packed)
        own_ref[n] = packed
    messages(own_ref, slice(0, ROWS), first_swap_ref, second_swap_ref)


def bloch_factors(theta_x, theta_y):
    count_x, count_y = lax.axis_size("gx"), lax.axis_size("gy")
    index_x, index_y = lax.axis_index("gx"), lax.axis_index("gy")
    row = lax.broadcasted_iota(jnp.int32, (8, COLS), 0)
    angle = jnp.where(row < 4, theta_x, theta_y)
    flags = [
        jnp.where(flag, 1, 0)
        for flag in (index_x == count_x - 1, index_x == 0, index_y == 0, index_y == count_y - 1)
    ]
    here = jnp.where(
        row < 4,
        jnp.where(row < 2, flags[0], flags[1]),
        jnp.where(row < 6, flags[2], flags[3]),
    )
    angle = jnp.where(here == 1, angle, 0.0)
    angle = jnp.where(row // 2 == 1, -angle, jnp.where(row // 2 == 2, -angle, angle))
    return jnp.where(row % 2 == 0, jnp.cos(angle), jnp.sin(angle))


def pack_kernel(
    main_a_hbm,
    main_b_hbm,
    rows_b_hbm,
    rows_a_hbm,
    phase_hbm,
    tail_ref,
    first_swap_ref,
    second_swap_ref,
    rot_ref,
    next_ref,
    prev_ref,
    phase_ref,
    sem,
):
    small = fetch([(phase_hbm, phase_ref)], sem)
    copies = fetch_swapped((rows_a_hbm, rows_b_hbm), next_ref, prev_ref, is_even("gx"), sem, 1)
    mains = fetch(
        [
            (main_a_hbm, first_swap_ref.at[:, 0:ROWS]),
            (main_b_hbm, second_swap_ref.at[:, 0:ROWS]),
        ],
        sem,
        3,
    )
    arrived(small)
    rot_ref[...] = bloch_factors(phase_ref[0], phase_ref[1])
    arrived(copies)
    rot = [rot_ref[k : k + 1, :] for k in range(8)]
    group = lanes_of((2, COLS)) // 8
    row = lax.broadcasted_iota(jnp.int32, (8, COLS), 0)
    lane = lanes_of((8, COLS))
    group = (lane + COLS + 2 - 4 * (row % 2)) % COLS // 8

    def packed(blocks):
        total = jnp.zeros((8, COLS), jnp.float32)
        for quad, values in enumerate(blocks):
            moved = pltpu.roll(values, 32 * quad, 1, stride=4, stride_axis=0)
            total = jnp.where(group == 4 * quad + row // 2, moved, total)
        total = jnp.where(row % 2 == 1, roll(total, 2, 1), roll(total, 6, 1))
        total = total + roll(total, 2, 0)
        return total + roll(total, 4, 0)

    quads = range(NZ // 4)
    def joined(ahead, behind):
        return jnp.where(row < 2, ahead, jnp.where(row < 6, 0.0, behind))

    for n in (0, 1, 2, 6, 7, 8):
        found = [
            [packed([ref[4 * (n + 3 * part) + quad] for quad in quads]) for part in range(2)]
            for ref in (next_ref, prev_ref)
        ]
        if n == 6:
            tail_ref[12] = joined(roll(found[0][0], -1, 0), roll(found[1][0], 1, 0))
        ahead = turned(*found[0], rot[0], rot[1])
        behind = turned(*found[1], rot[2], rot[3])
        for part in range(2):
            tail_ref[n + 3 * part] = joined(ahead[part], behind[part])
    messages(tail_ref, slice(ROWS, EXT), first_swap_ref, second_swap_ref)
    arrived(mains)


def turned(re, im, cos, sin):
    return re * cos - im * sin, im * cos + re * sin


def strip_of(own, right, left, rot):
    place = lanes_of(own[0].shape) % 8

    def joined(index, from_right, from_left):
        return jnp.where(
            place < 4,
            jnp.where(place < 2, roll(own[index], -4, 1), from_left),
            jnp.where(place < 6, from_right, own[index]),
        )

    strip = [None] * 13
    for c in range(3):
        r = right[c]
        l = left[c]
        e_right = turned(r, roll(r, -2, 1), rot[4], rot[5])
        h_right = turned(roll(r, 4, 1), roll(r, 2, 1), rot[4], rot[5])
        e_left = turned(roll(l, -4, 1), roll(l, -2, 1), rot[6], rot[7])
        h_left = turned(l, roll(l, 2, 1), rot[6], rot[7])
        for part in range(2):
            strip[3 * part + c] = joined(3 * part + c, e_right[part], e_left[part])
            strip[6 + 3 * part + c] = joined(6 + 3 * part + c, h_right[part], h_left[part])
    strip[12] = joined(12, roll(right[1], 5, 1), roll(left[1], -1, 1))
    return strip


def next_row(values):
    return roll(values, -1, 0)


def prev_row(values):
    return roll(values, 1, 0)


def h_new(h, e, e_up, e_xn, e_yn):
    return (
        h[0] - STEP_DT * (e_yn[1] - e[2] - (e_up[1] - e[1])),
        h[1] - STEP_DT * (e_up[0] - e[0] - (e_xn[1] - e[2])),
        h[2] - STEP_DT * (e_xn[0] - e[1] - (e_yn[0] - e[0])),
    )


def e_new(e, h, h_down, h_xp, h_yp, coef):
    return (
        e[0] + coef * (h[2] - h_yp[1] - (h[1] - h_down[1])),
        e[1] + coef * (h[0] - h_down[0] - (h[2] - h_xp[1])),
        e[2] + coef * (h[1] - h_xp[0] - (h[0] - h_yp[0])),
    )


def strip_h(h, e):
    up = lanes_of((EXT, COLS)) < 8 * (NZ - 1)
    above = [jnp.where(up, roll(e[c], -8, 1), 0.0) for c in range(2)]
    return h_new(
        h,
        e,
        above,
        (next_row(e[1]), next_row(e[2])),
        (roll(e[0], -1, 1), roll(e[2], -1, 1)),
    )


def strip_e(e, h, coef):
    up = lanes_of((EXT, COLS)) >= 8
    below = [jnp.where(up, roll(h[c], 8, 1), 0.0) for c in range(2)]
    return e_new(
        e,
        h,
        below,
        (prev_row(h[1]), prev_row(h[2])),
        (roll(h[0], 1, 1), roll(h[2], 1, 1)),
        coef,
    )


def feet_kernel(
    counts,
    rows_b_hbm,
    rows_a_hbm,
    rot_hbm,
    phase_hbm,
    e_ref,
    h_ref,
    coef_ref,
    y_ref,
    x_ref,
    next_ref,
    prev_ref,
    rot_ref,
    phase_ref,
    sem,
):
    copies = fetch([(phase_hbm, phase_ref), (rot_hbm, rot_ref)], sem)
    copies += fetch_swapped((rows_a_hbm, rows_b_hbm), next_ref, prev_ref, is_even("gx"), sem, 2)
    arrived(copies)
    fill_tables(*counts, phase_ref[0], phase_ref[1], y_ref, x_ref)
    rot = [rot_ref[k : k + 1, :] for k in range(8)]
    row = lax.broadcasted_iota(jnp.int32, (8, COLS), 0)

    def foot(ahead, behind, k):
        return jnp.where(
            row < 2,
            roll(ahead, -2 * k, 0),
            jnp.where(row < 6, 0.0, roll(behind, 6 - 2 * k, 0)),
        )

    for quad in range(NZ // 4):
        for field, target in ((0, e_ref), (1, h_ref)):
            for c in range(3):
                n = (6 * field + c) * 4 + quad
                m = n + 12
                ahead = turned(next_ref[n], next_ref[m], rot[0], rot[1])
                behind = turned(prev_ref[n], prev_ref[m], rot[2], rot[3])
                for part in range(2):
                    for k in range(4):
                        target[part, c, 4 * quad + k] = foot(ahead[part], behind[part], k)
        ahead = roll(next_ref[24 + quad], -1, 0)
        behind = roll(prev_ref[24 + quad], 1, 0)
        for k in range(4):
            coef_ref[4 * quad + k] = foot(ahead, behind, k)


def fetch_edges(own_hbm, tail_hbm, cols_hbm, rot_hbm, edges, sem, first):
    own_ref, right_ref, left_ref, rot_ref = edges
    copies = fetch(
        [
            (own_hbm, own_ref.at[:, 0:ROWS]),
            (tail_hbm, own_ref.at[:, ROWS:EXT]),
            (rot_hbm, rot_ref),
        ],
        sem,
        first,
    )
    copies += fetch_swapped(cols_hbm, left_ref, right_ref, is_even("gy"), sem, first + 3)
    return copies


def edge_scratch():
    return [
        VMEM(shape, jnp.float32)
        for shape in (
            (13, EXT, COLS),
            (3, EXT, COLS),
            (3, EXT, COLS),
            (8, COLS),
        )
    ]


def block_scratch(parts):
    return [
        VMEM((parts, 3, NZ + 1, EXT, COLS), jnp.float32),
        VMEM((parts, 3, NZ + 1, EXT, COLS), jnp.float32),
        VMEM((NZ, EXT, COLS), jnp.float32),
        VMEM((parts, 4, 2, EXT, COLS), jnp.float32),
    ]


def fill_edges(edges, block, parts):
    own_ref, right_ref, left_ref, rot_ref = edges
    e_all, h_all, coef_all, edge_ref = block
    rot = [rot_ref[k : k + 1, :] for k in range(8)]
    for at in range(len(parts)):
        for c in range(3):
            e_all[at, c, NZ] = jnp.zeros((EXT, COLS), jnp.float32)
            h_all[at, c, 0] = jnp.zeros((EXT, COLS), jnp.float32)
    strip = strip_of(
        [own_ref[a] for a in range(13)],
        [right_ref[a] for a in range(3)],
        [left_ref[a] for a in range(3)],
        rot,
    )
    for at, part in enumerate(parts):
        e = tuple(strip[3 * part + c] for c in range(3))
        h = tuple(strip[6 + 3 * part + c] for c in range(3))
        for step in range(2):
            edge_ref[at, 2 * step, 0] = e[0]
            edge_ref[at, 2 * step, 1] = e[2]
            h = strip_h(h, e)
            edge_ref[at, 2 * step + 1, 0] = h[0]
            edge_ref[at, 2 * step + 1, 1] = h[2]
            if step == 0:
                e = strip_e(e, h, strip[12])


def beside(edge, values, z, ahead):
    shift = COLS + (125 if ahead else 123) - 8 * z
    shift = shift % COLS if isinstance(z, int) else lax.rem(shift, COLS)
    lane = lanes_of(values.shape)
    if ahead:
        return jnp.where(lane == COLS - 1, roll(edge, shift, 1), roll(values, -1, 1))
    return jnp.where(lane == 0, roll(edge, shift, 1), roll(values, 1, 1))


def updates(block, parts):
    e_all, h_all, coef_all, edge_ref = block

    def do_h(step, layers):
        new = []
        for at in range(parts):
            for z in layers:
                e = tuple(e_all[at, c, z] for c in range(3))
                h = tuple(h_all[at, c, z + 1] for c in range(3))
                e_up = (e_all[at, 0, z + 1], e_all[at, 1, z + 1])
                e_yn = (
                    beside(edge_ref[at, 2 * step, 0], e[0], z, True),
                    beside(edge_ref[at, 2 * step, 1], e[2], z, True),
                )
                values = h_new(h, e, e_up, (next_row(e[1]), next_row(e[2])), e_yn)
                new.append((at, z, values))
        for at, z, values in new:
            for c in range(3):
                h_all[at, c, z + 1] = values[c]

    def do_e(step, layers):
        new = []
        for at in range(parts):
            for z in layers:
                e = tuple(e_all[at, c, z] for c in range(3))
                h = tuple(h_all[at, c, z + 1] for c in range(3))
                h_down = (h_all[at, 0, z], h_all[at, 1, z])
                h_yp = (
                    beside(edge_ref[at, 2 * step + 1, 0], h[0], z, False),
                    beside(edge_ref[at, 2 * step + 1, 1], h[2], z, False),
                )
                values = e_new(
                    e, h, h_down, (prev_row(h[1]), prev_row(h[2])), h_yp, coef_all[z]
                )
                new.append((at, z, values))
        rows = slice(0, EXT if step == 0 else ROWS)
        for at, z, values in new:
            for c in range(3):
                e_all[at, c, z, rows, :] = values[c][rows]

    return do_h, do_e


def plane_kernel(
    e_hbm,
    h_hbm,
    coef_hbm,
    e_foot_hbm,
    h_foot_hbm,
    coef_foot_hbm,
    own_hbm,
    tail_hbm,
    cols_b_hbm,
    cols_a_hbm,
    rot_hbm,
    wave_hbm,
    monitor_ref,
    spread_ref,
    *scratch,
):
    edges, block = scratch[0:4], scratch[4:8]
    wave_ref, sem = scratch[8:10]
    e_all, h_all, coef_all, edge_ref = block
    copies = fetch_edges(own_hbm, tail_hbm, (cols_a_hbm, cols_b_hbm), rot_hbm, edges, sem, 0)
    level = monitor_ref[0]
    low = jnp.clip(level - 2, 0, NZ - 5)
    here, there = pl.ds(low, 5), pl.ds(low + 1, 5)
    large = fetch(
        [
            (e_hbm.at[:, :, here], e_all.at[:, :, here, 0:ROWS, :]),
            (h_hbm.at[:, :, here], h_all.at[:, :, there, 0:ROWS, :]),
            (coef_hbm.at[here], coef_all.at[here, 0:ROWS, :]),
            (e_foot_hbm.at[:, :, here], e_all.at[:, :, here, ROWS:EXT, :]),
            (h_foot_hbm.at[:, :, here], h_all.at[:, :, there, ROWS:EXT, :]),
            (coef_foot_hbm.at[here], coef_all.at[here, ROWS:EXT, :]),
            (wave_hbm, wave_ref),
        ],
        sem,
        5,
    )
    arrived(copies)
    fill_edges(edges, block, (0, 1))
    arrived(large)
    near = {}
    for k in range(-2, 3):
        z = jnp.clip(level + k, 0, NZ - 1)
        for part in range(2):
            for c in range(3):
                if c < 2 or k < 2:
                    e = e_all[part, c, z]
                    near["e", part, c, k] = jnp.where(level + k < NZ, e, 0.0) if k > 0 else e
                if k < 2 and (c < 2 or k > -2):
                    h = h_all[part, c, z + 1]
                    near["h", part, c, k] = jnp.where(level + k >= 0, h, 0.0) if k < 0 else h
    def update_h(step, part, k, wanted):
        z = jnp.clip(level + k, 0, NZ - 1)
        ex, ey, ez = (near["e", part, c, k] for c in range(3))
        edge = edge_ref.at[part, 2 * step]
        new = {}
        if 0 in wanted:
            new[0] = beside(edge[1], ez, z, True) - ez - (near["e", part, 1, k + 1] - ey)
        if 1 in wanted:
            new[1] = near["e", part, 0, k + 1] - ex - (next_row(ez) - ez)
        if 2 in wanted:
            new[2] = next_row(ey) - ey - (beside(edge[0], ex, z, True) - ex)
        for c, curl in new.items():
            values = near["h", part, c, k] - STEP_DT * curl
            near["h", part, c, k] = jnp.where(level + k >= 0, values, 0.0) if k < 0 else values

    def update_e(step, part, k, wanted):
        z = jnp.clip(level + k, 0, NZ - 1)
        hx, hy, hz = (near["h", part, c, k] for c in range(3))
        edge = edge_ref.at[part, 2 * step + 1]
        coef = coef_all[z]
        new = {}
        if 0 in wanted:
            new[0] = hz - beside(edge[1], hz, z, False) - (hy - near["h", part, 1, k - 1])
        if 1 in wanted:
            new[1] = hx - near["h", part, 0, k - 1] - (hz - prev_row(hz))
        if 2 in wanted:
            new[2] = hy - prev_row(hy) - (hx - beside(edge[0], hx, z, False))
        for c, curl in new.items():
            values = near["e", part, c, k] + coef * curl
            near["e", part, c, k] = jnp.where(level + k < NZ, values, 0.0) if k > 0 else values

    for part in range(2):
        for k in range(-2, 2):
            update_h(0, part, k, (0, 1, 2) if k > -2 else (0, 1))
        for k in range(-1, 2):
            update_e(0, part, k, (0, 1, 2) if k < 1 else (0, 1))
        update_h(1, part, -1, (0, 1))
        update_h(1, part, 0, (0, 1, 2))
        update_e(1, part, 0, (0, 1))
    re, im = (
        jnp.concatenate([near["e", part, c, 0][0:ROWS] for c in range(2)], axis=0)
        for part in range(2)
    )
    y_section(re, im, wave_ref, spread_ref)


def field_kernel(parts, inputs, *refs):
    (
        e_hbm,
        h_hbm,
        coef_hbm,
        e_foot_hbm,
        h_foot_hbm,
        coef_foot_hbm,
        own_hbm,
        tail_hbm,
        cols_b_hbm,
        cols_a_hbm,
        rot_hbm,
    ) = refs[0:11]
    e_out, h_out, token_hbm = refs[inputs : inputs + 3]
    scratch = refs[inputs + 3 :]
    edges, block, sem = scratch[0:4], scratch[4:8], scratch[8]
    e_all, h_all, coef_all, _ = block
    copies = fetch_edges(own_hbm, tail_hbm, (cols_a_hbm, cols_b_hbm), rot_hbm, edges, sem, 0)
    some = slice(parts[0], parts[-1] + 1)
    quads = range(NZ // 4)
    loads = []
    for quad in quads:
        here, there = pl.ds(4 * quad, 4), pl.ds(4 * quad + 1, 4)
        loads.append(
            fetch(
                [
                    (e_hbm.at[some, :, here], e_all.at[:, :, here, 0:ROWS, :]),
                    (e_foot_hbm.at[some, :, here], e_all.at[:, :, here, ROWS:EXT, :]),
                    (h_hbm.at[some, :, here], h_all.at[:, :, there, 0:ROWS, :]),
                    (h_foot_hbm.at[some, :, here], h_all.at[:, :, there, ROWS:EXT, :]),
                    (coef_hbm.at[here], coef_all.at[here, 0:ROWS, :]),
                    (coef_foot_hbm.at[here], coef_all.at[here, ROWS:EXT, :]),
                ],
                sem,
                7 + 6 * quad,
            )
        )
    arrived(copies)
    token = fetch([(edges[3], token_hbm)], sem)
    fill_edges(edges, block, parts)
    do_h, do_e = updates(block, len(parts))

    def finish(quad):
        layers = [4 * quad + k for k in range(4)]
        here, there = pl.ds(4 * quad, 4), pl.ds(4 * quad + 1, 4)
        do_h(1, layers)
        fetch([(h_all.at[:, :, there, 0:ROWS, :], h_out.at[some, :, here])], sem, 5)
        do_e(1, layers)
        fetch([(e_all.at[:, :, here, 0:ROWS, :], e_out.at[some, :, here])], sem, 6)

    arrived(loads[0])
    for quad in quads:
        if quad + 1 < len(quads):
            arrived(loads[quad + 1])
        layers = [4 * quad + k for k in range(4)]
        do_h(0, layers)
        do_e(0, layers)
        if quad > 0:
            finish(quad - 1)
    finish(quads[-1])
    arrived(token)
    stored = (
        (h_all.at[:, :, 1 : NZ + 1, 0:ROWS, :], h_out.at[some]),
        (e_all.at[:, :, 0:NZ, 0:ROWS, :], e_out.at[some]),
    )
    for k, (source, target) in enumerate(stored):
        pltpu.make_async_copy(source, target, sem.at[5 + k]).wait()


def y_section(re, im, wave_ref, spread_ref):
    wave = wave_ref[...]
    _, owners, _, lanes = spread_ref.shape
    each = lanes // 4
    out = [
        jnp.dot(
            jnp.concatenate(pair, axis=1),
            wave,
            precision=lax.Precision.HIGHEST,
            preferred_element_type=jnp.float32,
        )
        for pair in ((re, im), (im, -re))
    ]
    for owner in range(owners):
        pieces = [
            out[part][c * ROWS : (c + 1) * ROWS, owner * each : (owner + 1) * each]
            for part in range(2)
            for c in range(2)
        ]
        joined = jnp.concatenate(pieces, axis=1)
        for half in range(2):
            spread_ref[half, owner] = joined


def x_kernel(got_ref, wave_ref, after_hbm, part_ref):
    each = got_ref.shape[0] // 2
    totals = []
    for half in range(2):
        total = got_ref[half * each]
        for source in range(1, each):
            total = total + got_ref[half * each + source]
        totals.append(total)
    total = jnp.concatenate(totals, axis=0)
    half = total.shape[1] // 2
    other = roll(total, half, 1)
    other = jnp.where(lanes_of(other.shape) < half, other, -other)
    result = jnp.dot(
        wave_ref[...],
        jnp.concatenate([total, other], axis=0),
        precision=lax.Precision.HIGHEST,
        preferred_element_type=jnp.float32,
    )
    part_ref[...] = result.reshape(part_ref.shape)


def groups(mesh_shape):
    count_x, count_y = mesh_shape
    rest = count_x // 2
    near = [
        [(half * rest + r) * count_y + y for half in range(2) for y in range(count_y)]
        for r in range(rest)
    ]
    far = [
        [(half * rest + r) * count_y + y for r in range(rest)]
        for half in range(2)
        for y in range(count_y)
    ]
    return near, far


def sum_kernel(got_ref, out_ref):
    total = got_ref[0]
    for source in range(1, got_ref.shape[0]):
        total = total + got_ref[source]
    each = total.shape[1] // 4
    for c in range(2):
        for part in range(2):
            start = (2 * part + c) * each
            out_ref[c, part] = total[:, start : start + each]


def fill_tables(count_x, count_y, theta_x, theta_y, y_ref, x_ref):
    index_x, index_y = lax.axis_index("gx"), lax.axis_index("gy")
    total_x, total_y = ROWS * count_x, COLS * count_y

    def waves(product, place, total, theta):
        angle = (
            2.0 * math.pi * (product & (total - 1)).astype(jnp.float32)
            + theta * place.astype(jnp.float32)
        ) / total
        return jnp.cos(angle), jnp.sin(angle)

    def joined(a, b):
        return a[0] * b[0] - a[1] * b[1], a[1] * b[0] + a[0] * b[1]

    scale = 1.0 / math.sqrt(total_x * total_y)
    blocks = COLS // 8
    start = index_y * COLS
    order = lax.broadcasted_iota(jnp.int32, (blocks, ORD_Y), 1) - ORD_Y // 2
    place = start + 8 * lax.broadcasted_iota(jnp.int32, (blocks, ORD_Y), 0)
    coarse = waves(order * place, place, total_y, theta_y)
    place = lax.broadcasted_iota(jnp.int32, (8, ORD_Y), 0)
    fine = waves(order[0:8] * place, place, total_y, theta_y)
    fine = (fine[0] * scale, fine[1] * scale)
    for block in range(blocks):
        part = tuple(values[block : block + 1] for values in coarse)
        cos, sin = joined(part, fine)
        y_ref[8 * block : 8 * block + 8, :] = cos
        y_ref[COLS + 8 * block : COLS + 8 * block + 8, :] = sin
    blocks = ORD_X // 16
    shape = (blocks, 4 * ROWS)
    rest = count_x // 2
    lane = lax.broadcasted_iota(jnp.int32, shape, 1)
    block_x = lax.rem(index_x, rest) + rest * (lane // ROWS % 2)
    place = block_x * ROWS + lane % ROWS
    own_half = index_x // rest * (ORD_X // 2)
    order = 8 * lax.broadcasted_iota(jnp.int32, shape, 0) + own_half - ORD_X // 2
    coarse = waves(order * place, place, total_x, theta_x)
    order = lax.broadcasted_iota(jnp.int32, (8, 4 * ROWS), 0)
    fine = waves(order * place[0:8], place[0:8], total_x, 0.0)
    for block in range(blocks):
        part = tuple(values[block : block + 1] for values in coarse)
        cos, sin = joined(part, fine)
        x_ref[8 * block : 8 * block + 8, :] = jnp.where(lane[0:8] < 2 * ROWS, cos, sin)


def params(mebibytes):
    return pltpu.CompilerParams(vmem_limit_bytes=mebibytes << 20)


def cost(microseconds):
    return pl.CostEstimate(
        flops=0, bytes_accessed=microseconds * 3_000_000, transcendentals=0
    )


def f32(*shape):
    return jax.ShapeDtypeStruct(shape, jnp.float32)


def shards(
    e_field, h_field, material, pattern, base_eps, mode_table, nodes, bloch_phase, monitor_z
):
    count_x = lax.axis_size("gx")
    count_y = lax.axis_size("gy")
    each_p = ORD_X // count_x
    each_q = ORD_Y // count_y
    vmem = pl.BlockSpec(memory_space=VMEM)
    hbm = pl.BlockSpec(memory_space=pltpu.HBM)
    f32_vmem = lambda *shape: VMEM(shape, jnp.float32)
    dma = pltpu.SemaphoreType.DMA

    table, rows_a, rows_b = pl.pallas_call(
        rows_kernel,
        out_shape=(
            f32(8, COLS),
            f32(MAIN_BLOCKS, 8, COLS),
            f32(MAIN_BLOCKS, 8, COLS),
        ),
        in_specs=[hbm] * 7,
        out_specs=(vmem,) * 3,
        scratch_shapes=[
            f32_vmem(2, 2, 3, NZ, 8, COLS),
            f32_vmem(2, 2, 3, NZ, 8, COLS),
            VMEM((2, NZ, 8, COLS), jnp.int32),
            VMEM((2, NZ, 8, COLS), jnp.int32),
            SMEM(base_eps.shape, jnp.float32),
            SMEM(mode_table.shape, jnp.float32),
            SMEM(nodes.shape, jnp.float32),
            dma((11,)),
        ],
        compiler_params=params(64),
        cost_estimate=cost(3),
        name="rows",
    )(e_field, h_field, material, pattern, base_eps, mode_table, nodes)
    rows_b = swapped(rows_b, "gx", False)
    rows_a = swapped(rows_a, "gx", True)
    own, cols_a, cols_b, coef = pl.pallas_call(
        own_kernel,
        out_shape=(
            f32(13, ROWS, COLS),
            f32(3, ROWS, COLS),
            f32(3, ROWS, COLS),
            f32(NZ, ROWS, COLS),
        ),
        in_specs=[hbm] * 5,
        out_specs=(vmem,) * 4,
        scratch_shapes=[
            f32_vmem(*e_field.shape),
            f32_vmem(*h_field.shape),
            VMEM(material.shape, jnp.int32),
            VMEM(pattern.shape, jnp.int32),
            f32_vmem(8, COLS),
            dma((5,)),
        ],
        compiler_params=params(64),
        cost_estimate=cost(4),
        name="own",
    )(e_field, h_field, material, pattern, table)
    tail, cols_a, cols_b, rot = pl.pallas_call(
        pack_kernel,
        out_shape=(
            f32(13, EXT - ROWS, COLS),
            f32(3, EXT, COLS),
            f32(3, EXT, COLS),
            f32(8, COLS),
        ),
        in_specs=[hbm] * 5,
        out_specs=(vmem,) * 4,
        scratch_shapes=[
            f32_vmem(MAIN_BLOCKS, 8, COLS),
            f32_vmem(MAIN_BLOCKS, 8, COLS),
            SMEM((2,), jnp.float32),
            dma((5,)),
        ],
        compiler_params=params(64),
        cost_estimate=cost(2),
        name="pack",
    )(cols_a, cols_b, rows_b, rows_a, bloch_phase)
    cols_b = swapped(cols_b, "gy", False)
    cols_a = swapped(cols_a, "gy", True)
    *feet, y_wave, x_wave = pl.pallas_call(
        functools.partial(feet_kernel, (count_x, count_y)),
        out_shape=(
            f32(2, 3, NZ, EXT - ROWS, COLS),
            f32(2, 3, NZ, EXT - ROWS, COLS),
            f32(NZ, EXT - ROWS, COLS),
            f32(2 * COLS, ORD_Y),
            f32(ORD_X // 2, 4 * ROWS),
        ),
        in_specs=[hbm] * 4,
        out_specs=(vmem,) * 5,
        scratch_shapes=[
            f32_vmem(MAIN_BLOCKS, 8, COLS),
            f32_vmem(MAIN_BLOCKS, 8, COLS),
            f32_vmem(8, COLS),
            SMEM((2,), jnp.float32),
            dma((4,)),
        ],
        compiler_params=params(64),
        cost_estimate=cost(2),
        name="feet",
    )(rows_b, rows_a, rot, bloch_phase)
    around = (e_field, h_field, coef, *feet, own, tail, cols_b, cols_a, rot)
    spread = pl.pallas_call(
        plane_kernel,
        out_shape=f32(2, count_y, ROWS, 4 * each_q),
        in_specs=[hbm] * 12 + [pl.BlockSpec(memory_space=SMEM)],
        out_specs=vmem,
        scratch_shapes=[
            *edge_scratch(),
            *block_scratch(2),
            f32_vmem(*y_wave.shape),
            dma((12,)),
        ],
        compiler_params=params(60),
        cost_estimate=cost(3),
        name="plane",
    )(*around, y_wave, monitor_z)

    near, far = groups((count_x, count_y))
    both = ("gx", "gy")
    spread = spread.reshape(2 * count_y, ROWS, 4 * each_q)
    got = lax.all_to_all(spread, both, 0, 0, tiled=True, axis_index_groups=near)
    e_out, h_out, token = pl.pallas_call(
        functools.partial(field_kernel, (0, 1), 12),
        out_shape=(f32(*e_field.shape), f32(*h_field.shape), f32(8, COLS)),
        in_specs=[hbm] * 12,
        out_specs=(hbm, hbm, hbm),
        scratch_shapes=[*edge_scratch(), *block_scratch(2), dma((31,))],
        compiler_params=params(60),
        cost_estimate=cost(6),
        name="fields",
    )(*around, spread)
    partial = pl.pallas_call(
        x_kernel,
        out_shape=f32(count_x // 2, each_p, 4 * each_q),
        in_specs=[vmem, vmem, hbm],
        out_specs=vmem,
        compiler_params=params(8),
        cost_estimate=cost(1),
        name="x_section",
    )(got, x_wave, token)
    got = lax.all_to_all(partial, both, 0, 0, tiled=True, axis_index_groups=far)
    orders = pl.pallas_call(
        sum_kernel,
        out_shape=f32(2, 2, each_p, each_q),
        in_specs=[vmem],
        out_specs=vmem,
        compiler_params=params(8),
        cost_estimate=cost(1),
        name="order_sum",
    )(got)
    return e_out, h_out, orders


def solution(mesh):
    grid = P(None, None, None, "gx", "gy")
    cells = P(None, "gx", "gy")
    return jax.shard_map(
        shards,
        mesh=mesh,
        in_specs=(grid, grid, cells, cells, P(), P(), P(), P(), P()),
        out_specs=(grid, grid, P(None, None, "gx", "gy")),
        check_vma=False,
    )
```

```python
import functools
import math

import jax
import jax.numpy as jnp
from jax import lax
from jax.experimental import pallas as pl
from jax.experimental.pallas import tpu as pltpu
from jax.sharding import PartitionSpec as P

STEP_DT = 0.5
ORD_X = 256
ORD_Y = 256
NZ = 16
ROWS = 32
COLS = 128
EXT = 40
MAIN_BLOCKS = 48
VMEM = pltpu.VMEM
SMEM = pltpu.SMEM


def swapped(block, axis, first):
    count = lax.axis_size(axis)
    route = []
    for i in range(count):
        ahead = (i % 2 == 0) == first
        route.append((i, (i + 1) % count if ahead else (i - 1) % count))
    return lax.ppermute(block, axis, route)


def roll(values, shift, axis):
    size = values.shape[axis]
    if isinstance(shift, int):
        shift = shift % size
        if shift == 0:
            return values
    return pltpu.roll(values, shift, axis)


def lanes_of(shape):
    return lax.broadcasted_iota(jnp.int32, shape, len(shape) - 1)


def coef_table(base_ref, mode_ref, node_ref):
    lane = lanes_of((8, 128))
    material = lane // 16
    pattern = lane % 16
    base = jnp.zeros((8, 128), jnp.float32)
    for m in range(8):
        base = jnp.where(material == m, base_ref[m], base)
    change = jnp.zeros((8, 128), jnp.float32)
    for k in range(4):
        mode = jnp.zeros((8, 128), jnp.float32)
        for p in range(16):
            mode = jnp.where(pattern == p, mode_ref[k, p], mode)
        change = change + node_ref[k] * mode
    return STEP_DT / (base * (1.0 + change))


def look_up(table, pair):
    rows = [
        jnp.take_along_axis(table, pair[8 * r : 8 * r + 8], axis=1)
        for r in range(pair.shape[0] // 8)
    ]
    return jnp.concatenate(rows, axis=0)


def fetch(pairs, sem, first=0):
    copies = [
        pltpu.make_async_copy(source, target, sem.at[first + k])
        for k, (source, target) in enumerate(pairs)
    ]
    for copy in copies:
        copy.start()
    return copies


def arrived(copies):
    for copy in copies:
        copy.wait()


def is_even(axis):
    return lax.rem(lax.axis_index(axis), 2) == 0


def fetch_swapped(got, ahead_ref, behind_ref, even, sem, first):
    @pl.when(even)
    def _():
        fetch(((got[0], ahead_ref), (got[1], behind_ref)), sem, first)

    @pl.when(jnp.logical_not(even))
    def _():
        fetch(((got[1], ahead_ref), (got[0], behind_ref)), sem, first)

    return [
        pltpu.make_async_copy(got[k], ref, sem.at[first + k])
        for k, ref in enumerate((ahead_ref, behind_ref))
    ]


def plane_of(e_ref, h_ref, n, z):
    ref = e_ref if n < 6 else h_ref
    return ref[(n % 6) // 3, n % 3, z]


def rows_kernel(
    e_hbm,
    h_hbm,
    material_hbm,
    pattern_hbm,
    base_hbm,
    mode_hbm,
    node_hbm,
    table_ref,
    first_swap_ref,
    second_swap_ref,
    e_ref,
    h_ref,
    material_ref,
    pattern_ref,
    base_ref,
    mode_ref,
    node_ref,
    sem,
):
    small = fetch([(base_hbm, base_ref), (mode_hbm, mode_ref), (node_hbm, node_ref)], sem)
    ends = (slice(0, 8), slice(ROWS - 8, ROWS))
    large = fetch(
        [
            (source.at[..., end, :], target.at[k])
            for source, target in (
                (e_hbm, e_ref),
                (h_hbm, h_ref),
                (material_hbm, material_ref),
                (pattern_hbm, pattern_ref),
            )
            for k, end in enumerate(ends)
        ],
        sem,
        3,
    )
    even = is_even("gx")
    arrived(small)
    table = coef_table(base_ref, mode_ref, node_ref)
    table_ref[...] = table
    row = lax.broadcasted_iota(jnp.int32, (8, COLS), 0)
    for n in range(12):
        if n % 6 == 0:
            arrived(large[0:2] if n == 0 else large[2:])
        for quad in range(NZ // 4):
            blocks = []
            for k in range(2):
                pieces = []
                for z in range(4 * quad, 4 * quad + 4):
                    ref = e_ref if n < 6 else h_ref
                    values = ref[k, (n % 6) // 3, n % 3, z]
                    if n == 6:
                        coef = look_up(table, material_ref[k, z] * 16 + pattern_ref[k, z])
                        coef = roll(coef, -1 if k else 1, 0)
                        values = jnp.where(row == (6 if k else 1), coef, values)
                    pieces.append(values[6 * k : 6 * k + 2])
                blocks.append(jnp.concatenate(pieces, axis=0))
            first_swap_ref[4 * n + quad] = jnp.where(even, blocks[1], blocks[0])
            second_swap_ref[4 * n + quad] = jnp.where(even, blocks[0], blocks[1])


def messages(own_ref, rows, first_swap_ref, second_swap_ref):
    even = is_even("gy")
    place = lanes_of((rows.stop - rows.start, COLS)) % 8
    for c in range(3):
        e_re, e_im, h_re, h_im = (own_ref[3 * k + c] for k in range(4))
        right = jnp.where(
            place < 4,
            jnp.where(place < 2, roll(h_re, -4, 1), roll(h_im, -2, 1)),
            jnp.where(place < 6, e_re, roll(e_im, 2, 1)),
        )
        left = jnp.where(
            place < 4,
            jnp.where(place < 2, roll(h_im, -6, 1), roll(h_re, -4, 1)),
            jnp.where(place < 6, roll(e_im, -2, 1), e_re),
        )
        if c == 1:
            coef = own_ref[12]
            right = jnp.where(place == 0, roll(coef, -5, 1), right)
            left = jnp.where(place == 3, roll(coef, -3, 1), left)
        first_swap_ref[c, rows, :] = jnp.where(even, right, left)
        second_swap_ref[c, rows, :] = jnp.where(even, left, right)


def own_kernel(
    e_hbm,
    h_hbm,
    material_hbm,
    pattern_hbm,
    table_hbm,
    own_ref,
    first_swap_ref,
    second_swap_ref,
    coef_ref,
    e_ref,
    h_ref,
    material_ref,
    pattern_ref,
    table_ref,
    sem,
):
    small = fetch(
        [(material_hbm, material_ref), (pattern_hbm, pattern_ref), (table_hbm, table_ref)], sem
    )
    large = fetch([(e_hbm, e_ref), (h_hbm, h_ref)], sem, 3)
    arrived(small)
    table = table_ref[...]
    for z in range(NZ):
        coef_ref[z] = look_up(table, material_ref[z] * 16 + pattern_ref[z])
    group = lanes_of((ROWS, COLS)) // 8
    for n in range(13):
        if n in (0, 6):
            arrived(large[n // 6 : n // 6 + 1])
        packed = jnp.zeros((ROWS, COLS), jnp.float32)
        for z in range(NZ):
            values = coef_ref[z] if n == 12 else plane_of(e_ref, h_ref, n, z)
            packed = jnp.where(group == z, roll(values, 8 * z + 6, 1), packed)
        own_ref[n] = packed
    messages(own_ref, slice(0, ROWS), first_swap_ref, second_swap_ref)


def bloch_factors(theta_x, theta_y):
    count_x, count_y = lax.axis_size("gx"), lax.axis_size("gy")
    index_x, index_y = lax.axis_index("gx"), lax.axis_index("gy")
    row = lax.broadcasted_iota(jnp.int32, (8, COLS), 0)
    angle = jnp.where(row < 4, theta_x, theta_y)
    flags = [
        jnp.where(flag, 1, 0)
        for flag in (index_x == count_x - 1, index_x == 0, index_y == 0, index_y == count_y - 1)
    ]
    here = jnp.where(
        row < 4,
        jnp.where(row < 2, flags[0], flags[1]),
        jnp.where(row < 6, flags[2], flags[3]),
    )
    angle = jnp.where(here == 1, angle, 0.0)
    angle = jnp.where(row // 2 == 1, -angle, jnp.where(row // 2 == 2, -angle, angle))
    return jnp.where(row % 2 == 0, jnp.cos(angle), jnp.sin(angle))


def pack_kernel(
    main_a_hbm,
    main_b_hbm,
    rows_b_hbm,
    rows_a_hbm,
    phase_hbm,
    tail_ref,
    first_swap_ref,
    second_swap_ref,
    rot_ref,
    next_ref,
    prev_ref,
    phase_ref,
    sem,
):
    small = fetch([(phase_hbm, phase_ref)], sem)
    copies = fetch_swapped((rows_a_hbm, rows_b_hbm), next_ref, prev_ref, is_even("gx"), sem, 1)
    mains = fetch(
        [
            (main_a_hbm, first_swap_ref.at[:, 0:ROWS]),
            (main_b_hbm, second_swap_ref.at[:, 0:ROWS]),
        ],
        sem,
        3,
    )
    arrived(small)
    rot_ref[...] = bloch_factors(phase_ref[0], phase_ref[1])
    arrived(copies)
    rot = [rot_ref[k : k + 1, :] for k in range(8)]
    group = lanes_of((2, COLS)) // 8
    row = lax.broadcasted_iota(jnp.int32, (8, COLS), 0)
    lane = lanes_of((8, COLS))
    group = (lane + COLS + 2 - 4 * (row % 2)) % COLS // 8

    def packed(blocks):
        total = jnp.zeros((8, COLS), jnp.float32)
        for quad, values in enumerate(blocks):
            moved = pltpu.roll(values, 32 * quad, 1, stride=4, stride_axis=0)
            total = jnp.where(group == 4 * quad + row // 2, moved, total)
        total = jnp.where(row % 2 == 1, roll(total, 2, 1), roll(total, 6, 1))
        total = total + roll(total, 2, 0)
        return total + roll(total, 4, 0)

    quads = range(NZ // 4)
    def joined(ahead, behind):
        return jnp.where(row < 2, ahead, jnp.where(row < 6, 0.0, behind))

    for n in (0, 1, 2, 6, 7, 8):
        found = [
            [packed([ref[4 * (n + 3 * part) + quad] for quad in quads]) for part in range(2)]
            for ref in (next_ref, prev_ref)
        ]
        if n == 6:
            tail_ref[12] = joined(roll(found[0][0], -1, 0), roll(found[1][0], 1, 0))
        ahead = turned(*found[0], rot[0], rot[1])
        behind = turned(*found[1], rot[2], rot[3])
        for part in range(2):
            tail_ref[n + 3 * part] = joined(ahead[part], behind[part])
    messages(tail_ref, slice(ROWS, EXT), first_swap_ref, second_swap_ref)
    arrived(mains)


def turned(re, im, cos, sin):
    return re * cos - im * sin, im * cos + re * sin


def strip_of(own, right, left, rot):
    place = lanes_of(own[0].shape) % 8

    def joined(index, from_right, from_left):
        return jnp.where(
            place < 4,
            jnp.where(place < 2, roll(own[index], -4, 1), from_left),
            jnp.where(place < 6, from_right, own[index]),
        )

    strip = [None] * 13
    for c in range(3):
        r = right[c]
        l = left[c]
        e_right = turned(r, roll(r, -2, 1), rot[4], rot[5])
        h_right = turned(roll(r, 4, 1), roll(r, 2, 1), rot[4], rot[5])
        e_left = turned(roll(l, -4, 1), roll(l, -2, 1), rot[6], rot[7])
        h_left = turned(l, roll(l, 2, 1), rot[6], rot[7])
        for part in range(2):
            strip[3 * part + c] = joined(3 * part + c, e_right[part], e_left[part])
            strip[6 + 3 * part + c] = joined(6 + 3 * part + c, h_right[part], h_left[part])
    strip[12] = joined(12, roll(right[1], 5, 1), roll(left[1], -1, 1))
    return strip


def next_row(values):
    return roll(values, -1, 0)


def prev_row(values):
    return roll(values, 1, 0)


def h_new(h, e, e_up, e_xn, e_yn):
    return (
        h[0] - STEP_DT * (e_yn[1] - e[2] - (e_up[1] - e[1])),
        h[1] - STEP_DT * (e_up[0] - e[0] - (e_xn[1] - e[2])),
        h[2] - STEP_DT * (e_xn[0] - e[1] - (e_yn[0] - e[0])),
    )


def e_new(e, h, h_down, h_xp, h_yp, coef):
    return (
        e[0] + coef * (h[2] - h_yp[1] - (h[1] - h_down[1])),
        e[1] + coef * (h[0] - h_down[0] - (h[2] - h_xp[1])),
        e[2] + coef * (h[1] - h_xp[0] - (h[0] - h_yp[0])),
    )


def strip_h(h, e):
    up = lanes_of((EXT, COLS)) < 8 * (NZ - 1)
    above = [jnp.where(up, roll(e[c], -8, 1), 0.0) for c in range(2)]
    return h_new(
        h,
        e,
        above,
        (next_row(e[1]), next_row(e[2])),
        (roll(e[0], -1, 1), roll(e[2], -1, 1)),
    )


def strip_e(e, h, coef):
    up = lanes_of((EXT, COLS)) >= 8
    below = [jnp.where(up, roll(h[c], 8, 1), 0.0) for c in range(2)]
    return e_new(
        e,
        h,
        below,
        (prev_row(h[1]), prev_row(h[2])),
        (roll(h[0], 1, 1), roll(h[2], 1, 1)),
        coef,
    )


def feet_kernel(
    counts,
    rows_b_hbm,
    rows_a_hbm,
    rot_hbm,
    phase_hbm,
    e_ref,
    h_ref,
    coef_ref,
    y_ref,
    x_ref,
    next_ref,
    prev_ref,
    rot_ref,
    phase_ref,
    sem,
):
    copies = fetch([(phase_hbm, phase_ref), (rot_hbm, rot_ref)], sem)
    copies += fetch_swapped((rows_a_hbm, rows_b_hbm), next_ref, prev_ref, is_even("gx"), sem, 2)
    arrived(copies)
    fill_tables(*counts, phase_ref[0], phase_ref[1], y_ref, x_ref)
    rot = [rot_ref[k : k + 1, :] for k in range(8)]
    row = lax.broadcasted_iota(jnp.int32, (8, COLS), 0)

    def foot(ahead, behind, k):
        return jnp.where(
            row < 2,
            roll(ahead, -2 * k, 0),
            jnp.where(row < 6, 0.0, roll(behind, 6 - 2 * k, 0)),
        )

    for quad in range(NZ // 4):
        for field, target in ((0, e_ref), (1, h_ref)):
            for c in range(3):
                n = (6 * field + c) * 4 + quad
                m = n + 12
                ahead = turned(next_ref[n], next_ref[m], rot[0], rot[1])
                behind = turned(prev_ref[n], prev_ref[m], rot[2], rot[3])
                for part in range(2):
                    for k in range(4):
                        target[part, c, 4 * quad + k] = foot(ahead[part], behind[part], k)
        ahead = roll(next_ref[24 + quad], -1, 0)
        behind = roll(prev_ref[24 + quad], 1, 0)
        for k in range(4):
            coef_ref[4 * quad + k] = foot(ahead, behind, k)


def fetch_edges(own_hbm, tail_hbm, cols_hbm, rot_hbm, edges, sem, first):
    own_ref, right_ref, left_ref, rot_ref = edges
    copies = fetch(
        [
            (own_hbm, own_ref.at[:, 0:ROWS]),
            (tail_hbm, own_ref.at[:, ROWS:EXT]),
            (rot_hbm, rot_ref),
        ],
        sem,
        first,
    )
    copies += fetch_swapped(cols_hbm, left_ref, right_ref, is_even("gy"), sem, first + 3)
    return copies


def edge_scratch():
    return [
        VMEM(shape, jnp.float32)
        for shape in (
            (13, EXT, COLS),
            (3, EXT, COLS),
            (3, EXT, COLS),
            (8, COLS),
        )
    ]


def block_scratch(parts):
    return [
        VMEM((parts, 3, NZ + 1, EXT, COLS), jnp.float32),
        VMEM((parts, 3, NZ + 1, EXT, COLS), jnp.float32),
        VMEM((NZ, EXT, COLS), jnp.float32),
        VMEM((parts, 4, 2, EXT, COLS), jnp.float32),
    ]


def fill_edges(edges, block, parts):
    own_ref, right_ref, left_ref, rot_ref = edges
    e_all, h_all, coef_all, edge_ref = block
    rot = [rot_ref[k : k + 1, :] for k in range(8)]
    for at in range(len(parts)):
        for c in range(3):
            e_all[at, c, NZ] = jnp.zeros((EXT, COLS), jnp.float32)
            h_all[at, c, 0] = jnp.zeros((EXT, COLS), jnp.float32)
    strip = strip_of(
        [own_ref[a] for a in range(13)],
        [right_ref[a] for a in range(3)],
        [left_ref[a] for a in range(3)],
        rot,
    )
    for at, part in enumerate(parts):
        e = tuple(strip[3 * part + c] for c in range(3))
        h = tuple(strip[6 + 3 * part + c] for c in range(3))
        for step in range(2):
            edge_ref[at, 2 * step, 0] = e[0]
            edge_ref[at, 2 * step, 1] = e[2]
            h = strip_h(h, e)
            edge_ref[at, 2 * step + 1, 0] = h[0]
            edge_ref[at, 2 * step + 1, 1] = h[2]
            if step == 0:
                e = strip_e(e, h, strip[12])


def beside(edge, values, z, ahead):
    shift = COLS + (125 if ahead else 123) - 8 * z
    shift = shift % COLS if isinstance(z, int) else lax.rem(shift, COLS)
    lane = lanes_of(values.shape)
    if ahead:
        return jnp.where(lane == COLS - 1, roll(edge, shift, 1), roll(values, -1, 1))
    return jnp.where(lane == 0, roll(edge, shift, 1), roll(values, 1, 1))


def updates(block, parts):
    e_all, h_all, coef_all, edge_ref = block

    def do_h(step, layers):
        new = []
        for at in range(parts):
            for z in layers:
                e = tuple(e_all[at, c, z] for c in range(3))
                h = tuple(h_all[at, c, z + 1] for c in range(3))
                e_up = (e_all[at, 0, z + 1], e_all[at, 1, z + 1])
                e_yn = (
                    beside(edge_ref[at, 2 * step, 0], e[0], z, True),
                    beside(edge_ref[at, 2 * step, 1], e[2], z, True),
                )
                values = h_new(h, e, e_up, (next_row(e[1]), next_row(e[2])), e_yn)
                new.append((at, z, values))
        for at, z, values in new:
            for c in range(3):
                h_all[at, c, z + 1] = values[c]

    def do_e(step, layers):
        new = []
        for at in range(parts):
            for z in layers:
                e = tuple(e_all[at, c, z] for c in range(3))
                h = tuple(h_all[at, c, z + 1] for c in range(3))
                h_down = (h_all[at, 0, z], h_all[at, 1, z])
                h_yp = (
                    beside(edge_ref[at, 2 * step + 1, 0], h[0], z, False),
                    beside(edge_ref[at, 2 * step + 1, 1], h[2], z, False),
                )
                values = e_new(
                    e, h, h_down, (prev_row(h[1]), prev_row(h[2])), h_yp, coef_all[z]
                )
                new.append((at, z, values))
        rows = slice(0, EXT if step == 0 else ROWS)
        for at, z, values in new:
            for c in range(3):
                e_all[at, c, z, rows, :] = values[c][rows]

    return do_h, do_e


def plane_kernel(
    e_hbm,
    h_hbm,
    coef_hbm,
    e_foot_hbm,
    h_foot_hbm,
    coef_foot_hbm,
    own_hbm,
    tail_hbm,
    cols_b_hbm,
    cols_a_hbm,
    rot_hbm,
    wave_hbm,
    monitor_ref,
    spread_ref,
    *scratch,
):
    edges, block = scratch[0:4], scratch[4:8]
    wave_ref, sem = scratch[8:10]
    e_all, h_all, coef_all, edge_ref = block
    copies = fetch_edges(own_hbm, tail_hbm, (cols_a_hbm, cols_b_hbm), rot_hbm, edges, sem, 0)
    level = monitor_ref[0]
    low = jnp.clip(level - 2, 0, NZ - 5)
    here, there = pl.ds(low, 5), pl.ds(low + 1, 5)
    large = fetch(
        [
            (e_hbm.at[:, :, here], e_all.at[:, :, here, 0:ROWS, :]),
            (h_hbm.at[:, :, here], h_all.at[:, :, there, 0:ROWS, :]),
            (coef_hbm.at[here], coef_all.at[here, 0:ROWS, :]),
            (e_foot_hbm.at[:, :, here], e_all.at[:, :, here, ROWS:EXT, :]),
            (h_foot_hbm.at[:, :, here], h_all.at[:, :, there, ROWS:EXT, :]),
            (coef_foot_hbm.at[here], coef_all.at[here, ROWS:EXT, :]),
            (wave_hbm, wave_ref),
        ],
        sem,
        5,
    )
    arrived(copies)
    fill_edges(edges, block, (0, 1))
    arrived(large)
    near = {}
    for k in range(-2, 3):
        z = jnp.clip(level + k, 0, NZ - 1)
        for part in range(2):
            for c in range(3):
                if c < 2 or k < 2:
                    e = e_all[part, c, z]
                    near["e", part, c, k] = jnp.where(level + k < NZ, e, 0.0) if k > 0 else e
                if k < 2 and (c < 2 or k > -2):
                    h = h_all[part, c, z + 1]
                    near["h", part, c, k] = jnp.where(level + k >= 0, h, 0.0) if k < 0 else h
    def update_h(step, part, k, wanted):
        z = jnp.clip(level + k, 0, NZ - 1)
        ex, ey, ez = (near["e", part, c, k] for c in range(3))
        edge = edge_ref.at[part, 2 * step]
        new = {}
        if 0 in wanted:
            new[0] = beside(edge[1], ez, z, True) - ez - (near["e", part, 1, k + 1] - ey)
        if 1 in wanted:
            new[1] = near["e", part, 0, k + 1] - ex - (next_row(ez) - ez)
        if 2 in wanted:
            new[2] = next_row(ey) - ey - (beside(edge[0], ex, z, True) - ex)
        for c, curl in new.items():
            values = near["h", part, c, k] - STEP_DT * curl
            near["h", part, c, k] = jnp.where(level + k >= 0, values, 0.0) if k < 0 else values

    def update_e(step, part, k, wanted):
        z = jnp.clip(level + k, 0, NZ - 1)
        hx, hy, hz = (near["h", part, c, k] for c in range(3))
        edge = edge_ref.at[part, 2 * step + 1]
        coef = coef_all[z]
        new = {}
        if 0 in wanted:
            new[0] = hz - beside(edge[1], hz, z, False) - (hy - near["h", part, 1, k - 1])
        if 1 in wanted:
            new[1] = hx - near["h", part, 0, k - 1] - (hz - prev_row(hz))
        if 2 in wanted:
            new[2] = hy - prev_row(hy) - (hx - beside(edge[0], hx, z, False))
        for c, curl in new.items():
            values = near["e", part, c, k] + coef * curl
            near["e", part, c, k] = jnp.where(level + k < NZ, values, 0.0) if k > 0 else values

    for part in range(2):
        for k in range(-2, 2):
            update_h(0, part, k, (0, 1, 2) if k > -2 else (0, 1))
        for k in range(-1, 2):
            update_e(0, part, k, (0, 1, 2) if k < 1 else (0, 1))
        update_h(1, part, -1, (0, 1))
        update_h(1, part, 0, (0, 1, 2))
        update_e(1, part, 0, (0, 1))
    re, im = (
        jnp.concatenate([near["e", part, c, 0][0:ROWS] for c in range(2)], axis=0)
        for part in range(2)
    )
    y_section(re, im, wave_ref, spread_ref)


def field_kernel(parts, inputs, *refs):
    (
        e_hbm,
        h_hbm,
        coef_hbm,
        e_foot_hbm,
        h_foot_hbm,
        coef_foot_hbm,
        own_hbm,
        tail_hbm,
        cols_b_hbm,
        cols_a_hbm,
        rot_hbm,
    ) = refs[0:11]
    e_out, h_out, token_hbm = refs[inputs : inputs + 3]
    scratch = refs[inputs + 3 :]
    edges, block, sem = scratch[0:4], scratch[4:8], scratch[8]
    e_all, h_all, coef_all, _ = block
    copies = fetch_edges(own_hbm, tail_hbm, (cols_a_hbm, cols_b_hbm), rot_hbm, edges, sem, 0)
    some = slice(parts[0], parts[-1] + 1)
    quads = range(NZ // 4)
    loads = []
    for quad in quads:
        here, there = pl.ds(4 * quad, 4), pl.ds(4 * quad + 1, 4)
        loads.append(
            fetch(
                [
                    (e_hbm.at[some, :, here], e_all.at[:, :, here, 0:ROWS, :]),
                    (e_foot_hbm.at[some, :, here], e_all.at[:, :, here, ROWS:EXT, :]),
                    (h_hbm.at[some, :, here], h_all.at[:, :, there, 0:ROWS, :]),
                    (h_foot_hbm.at[some, :, here], h_all.at[:, :, there, ROWS:EXT, :]),
                    (coef_hbm.at[here], coef_all.at[here, 0:ROWS, :]),
                    (coef_foot_hbm.at[here], coef_all.at[here, ROWS:EXT, :]),
                ],
                sem,
                7 + 6 * quad,
            )
        )
    arrived(copies)
    token = fetch([(edges[3], token_hbm)], sem)
    fill_edges(edges, block, parts)
    do_h, do_e = updates(block, len(parts))

    def finish(quad):
        layers = [4 * quad + k for k in range(4)]
        here, there = pl.ds(4 * quad, 4), pl.ds(4 * quad + 1, 4)
        do_h(1, layers)
        fetch([(h_all.at[:, :, there, 0:ROWS, :], h_out.at[some, :, here])], sem, 5)
        do_e(1, layers)
        fetch([(e_all.at[:, :, here, 0:ROWS, :], e_out.at[some, :, here])], sem, 6)

    arrived(loads[0])
    for quad in quads:
        if quad + 1 < len(quads):
            arrived(loads[quad + 1])
        layers = [4 * quad + k for k in range(4)]
        do_h(0, layers)
        do_e(0, layers)
        if quad > 0:
            finish(quad - 1)
    finish(quads[-1])
    arrived(token)
    stored = (
        (h_all.at[:, :, 1 : NZ + 1, 0:ROWS, :], h_out.at[some]),
        (e_all.at[:, :, 0:NZ, 0:ROWS, :], e_out.at[some]),
    )
    for k, (source, target) in enumerate(stored):
        pltpu.make_async_copy(source, target, sem.at[5 + k]).wait()


def y_section(re, im, wave_ref, spread_ref):
    wave = wave_ref[...]
    _, owners, _, lanes = spread_ref.shape
    each = lanes // 4
    rows = re.shape[0]
    both = jnp.concatenate(
        [jnp.concatenate([re, im], axis=1), jnp.concatenate([im, -re], axis=1)], axis=0
    )
    both = jnp.dot(
        both, wave, precision=lax.Precision.HIGHEST, preferred_element_type=jnp.float32
    )
    out = (both[0:rows], both[rows:])
    for owner in range(owners):
        pieces = [
            out[part][c * ROWS : (c + 1) * ROWS, owner * each : (owner + 1) * each]
            for part in range(2)
            for c in range(2)
        ]
        joined = jnp.concatenate(pieces, axis=1)
        for half in range(2):
            spread_ref[half, owner] = joined


def x_kernel(got_ref, wave_ref, after_hbm, part_ref):
    each = got_ref.shape[0] // 2
    totals = []
    for half in range(2):
        total = got_ref[half * each]
        for source in range(1, each):
            total = total + got_ref[half * each + source]
        totals.append(total)
    total = jnp.concatenate(totals, axis=0)
    half = total.shape[1] // 2
    other = roll(total, half, 1)
    other = jnp.where(lanes_of(other.shape) < half, other, -other)
    result = jnp.dot(
        wave_ref[...],
        jnp.concatenate([total, other], axis=0),
        precision=lax.Precision.HIGHEST,
        preferred_element_type=jnp.float32,
    )
    part_ref[...] = result.reshape(part_ref.shape)


def groups(mesh_shape):
    count_x, count_y = mesh_shape
    rest = count_x // 2
    near = [
        [(half * rest + r) * count_y + y for half in range(2) for y in range(count_y)]
        for r in range(rest)
    ]
    far = [
        [(half * rest + r) * count_y + y for r in range(rest)]
        for half in range(2)
        for y in range(count_y)
    ]
    return near, far


def sum_kernel(got_ref, out_ref):
    total = got_ref[0]
    for source in range(1, got_ref.shape[0]):
        total = total + got_ref[source]
    each = total.shape[1] // 4
    for c in range(2):
        for part in range(2):
            start = (2 * part + c) * each
            out_ref[c, part] = total[:, start : start + each]


def fill_tables(count_x, count_y, theta_x, theta_y, y_ref, x_ref):
    index_x, index_y = lax.axis_index("gx"), lax.axis_index("gy")
    total_x, total_y = ROWS * count_x, COLS * count_y

    def waves(product, place, total, theta):
        angle = (
            2.0 * math.pi * (product & (total - 1)).astype(jnp.float32)
            + theta * place.astype(jnp.float32)
        ) / total
        return jnp.cos(angle), jnp.sin(angle)

    def joined(a, b):
        return a[0] * b[0] - a[1] * b[1], a[1] * b[0] + a[0] * b[1]

    scale = 1.0 / math.sqrt(total_x * total_y)
    blocks = COLS // 8
    start = index_y * COLS
    order = lax.broadcasted_iota(jnp.int32, (blocks, ORD_Y), 1) - ORD_Y // 2
    place = start + 8 * lax.broadcasted_iota(jnp.int32, (blocks, ORD_Y), 0)
    coarse = waves(order * place, place, total_y, theta_y)
    place = lax.broadcasted_iota(jnp.int32, (8, ORD_Y), 0)
    fine = waves(order[0:8] * place, place, total_y, theta_y)
    fine = (fine[0] * scale, fine[1] * scale)
    for block in range(blocks):
        part = tuple(values[block : block + 1] for values in coarse)
        cos, sin = joined(part, fine)
        y_ref[8 * block : 8 * block + 8, :] = cos
        y_ref[COLS + 8 * block : COLS + 8 * block + 8, :] = sin
    blocks = ORD_X // 16
    shape = (blocks, 4 * ROWS)
    rest = count_x // 2
    lane = lax.broadcasted_iota(jnp.int32, shape, 1)
    block_x = lax.rem(index_x, rest) + rest * (lane // ROWS % 2)
    place = block_x * ROWS + lane % ROWS
    own_half = index_x // rest * (ORD_X // 2)
    order = 8 * lax.broadcasted_iota(jnp.int32, shape, 0) + own_half - ORD_X // 2
    coarse = waves(order * place, place, total_x, theta_x)
    order = lax.broadcasted_iota(jnp.int32, (8, 4 * ROWS), 0)
    fine = waves(order * place[0:8], place[0:8], total_x, 0.0)
    for block in range(blocks):
        part = tuple(values[block : block + 1] for values in coarse)
        cos, sin = joined(part, fine)
        x_ref[8 * block : 8 * block + 8, :] = jnp.where(lane[0:8] < 2 * ROWS, cos, sin)


def params(mebibytes):
    return pltpu.CompilerParams(vmem_limit_bytes=mebibytes << 20)


def cost(microseconds):
    return pl.CostEstimate(
        flops=0, bytes_accessed=microseconds * 3_000_000, transcendentals=0
    )


def f32(*shape):
    return jax.ShapeDtypeStruct(shape, jnp.float32)


def shards(
    e_field, h_field, material, pattern, base_eps, mode_table, nodes, bloch_phase, monitor_z
):
    count_x = lax.axis_size("gx")
    count_y = lax.axis_size("gy")
    each_p = ORD_X // count_x
    each_q = ORD_Y // count_y
    vmem = pl.BlockSpec(memory_space=VMEM)
    hbm = pl.BlockSpec(memory_space=pltpu.HBM)
    f32_vmem = lambda *shape: VMEM(shape, jnp.float32)
    dma = pltpu.SemaphoreType.DMA

    table, rows_a, rows_b = pl.pallas_call(
        rows_kernel,
        out_shape=(
            f32(8, COLS),
            f32(MAIN_BLOCKS, 8, COLS),
            f32(MAIN_BLOCKS, 8, COLS),
        ),
        in_specs=[hbm] * 7,
        out_specs=(vmem,) * 3,
        scratch_shapes=[
            f32_vmem(2, 2, 3, NZ, 8, COLS),
            f32_vmem(2, 2, 3, NZ, 8, COLS),
            VMEM((2, NZ, 8, COLS), jnp.int32),
            VMEM((2, NZ, 8, COLS), jnp.int32),
            SMEM(base_eps.shape, jnp.float32),
            SMEM(mode_table.shape, jnp.float32),
            SMEM(nodes.shape, jnp.float32),
            dma((11,)),
        ],
        compiler_params=params(64),
        cost_estimate=cost(3),
        name="rows",
    )(e_field, h_field, material, pattern, base_eps, mode_table, nodes)
    rows_b = swapped(rows_b, "gx", False)
    rows_a = swapped(rows_a, "gx", True)
    own, cols_a, cols_b, coef = pl.pallas_call(
        own_kernel,
        out_shape=(
            f32(13, ROWS, COLS),
            f32(3, ROWS, COLS),
            f32(3, ROWS, COLS),
            f32(NZ, ROWS, COLS),
        ),
        in_specs=[hbm] * 5,
        out_specs=(vmem,) * 4,
        scratch_shapes=[
            f32_vmem(*e_field.shape),
            f32_vmem(*h_field.shape),
            VMEM(material.shape, jnp.int32),
            VMEM(pattern.shape, jnp.int32),
            f32_vmem(8, COLS),
            dma((5,)),
        ],
        compiler_params=params(64),
        cost_estimate=cost(4),
        name="own",
    )(e_field, h_field, material, pattern, table)
    tail, cols_a, cols_b, rot = pl.pallas_call(
        pack_kernel,
        out_shape=(
            f32(13, EXT - ROWS, COLS),
            f32(3, EXT, COLS),
            f32(3, EXT, COLS),
            f32(8, COLS),
        ),
        in_specs=[hbm] * 5,
        out_specs=(vmem,) * 4,
        scratch_shapes=[
            f32_vmem(MAIN_BLOCKS, 8, COLS),
            f32_vmem(MAIN_BLOCKS, 8, COLS),
            SMEM((2,), jnp.float32),
            dma((5,)),
        ],
        compiler_params=params(64),
        cost_estimate=cost(2),
        name="pack",
    )(cols_a, cols_b, rows_b, rows_a, bloch_phase)
    cols_b = swapped(cols_b, "gy", False)
    cols_a = swapped(cols_a, "gy", True)
    *feet, y_wave, x_wave = pl.pallas_call(
        functools.partial(feet_kernel, (count_x, count_y)),
        out_shape=(
            f32(2, 3, NZ, EXT - ROWS, COLS),
            f32(2, 3, NZ, EXT - ROWS, COLS),
            f32(NZ, EXT - ROWS, COLS),
            f32(2 * COLS, ORD_Y),
            f32(ORD_X // 2, 4 * ROWS),
        ),
        in_specs=[hbm] * 4,
        out_specs=(vmem,) * 5,
        scratch_shapes=[
            f32_vmem(MAIN_BLOCKS, 8, COLS),
            f32_vmem(MAIN_BLOCKS, 8, COLS),
            f32_vmem(8, COLS),
            SMEM((2,), jnp.float32),
            dma((4,)),
        ],
        compiler_params=params(64),
        cost_estimate=cost(2),
        name="feet",
    )(rows_b, rows_a, rot, bloch_phase)
    around = (e_field, h_field, coef, *feet, own, tail, cols_b, cols_a, rot)
    spread = pl.pallas_call(
        plane_kernel,
        out_shape=f32(2, count_y, ROWS, 4 * each_q),
        in_specs=[hbm] * 12 + [pl.BlockSpec(memory_space=SMEM)],
        out_specs=vmem,
        scratch_shapes=[
            *edge_scratch(),
            *block_scratch(2),
            f32_vmem(*y_wave.shape),
            dma((12,)),
        ],
        compiler_params=params(60),
        cost_estimate=cost(3),
        name="plane",
    )(*around, y_wave, monitor_z)

    near, far = groups((count_x, count_y))
    both = ("gx", "gy")
    spread = spread.reshape(2 * count_y, ROWS, 4 * each_q)
    got = lax.all_to_all(spread, both, 0, 0, tiled=True, axis_index_groups=near)
    e_out, h_out, token = pl.pallas_call(
        functools.partial(field_kernel, (0, 1), 12),
        out_shape=(f32(*e_field.shape), f32(*h_field.shape), f32(8, COLS)),
        in_specs=[hbm] * 12,
        out_specs=(hbm, hbm, hbm),
        scratch_shapes=[*edge_scratch(), *block_scratch(2), dma((31,))],
        compiler_params=params(60),
        cost_estimate=cost(6),
        name="fields",
    )(*around, spread)
    partial = pl.pallas_call(
        x_kernel,
        out_shape=f32(count_x // 2, each_p, 4 * each_q),
        in_specs=[vmem, vmem, hbm],
        out_specs=vmem,
        compiler_params=params(8),
        cost_estimate=cost(1),
        name="x_section",
    )(got, x_wave, token)
    got = lax.all_to_all(partial, both, 0, 0, tiled=True, axis_index_groups=far)
    orders = pl.pallas_call(
        sum_kernel,
        out_shape=f32(2, 2, each_p, each_q),
        in_specs=[vmem],
        out_specs=vmem,
        compiler_params=params(8),
        cost_estimate=cost(1),
        name="order_sum",
    )(got)
    return e_out, h_out, orders


def solution(mesh):
    grid = P(None, None, None, "gx", "gy")
    cells = P(None, "gx", "gy")
    return jax.shard_map(
        shards,
        mesh=mesh,
        in_specs=(grid, grid, cells, cells, P(), P(), P(), P(), P()),
        out_specs=(grid, grid, P(None, None, "gx", "gy")),
        check_vma=False,
    )
```

```python
import functools
import math

import jax
import jax.numpy as jnp
from jax import lax
from jax.experimental import pallas as pl
from jax.experimental.pallas import tpu as pltpu
from jax.sharding import PartitionSpec as P

STEP_DT = 0.5
ORD_X = 256
ORD_Y = 256
NZ = 16
ROWS = 32
COLS = 128
EXT = 40
MAIN_BLOCKS = 48
VMEM = pltpu.VMEM
SMEM = pltpu.SMEM


def swapped(block, axis, first):
    count = lax.axis_size(axis)
    route = []
    for i in range(count):
        ahead = (i % 2 == 0) == first
        route.append((i, (i + 1) % count if ahead else (i - 1) % count))
    return lax.ppermute(block, axis, route)


def roll(values, shift, axis):
    size = values.shape[axis]
    if isinstance(shift, int):
        shift = shift % size
        if shift == 0:
            return values
    return pltpu.roll(values, shift, axis)


def lanes_of(shape):
    return lax.broadcasted_iota(jnp.int32, shape, len(shape) - 1)


def coef_table(base_ref, mode_ref, node_ref):
    lane = lanes_of((8, 128))
    material = lane // 16
    pattern = lane % 16
    base = jnp.zeros((8, 128), jnp.float32)
    for m in range(8):
        base = jnp.where(material == m, base_ref[m], base)
    change = jnp.zeros((8, 128), jnp.float32)
    for k in range(4):
        mode = jnp.zeros((8, 128), jnp.float32)
        for p in range(16):
            mode = jnp.where(pattern == p, mode_ref[k, p], mode)
        change = change + node_ref[k] * mode
    return STEP_DT / (base * (1.0 + change))


def look_up(table, pair):
    rows = [
        jnp.take_along_axis(table, pair[8 * r : 8 * r + 8], axis=1)
        for r in range(pair.shape[0] // 8)
    ]
    return jnp.concatenate(rows, axis=0)


def fetch(pairs, sem, first=0):
    copies = [
        pltpu.make_async_copy(source, target, sem.at[first + k])
        for k, (source, target) in enumerate(pairs)
    ]
    for copy in copies:
        copy.start()
    return copies


def arrived(copies):
    for copy in copies:
        copy.wait()


def is_even(axis):
    return lax.rem(lax.axis_index(axis), 2) == 0


def fetch_swapped(got, ahead_ref, behind_ref, even, sem, first):
    @pl.when(even)
    def _():
        fetch(((got[0], ahead_ref), (got[1], behind_ref)), sem, first)

    @pl.when(jnp.logical_not(even))
    def _():
        fetch(((got[1], ahead_ref), (got[0], behind_ref)), sem, first)

    return [
        pltpu.make_async_copy(got[k], ref, sem.at[first + k])
        for k, ref in enumerate((ahead_ref, behind_ref))
    ]


def plane_of(e_ref, h_ref, n, z):
    ref = e_ref if n < 6 else h_ref
    return ref[(n % 6) // 3, n % 3, z]


def rows_kernel(
    e_hbm,
    h_hbm,
    material_hbm,
    pattern_hbm,
    base_hbm,
    mode_hbm,
    node_hbm,
    table_ref,
    first_swap_ref,
    second_swap_ref,
    e_ref,
    h_ref,
    material_ref,
    pattern_ref,
    base_ref,
    mode_ref,
    node_ref,
    sem,
):
    small = fetch([(base_hbm, base_ref), (mode_hbm, mode_ref), (node_hbm, node_ref)], sem)
    ends = (slice(0, 8), slice(ROWS - 8, ROWS))
    large = fetch(
        [
            (source.at[..., end, :], target.at[k])
            for source, target in (
                (e_hbm, e_ref),
                (h_hbm, h_ref),
                (material_hbm, material_ref),
                (pattern_hbm, pattern_ref),
            )
            for k, end in enumerate(ends)
        ],
        sem,
        3,
    )
    even = is_even("gx")
    arrived(small)
    table = coef_table(base_ref, mode_ref, node_ref)
    table_ref[...] = table
    row = lax.broadcasted_iota(jnp.int32, (8, COLS), 0)
    for n in range(12):
        if n % 6 == 0:
            arrived(large[0:2] if n == 0 else large[2:])
        for quad in range(NZ // 4):
            blocks = []
            for k in range(2):
                pieces = []
                for z in range(4 * quad, 4 * quad + 4):
                    ref = e_ref if n < 6 else h_ref
                    values = ref[k, (n % 6) // 3, n % 3, z]
                    if n == 6:
                        coef = look_up(table, material_ref[k, z] * 16 + pattern_ref[k, z])
                        coef = roll(coef, -1 if k else 1, 0)
                        values = jnp.where(row == (6 if k else 1), coef, values)
                    pieces.append(values[6 * k : 6 * k + 2])
                blocks.append(jnp.concatenate(pieces, axis=0))
            first_swap_ref[4 * n + quad] = jnp.where(even, blocks[1], blocks[0])
            second_swap_ref[4 * n + quad] = jnp.where(even, blocks[0], blocks[1])


def messages(own_ref, rows, first_swap_ref, second_swap_ref):
    even = is_even("gy")
    place = lanes_of((rows.stop - rows.start, COLS)) % 8
    for c in range(3):
        e_re, e_im, h_re, h_im = (own_ref[3 * k + c] for k in range(4))
        right = jnp.where(
            place < 4,
            jnp.where(place < 2, roll(h_re, -4, 1), roll(h_im, -2, 1)),
            jnp.where(place < 6, e_re, roll(e_im, 2, 1)),
        )
        left = jnp.where(
            place < 4,
            jnp.where(place < 2, roll(h_im, -6, 1), roll(h_re, -4, 1)),
            jnp.where(place < 6, roll(e_im, -2, 1), e_re),
        )
        if c == 1:
            coef = own_ref[12]
            right = jnp.where(place == 0, roll(coef, -5, 1), right)
            left = jnp.where(place == 3, roll(coef, -3, 1), left)
        first_swap_ref[c, rows, :] = jnp.where(even, right, left)
        second_swap_ref[c, rows, :] = jnp.where(even, left, right)


def own_kernel(
    e_hbm,
    h_hbm,
    material_hbm,
    pattern_hbm,
    table_hbm,
    own_ref,
    first_swap_ref,
    second_swap_ref,
    coef_ref,
    e_ref,
    h_ref,
    material_ref,
    pattern_ref,
    table_ref,
    sem,
):
    small = fetch(
        [(material_hbm, material_ref), (pattern_hbm, pattern_ref), (table_hbm, table_ref)], sem
    )
    large = fetch([(e_hbm, e_ref), (h_hbm, h_ref)], sem, 3)
    arrived(small)
    table = table_ref[...]
    for z in range(NZ):
        coef_ref[z] = look_up(table, material_ref[z] * 16 + pattern_ref[z])
    group = lanes_of((ROWS, COLS)) // 8
    for n in range(13):
        if n in (0, 6):
            arrived(large[n // 6 : n // 6 + 1])
        packed = jnp.zeros((ROWS, COLS), jnp.float32)
        for z in range(NZ):
            values = coef_ref[z] if n == 12 else plane_of(e_ref, h_ref, n, z)
            packed = jnp.where(group == z, roll(values, 8 * z + 6, 1), packed)
        own_ref[n] = packed
    messages(own_ref, slice(0, ROWS), first_swap_ref, second_swap_ref)


def bloch_factors(theta_x, theta_y):
    count_x, count_y = lax.axis_size("gx"), lax.axis_size("gy")
    index_x, index_y = lax.axis_index("gx"), lax.axis_index("gy")
    row = lax.broadcasted_iota(jnp.int32, (8, COLS), 0)
    angle = jnp.where(row < 4, theta_x, theta_y)
    flags = [
        jnp.where(flag, 1, 0)
        for flag in (index_x == count_x - 1, index_x == 0, index_y == 0, index_y == count_y - 1)
    ]
    here = jnp.where(
        row < 4,
        jnp.where(row < 2, flags[0], flags[1]),
        jnp.where(row < 6, flags[2], flags[3]),
    )
    angle = jnp.where(here == 1, angle, 0.0)
    angle = jnp.where(row // 2 == 1, -angle, jnp.where(row // 2 == 2, -angle, angle))
    return jnp.where(row % 2 == 0, jnp.cos(angle), jnp.sin(angle))


def pack_kernel(
    main_a_hbm,
    main_b_hbm,
    rows_b_hbm,
    rows_a_hbm,
    phase_hbm,
    tail_ref,
    first_swap_ref,
    second_swap_ref,
    rot_ref,
    next_ref,
    prev_ref,
    phase_ref,
    sem,
):
    small = fetch([(phase_hbm, phase_ref)], sem)
    copies = fetch_swapped((rows_a_hbm, rows_b_hbm), next_ref, prev_ref, is_even("gx"), sem, 1)
    mains = fetch(
        [
            (main_a_hbm, first_swap_ref.at[:, 0:ROWS]),
            (main_b_hbm, second_swap_ref.at[:, 0:ROWS]),
        ],
        sem,
        3,
    )
    arrived(small)
    rot_ref[...] = bloch_factors(phase_ref[0], phase_ref[1])
    arrived(copies)
    rot = [rot_ref[k : k + 1, :] for k in range(8)]
    group = lanes_of((2, COLS)) // 8
    row = lax.broadcasted_iota(jnp.int32, (8, COLS), 0)
    lane = lanes_of((8, COLS))
    group = (lane + COLS + 2 - 4 * (row % 2)) % COLS // 8

    def packed(blocks):
        total = jnp.zeros((8, COLS), jnp.float32)
        for quad, values in enumerate(blocks):
            moved = pltpu.roll(values, 32 * quad, 1, stride=4, stride_axis=0)
            total = jnp.where(group == 4 * quad + row // 2, moved, total)
        total = jnp.where(row % 2 == 1, roll(total, 2, 1), roll(total, 6, 1))
        total = total + roll(total, 2, 0)
        return total + roll(total, 4, 0)

    quads = range(NZ // 4)
    def joined(ahead, behind):
        return jnp.where(row < 2, ahead, jnp.where(row < 6, 0.0, behind))

    for n in (0, 1, 2, 6, 7, 8):
        found = [
            [packed([ref[4 * (n + 3 * part) + quad] for quad in quads]) for part in range(2)]
            for ref in (next_ref, prev_ref)
        ]
        if n == 6:
            tail_ref[12] = joined(roll(found[0][0], -1, 0), roll(found[1][0], 1, 0))
        ahead = turned(*found[0], rot[0], rot[1])
        behind = turned(*found[1], rot[2], rot[3])
        for part in range(2):
            tail_ref[n + 3 * part] = joined(ahead[part], behind[part])
    messages(tail_ref, slice(ROWS, EXT), first_swap_ref, second_swap_ref)
    arrived(mains)


def turned(re, im, cos, sin):
    return re * cos - im * sin, im * cos + re * sin


def strip_of(own, right, left, rot):
    place = lanes_of(own[0].shape) % 8

    def joined(index, from_right, from_left):
        return jnp.where(
            place < 4,
            jnp.where(place < 2, roll(own[index], -4, 1), from_left),
            jnp.where(place < 6, from_right, own[index]),
        )

    strip = [None] * 13
    for c in range(3):
        r = right[c]
        l = left[c]
        e_right = turned(r, roll(r, -2, 1), rot[4], rot[5])
        h_right = turned(roll(r, 4, 1), roll(r, 2, 1), rot[4], rot[5])
        e_left = turned(roll(l, -4, 1), roll(l, -2, 1), rot[6], rot[7])
        h_left = turned(l, roll(l, 2, 1), rot[6], rot[7])
        for part in range(2):
            strip[3 * part + c] = joined(3 * part + c, e_right[part], e_left[part])
            strip[6 + 3 * part + c] = joined(6 + 3 * part + c, h_right[part], h_left[part])
    strip[12] = joined(12, roll(right[1], 5, 1), roll(left[1], -1, 1))
    return strip


def next_row(values):
    return roll(values, -1, 0)


def prev_row(values):
    return roll(values, 1, 0)


def h_new(h, e, e_up, e_xn, e_yn):
    return (
        h[0] - STEP_DT * (e_yn[1] - e[2] - (e_up[1] - e[1])),
        h[1] - STEP_DT * (e_up[0] - e[0] - (e_xn[1] - e[2])),
        h[2] - STEP_DT * (e_xn[0] - e[1] - (e_yn[0] - e[0])),
    )


def e_new(e, h, h_down, h_xp, h_yp, coef):
    return (
        e[0] + coef * (h[2] - h_yp[1] - (h[1] - h_down[1])),
        e[1] + coef * (h[0] - h_down[0] - (h[2] - h_xp[1])),
        e[2] + coef * (h[1] - h_xp[0] - (h[0] - h_yp[0])),
    )


def strip_h(h, e):
    up = lanes_of((EXT, COLS)) < 8 * (NZ - 1)
    above = [jnp.where(up, roll(e[c], -8, 1), 0.0) for c in range(2)]
    return h_new(
        h,
        e,
        above,
        (next_row(e[1]), next_row(e[2])),
        (roll(e[0], -1, 1), roll(e[2], -1, 1)),
    )


def strip_e(e, h, coef):
    up = lanes_of((EXT, COLS)) >= 8
    below = [jnp.where(up, roll(h[c], 8, 1), 0.0) for c in range(2)]
    return e_new(
        e,
        h,
        below,
        (prev_row(h[1]), prev_row(h[2])),
        (roll(h[0], 1, 1), roll(h[2], 1, 1)),
        coef,
    )


def feet_kernel(
    counts,
    rows_b_hbm,
    rows_a_hbm,
    rot_hbm,
    phase_hbm,
    e_ref,
    h_ref,
    coef_ref,
    y_ref,
    x_ref,
    next_ref,
    prev_ref,
    rot_ref,
    phase_ref,
    sem,
):
    copies = fetch([(phase_hbm, phase_ref), (rot_hbm, rot_ref)], sem)
    copies += fetch_swapped((rows_a_hbm, rows_b_hbm), next_ref, prev_ref, is_even("gx"), sem, 2)
    arrived(copies)
    fill_tables(*counts, phase_ref[0], phase_ref[1], y_ref, x_ref)
    rot = [rot_ref[k : k + 1, :] for k in range(8)]
    row = lax.broadcasted_iota(jnp.int32, (8, COLS), 0)

    def foot(ahead, behind, k):
        return jnp.where(
            row < 2,
            roll(ahead, -2 * k, 0),
            jnp.where(row < 6, 0.0, roll(behind, 6 - 2 * k, 0)),
        )

    for quad in range(NZ // 4):
        for field, target in ((0, e_ref), (1, h_ref)):
            for c in range(3):
                n = (6 * field + c) * 4 + quad
                m = n + 12
                ahead = turned(next_ref[n], next_ref[m], rot[0], rot[1])
                behind = turned(prev_ref[n], prev_ref[m], rot[2], rot[3])
                for part in range(2):
                    for k in range(4):
                        target[part, c, 4 * quad + k] = foot(ahead[part], behind[part], k)
        ahead = roll(next_ref[24 + quad], -1, 0)
        behind = roll(prev_ref[24 + quad], 1, 0)
        for k in range(4):
            coef_ref[4 * quad + k] = foot(ahead, behind, k)


def fetch_edges(own_hbm, tail_hbm, cols_hbm, rot_hbm, edges, sem, first):
    own_ref, right_ref, left_ref, rot_ref = edges
    copies = fetch(
        [
            (own_hbm, own_ref.at[:, 0:ROWS]),
            (tail_hbm, own_ref.at[:, ROWS:EXT]),
            (rot_hbm, rot_ref),
        ],
        sem,
        first,
    )
    copies += fetch_swapped(cols_hbm, left_ref, right_ref, is_even("gy"), sem, first + 3)
    return copies


def edge_scratch():
    return [
        VMEM(shape, jnp.float32)
        for shape in (
            (13, EXT, COLS),
            (3, EXT, COLS),
            (3, EXT, COLS),
            (8, COLS),
        )
    ]


def block_scratch(parts):
    return [
        VMEM((parts, 3, NZ + 1, EXT, COLS), jnp.float32),
        VMEM((parts, 3, NZ + 1, EXT, COLS), jnp.float32),
        VMEM((NZ, EXT, COLS), jnp.float32),
        VMEM((parts, 4, 2, EXT, COLS), jnp.float32),
    ]


def fill_edges(edges, block, parts):
    own_ref, right_ref, left_ref, rot_ref = edges
    e_all, h_all, coef_all, edge_ref = block
    rot = [rot_ref[k : k + 1, :] for k in range(8)]
    for at in range(len(parts)):
        for c in range(3):
            e_all[at, c, NZ] = jnp.zeros((EXT, COLS), jnp.float32)
            h_all[at, c, 0] = jnp.zeros((EXT, COLS), jnp.float32)
    strip = strip_of(
        [own_ref[a] for a in range(13)],
        [right_ref[a] for a in range(3)],
        [left_ref[a] for a in range(3)],
        rot,
    )
    for at, part in enumerate(parts):
        e = tuple(strip[3 * part + c] for c in range(3))
        h = tuple(strip[6 + 3 * part + c] for c in range(3))
        for step in range(2):
            edge_ref[at, 2 * step, 0] = e[0]
            edge_ref[at, 2 * step, 1] = e[2]
            h = strip_h(h, e)
            edge_ref[at, 2 * step + 1, 0] = h[0]
            edge_ref[at, 2 * step + 1, 1] = h[2]
            if step == 0:
                e = strip_e(e, h, strip[12])


def beside(edge, values, z, ahead):
    shift = COLS + (125 if ahead else 123) - 8 * z
    shift = shift % COLS if isinstance(z, int) else lax.rem(shift, COLS)
    lane = lanes_of(values.shape)
    if ahead:
        return jnp.where(lane == COLS - 1, roll(edge, shift, 1), roll(values, -1, 1))
    return jnp.where(lane == 0, roll(edge, shift, 1), roll(values, 1, 1))


def updates(block, parts):
    e_all, h_all, coef_all, edge_ref = block

    def do_h(step, layers):
        new = []
        for at in range(parts):
            for z in layers:
                e = tuple(e_all[at, c, z] for c in range(3))
                h = tuple(h_all[at, c, z + 1] for c in range(3))
                e_up = (e_all[at, 0, z + 1], e_all[at, 1, z + 1])
                e_yn = (
                    beside(edge_ref[at, 2 * step, 0], e[0], z, True),
                    beside(edge_ref[at, 2 * step, 1], e[2], z, True),
                )
                values = h_new(h, e, e_up, (next_row(e[1]), next_row(e[2])), e_yn)
                new.append((at, z, values))
        for at, z, values in new:
            for c in range(3):
                h_all[at, c, z + 1] = values[c]

    def do_e(step, layers):
        new = []
        for at in range(parts):
            for z in layers:
                e = tuple(e_all[at, c, z] for c in range(3))
                h = tuple(h_all[at, c, z + 1] for c in range(3))
                h_down = (h_all[at, 0, z], h_all[at, 1, z])
                h_yp = (
                    beside(edge_ref[at, 2 * step + 1, 0], h[0], z, False),
                    beside(edge_ref[at, 2 * step + 1, 1], h[2], z, False),
                )
                values = e_new(
                    e, h, h_down, (prev_row(h[1]), prev_row(h[2])), h_yp, coef_all[z]
                )
                new.append((at, z, values))
        rows = slice(0, EXT if step == 0 else ROWS)
        for at, z, values in new:
            for c in range(3):
                e_all[at, c, z, rows, :] = values[c][rows]

    return do_h, do_e


def plane_kernel(
    e_hbm,
    h_hbm,
    coef_hbm,
    e_foot_hbm,
    h_foot_hbm,
    coef_foot_hbm,
    own_hbm,
    tail_hbm,
    cols_b_hbm,
    cols_a_hbm,
    rot_hbm,
    wave_hbm,
    monitor_ref,
    spread_ref,
    *scratch,
):
    edges, block = scratch[0:4], scratch[4:8]
    wave_ref, sem = scratch[8:10]
    e_all, h_all, coef_all, edge_ref = block
    level = monitor_ref[0]
    low = jnp.clip(level - 2, 0, NZ - 5)
    here, there = pl.ds(low, 5), pl.ds(low + 1, 5)
    large = fetch(
        [
            (e_hbm.at[:, :, here], e_all.at[:, :, here, 0:ROWS, :]),
            (h_hbm.at[:, :, here], h_all.at[:, :, there, 0:ROWS, :]),
            (coef_hbm.at[here], coef_all.at[here, 0:ROWS, :]),
            (e_foot_hbm.at[:, :, here], e_all.at[:, :, here, ROWS:EXT, :]),
            (h_foot_hbm.at[:, :, here], h_all.at[:, :, there, ROWS:EXT, :]),
            (coef_foot_hbm.at[here], coef_all.at[here, ROWS:EXT, :]),
            (wave_hbm, wave_ref),
        ],
        sem,
        5,
    )
    copies = fetch_edges(own_hbm, tail_hbm, (cols_a_hbm, cols_b_hbm), rot_hbm, edges, sem, 0)
    arrived(copies)
    fill_edges(edges, block, (0, 1))
    arrived(large)
    near = {}
    for k in range(-2, 3):
        z = jnp.clip(level + k, 0, NZ - 1)
        for part in range(2):
            for c in range(3):
                if c < 2 or k < 2:
                    e = e_all[part, c, z]
                    near["e", part, c, k] = jnp.where(level + k < NZ, e, 0.0) if k > 0 else e
                if k < 2 and (c < 2 or k > -2):
                    h = h_all[part, c, z + 1]
                    near["h", part, c, k] = jnp.where(level + k >= 0, h, 0.0) if k < 0 else h
    def update_h(step, part, k, wanted):
        z = jnp.clip(level + k, 0, NZ - 1)
        ex, ey, ez = (near["e", part, c, k] for c in range(3))
        edge = edge_ref.at[part, 2 * step]
        new = {}
        if 0 in wanted:
            new[0] = beside(edge[1], ez, z, True) - ez - (near["e", part, 1, k + 1] - ey)
        if 1 in wanted:
            new[1] = near["e", part, 0, k + 1] - ex - (next_row(ez) - ez)
        if 2 in wanted:
            new[2] = next_row(ey) - ey - (beside(edge[0], ex, z, True) - ex)
        for c, curl in new.items():
            values = near["h", part, c, k] - STEP_DT * curl
            near["h", part, c, k] = jnp.where(level + k >= 0, values, 0.0) if k < 0 else values

    def update_e(step, part, k, wanted):
        z = jnp.clip(level + k, 0, NZ - 1)
        hx, hy, hz = (near["h", part, c, k] for c in range(3))
        edge = edge_ref.at[part, 2 * step + 1]
        coef = coef_all[z]
        new = {}
        if 0 in wanted:
            new[0] = hz - beside(edge[1], hz, z, False) - (hy - near["h", part, 1, k - 1])
        if 1 in wanted:
            new[1] = hx - near["h", part, 0, k - 1] - (hz - prev_row(hz))
        if 2 in wanted:
            new[2] = hy - prev_row(hy) - (hx - beside(edge[0], hx, z, False))
        for c, curl in new.items():
            values = near["e", part, c, k] + coef * curl
            near["e", part, c, k] = jnp.where(level + k < NZ, values, 0.0) if k > 0 else values

    for part in range(2):
        for k in range(-2, 2):
            update_h(0, part, k, (0, 1, 2) if k > -2 else (0, 1))
        for k in range(-1, 2):
            update_e(0, part, k, (0, 1, 2) if k < 1 else (0, 1))
        update_h(1, part, -1, (0, 1))
        update_h(1, part, 0, (0, 1, 2))
        update_e(1, part, 0, (0, 1))
    re, im = (
        jnp.concatenate([near["e", part, c, 0][0:ROWS] for c in range(2)], axis=0)
        for part in range(2)
    )
    y_section(re, im, wave_ref, spread_ref)


def field_kernel(parts, inputs, *refs):
    (
        e_hbm,
        h_hbm,
        coef_hbm,
        e_foot_hbm,
        h_foot_hbm,
        coef_foot_hbm,
        own_hbm,
        tail_hbm,
        cols_b_hbm,
        cols_a_hbm,
        rot_hbm,
    ) = refs[0:11]
    e_out, h_out, token_hbm = refs[inputs : inputs + 3]
    scratch = refs[inputs + 3 :]
    edges, block, sem = scratch[0:4], scratch[4:8], scratch[8]
    e_all, h_all, coef_all, _ = block
    copies = fetch_edges(own_hbm, tail_hbm, (cols_a_hbm, cols_b_hbm), rot_hbm, edges, sem, 0)
    some = slice(parts[0], parts[-1] + 1)
    quads = range(NZ // 4)
    loads = []
    for quad in quads:
        here, there = pl.ds(4 * quad, 4), pl.ds(4 * quad + 1, 4)
        loads.append(
            fetch(
                [
                    (e_hbm.at[some, :, here], e_all.at[:, :, here, 0:ROWS, :]),
                    (e_foot_hbm.at[some, :, here], e_all.at[:, :, here, ROWS:EXT, :]),
                    (h_hbm.at[some, :, here], h_all.at[:, :, there, 0:ROWS, :]),
                    (h_foot_hbm.at[some, :, here], h_all.at[:, :, there, ROWS:EXT, :]),
                    (coef_hbm.at[here], coef_all.at[here, 0:ROWS, :]),
                    (coef_foot_hbm.at[here], coef_all.at[here, ROWS:EXT, :]),
                ],
                sem,
                7 + 6 * quad,
            )
        )
    arrived(copies)
    token = fetch([(edges[3], token_hbm)], sem)
    fill_edges(edges, block, parts)
    do_h, do_e = updates(block, len(parts))

    def finish(quad):
        layers = [4 * quad + k for k in range(4)]
        here, there = pl.ds(4 * quad, 4), pl.ds(4 * quad + 1, 4)
        do_h(1, layers)
        fetch([(h_all.at[:, :, there, 0:ROWS, :], h_out.at[some, :, here])], sem, 5)
        do_e(1, layers)
        fetch([(e_all.at[:, :, here, 0:ROWS, :], e_out.at[some, :, here])], sem, 6)

    arrived(loads[0])
    for quad in quads:
        if quad + 1 < len(quads):
            arrived(loads[quad + 1])
        layers = [4 * quad + k for k in range(4)]
        do_h(0, layers)
        do_e(0, layers)
        if quad > 0:
            finish(quad - 1)
    finish(quads[-1])
    arrived(token)
    stored = (
        (h_all.at[:, :, 1 : NZ + 1, 0:ROWS, :], h_out.at[some]),
        (e_all.at[:, :, 0:NZ, 0:ROWS, :], e_out.at[some]),
    )
    for k, (source, target) in enumerate(stored):
        pltpu.make_async_copy(source, target, sem.at[5 + k]).wait()


def y_section(re, im, wave_ref, spread_ref):
    wave = wave_ref[...]
    _, owners, _, lanes = spread_ref.shape
    each = lanes // 4
    rows = re.shape[0]
    both = jnp.concatenate(
        [jnp.concatenate([re, im], axis=1), jnp.concatenate([im, -re], axis=1)], axis=0
    )
    both = jnp.dot(
        both, wave, precision=lax.Precision.HIGHEST, preferred_element_type=jnp.float32
    )
    out = (both[0:rows], both[rows:])
    for owner in range(owners):
        pieces = [
            out[part][c * ROWS : (c + 1) * ROWS, owner * each : (owner + 1) * each]
            for part in range(2)
            for c in range(2)
        ]
        joined = jnp.concatenate(pieces, axis=1)
        for half in range(2):
            spread_ref[half, owner] = joined


def x_kernel(got_ref, wave_ref, after_hbm, part_ref):
    each = got_ref.shape[0] // 2
    totals = []
    for half in range(2):
        total = got_ref[half * each]
        for source in range(1, each):
            total = total + got_ref[half * each + source]
        totals.append(total)
    total = jnp.concatenate(totals, axis=0)
    half = total.shape[1] // 2
    other = roll(total, half, 1)
    other = jnp.where(lanes_of(other.shape) < half, other, -other)
    result = jnp.dot(
        wave_ref[...],
        jnp.concatenate([total, other], axis=0),
        precision=lax.Precision.HIGHEST,
        preferred_element_type=jnp.float32,
    )
    part_ref[...] = result.reshape(part_ref.shape)


def groups(mesh_shape):
    count_x, count_y = mesh_shape
    rest = count_x // 2
    near = [
        [(half * rest + r) * count_y + y for half in range(2) for y in range(count_y)]
        for r in range(rest)
    ]
    far = [
        [(half * rest + r) * count_y + y for r in range(rest)]
        for half in range(2)
        for y in range(count_y)
    ]
    return near, far


def sum_kernel(got_ref, out_ref):
    total = got_ref[0]
    for source in range(1, got_ref.shape[0]):
        total = total + got_ref[source]
    each = total.shape[1] // 4
    for c in range(2):
        for part in range(2):
            start = (2 * part + c) * each
            out_ref[c, part] = total[:, start : start + each]


def fill_tables(count_x, count_y, theta_x, theta_y, y_ref, x_ref):
    index_x, index_y = lax.axis_index("gx"), lax.axis_index("gy")
    total_x, total_y = ROWS * count_x, COLS * count_y

    def waves(product, place, total, theta):
        angle = (
            2.0 * math.pi * (product & (total - 1)).astype(jnp.float32)
            + theta * place.astype(jnp.float32)
        ) / total
        return jnp.cos(angle), jnp.sin(angle)

    def joined(a, b):
        return a[0] * b[0] - a[1] * b[1], a[1] * b[0] + a[0] * b[1]

    scale = 1.0 / math.sqrt(total_x * total_y)
    blocks = COLS // 8
    start = index_y * COLS
    order = lax.broadcasted_iota(jnp.int32, (blocks, ORD_Y), 1) - ORD_Y // 2
    place = start + 8 * lax.broadcasted_iota(jnp.int32, (blocks, ORD_Y), 0)
    coarse = waves(order * place, place, total_y, theta_y)
    place = lax.broadcasted_iota(jnp.int32, (8, ORD_Y), 0)
    fine = waves(order[0:8] * place, place, total_y, theta_y)
    fine = (fine[0] * scale, fine[1] * scale)
    for block in range(blocks):
        part = tuple(values[block : block + 1] for values in coarse)
        cos, sin = joined(part, fine)
        y_ref[8 * block : 8 * block + 8, :] = cos
        y_ref[COLS + 8 * block : COLS + 8 * block + 8, :] = sin
    blocks = ORD_X // 16
    shape = (blocks, 4 * ROWS)
    rest = count_x // 2
    lane = lax.broadcasted_iota(jnp.int32, shape, 1)
    block_x = lax.rem(index_x, rest) + rest * (lane // ROWS % 2)
    place = block_x * ROWS + lane % ROWS
    own_half = index_x // rest * (ORD_X // 2)
    order = 8 * lax.broadcasted_iota(jnp.int32, shape, 0) + own_half - ORD_X // 2
    coarse = waves(order * place, place, total_x, theta_x)
    order = lax.broadcasted_iota(jnp.int32, (8, 4 * ROWS), 0)
    fine = waves(order * place[0:8], place[0:8], total_x, 0.0)
    for block in range(blocks):
        part = tuple(values[block : block + 1] for values in coarse)
        cos, sin = joined(part, fine)
        x_ref[8 * block : 8 * block + 8, :] = jnp.where(lane[0:8] < 2 * ROWS, cos, sin)


def params(mebibytes):
    return pltpu.CompilerParams(vmem_limit_bytes=mebibytes << 20)


def cost(microseconds):
    return pl.CostEstimate(
        flops=0, bytes_accessed=microseconds * 3_000_000, transcendentals=0
    )


def f32(*shape):
    return jax.ShapeDtypeStruct(shape, jnp.float32)


def shards(
    e_field, h_field, material, pattern, base_eps, mode_table, nodes, bloch_phase, monitor_z
):
    count_x = lax.axis_size("gx")
    count_y = lax.axis_size("gy")
    each_p = ORD_X // count_x
    each_q = ORD_Y // count_y
    vmem = pl.BlockSpec(memory_space=VMEM)
    hbm = pl.BlockSpec(memory_space=pltpu.HBM)
    f32_vmem = lambda *shape: VMEM(shape, jnp.float32)
    dma = pltpu.SemaphoreType.DMA

    table, rows_a, rows_b = pl.pallas_call(
        rows_kernel,
        out_shape=(
            f32(8, COLS),
            f32(MAIN_BLOCKS, 8, COLS),
            f32(MAIN_BLOCKS, 8, COLS),
        ),
        in_specs=[hbm] * 7,
        out_specs=(vmem,) * 3,
        scratch_shapes=[
            f32_vmem(2, 2, 3, NZ, 8, COLS),
            f32_vmem(2, 2, 3, NZ, 8, COLS),
            VMEM((2, NZ, 8, COLS), jnp.int32),
            VMEM((2, NZ, 8, COLS), jnp.int32),
            SMEM(base_eps.shape, jnp.float32),
            SMEM(mode_table.shape, jnp.float32),
            SMEM(nodes.shape, jnp.float32),
            dma((11,)),
        ],
        compiler_params=params(64),
        cost_estimate=cost(3),
        name="rows",
    )(e_field, h_field, material, pattern, base_eps, mode_table, nodes)
    rows_b = swapped(rows_b, "gx", False)
    rows_a = swapped(rows_a, "gx", True)
    own, cols_a, cols_b, coef = pl.pallas_call(
        own_kernel,
        out_shape=(
            f32(13, ROWS, COLS),
            f32(3, ROWS, COLS),
            f32(3, ROWS, COLS),
            f32(NZ, ROWS, COLS),
        ),
        in_specs=[hbm] * 5,
        out_specs=(vmem,) * 4,
        scratch_shapes=[
            f32_vmem(*e_field.shape),
            f32_vmem(*h_field.shape),
            VMEM(material.shape, jnp.int32),
            VMEM(pattern.shape, jnp.int32),
            f32_vmem(8, COLS),
            dma((5,)),
        ],
        compiler_params=params(64),
        cost_estimate=cost(4),
        name="own",
    )(e_field, h_field, material, pattern, table)
    tail, cols_a, cols_b, rot = pl.pallas_call(
        pack_kernel,
        out_shape=(
            f32(13, EXT - ROWS, COLS),
            f32(3, EXT, COLS),
            f32(3, EXT, COLS),
            f32(8, COLS),
        ),
        in_specs=[hbm] * 5,
        out_specs=(vmem,) * 4,
        scratch_shapes=[
            f32_vmem(MAIN_BLOCKS, 8, COLS),
            f32_vmem(MAIN_BLOCKS, 8, COLS),
            SMEM((2,), jnp.float32),
            dma((5,)),
        ],
        compiler_params=params(64),
        cost_estimate=cost(2),
        name="pack",
    )(cols_a, cols_b, rows_b, rows_a, bloch_phase)
    cols_b = swapped(cols_b, "gy", False)
    cols_a = swapped(cols_a, "gy", True)
    *feet, y_wave, x_wave = pl.pallas_call(
        functools.partial(feet_kernel, (count_x, count_y)),
        out_shape=(
            f32(2, 3, NZ, EXT - ROWS, COLS),
            f32(2, 3, NZ, EXT - ROWS, COLS),
            f32(NZ, EXT - ROWS, COLS),
            f32(2 * COLS, ORD_Y),
            f32(ORD_X // 2, 4 * ROWS),
        ),
        in_specs=[hbm] * 4,
        out_specs=(vmem,) * 5,
        scratch_shapes=[
            f32_vmem(MAIN_BLOCKS, 8, COLS),
            f32_vmem(MAIN_BLOCKS, 8, COLS),
            f32_vmem(8, COLS),
            SMEM((2,), jnp.float32),
            dma((4,)),
        ],
        compiler_params=params(64),
        cost_estimate=cost(2),
        name="feet",
    )(rows_b, rows_a, rot, bloch_phase)
    around = (e_field, h_field, coef, *feet, own, tail, cols_b, cols_a, rot)
    spread = pl.pallas_call(
        plane_kernel,
        out_shape=f32(2, count_y, ROWS, 4 * each_q),
        in_specs=[hbm] * 12 + [pl.BlockSpec(memory_space=SMEM)],
        out_specs=vmem,
        scratch_shapes=[
            *edge_scratch(),
            *block_scratch(2),
            f32_vmem(*y_wave.shape),
            dma((12,)),
        ],
        compiler_params=params(60),
        cost_estimate=cost(3),
        name="plane",
    )(*around, y_wave, monitor_z)

    near, far = groups((count_x, count_y))
    both = ("gx", "gy")
    spread = spread.reshape(2 * count_y, ROWS, 4 * each_q)
    got = lax.all_to_all(spread, both, 0, 0, tiled=True, axis_index_groups=near)
    e_out, h_out, token = pl.pallas_call(
        functools.partial(field_kernel, (0, 1), 12),
        out_shape=(f32(*e_field.shape), f32(*h_field.shape), f32(8, COLS)),
        in_specs=[hbm] * 12,
        out_specs=(hbm, hbm, hbm),
        scratch_shapes=[*edge_scratch(), *block_scratch(2), dma((31,))],
        compiler_params=params(60),
        cost_estimate=cost(6),
        name="fields",
    )(*around, spread)
    partial = pl.pallas_call(
        x_kernel,
        out_shape=f32(count_x // 2, each_p, 4 * each_q),
        in_specs=[vmem, vmem, hbm],
        out_specs=vmem,
        compiler_params=params(8),
        cost_estimate=cost(1),
        name="x_section",
    )(got, x_wave, token)
    got = lax.all_to_all(partial, both, 0, 0, tiled=True, axis_index_groups=far)
    orders = pl.pallas_call(
        sum_kernel,
        out_shape=f32(2, 2, each_p, each_q),
        in_specs=[vmem],
        out_specs=vmem,
        compiler_params=params(8),
        cost_estimate=cost(1),
        name="order_sum",
    )(got)
    return e_out, h_out, orders


def solution(mesh):
    grid = P(None, None, None, "gx", "gy")
    cells = P(None, "gx", "gy")
    return jax.shard_map(
        shards,
        mesh=mesh,
        in_specs=(grid, grid, cells, cells, P(), P(), P(), P(), P()),
        out_specs=(grid, grid, P(None, None, "gx", "gy")),
        check_vma=False,
    )
```
